32 devices in a mesh: seq: 32 (over z, y, x, core).
Axes of the slice: x: 2, y: 2, z: 4, core: 2. Of those that a mesh axis runs over, the one named last changes fastest.
Arguments:
- inputs: bfloat16 [131072, 128], P('seq'), may hold values from -6 to 6
- segment_ids: int32 [512, 256], P('seq'), may hold values from 0 to 7, never falling along the last dimension, each value on 1 to 64 neighbouring positions
- cotangent: bfloat16 [131072, 128], P('seq'), may hold values from -6 to 6
- norm_gains: float32 [2, 2, 128], replicated, may hold values from 0.5 to 1.5
- norm_shifts: float32 [2, 2, 128], replicated, may hold values from -3 to 3
- w_qkv: bfloat16 [2, 128, 384], replicated, may hold values from -0.5 to 0.5
- qv_bias: float32 [2, 256], replicated, may hold values from -3 to 3
- w_out: bfloat16 [2, 128, 128], replicated, may hold values from -3 to 3
- out_bias: float32 [2, 128], replicated, may hold values from -3 to 3
- w_gate: bfloat16 [2, 128], replicated, may hold values from -0.5 to 0.5
- w_up: bfloat16 [2, 128, 256], replicated, may hold values from -0.5 to 0.5
- up_bias: float32 [2, 256], replicated, may hold values from -3 to 3
- w_down: bfloat16 [2, 256, 128], replicated, may hold values from -0.75 to 0.75
- down_bias: float32 [2, 128], replicated, may hold values from -3 to 3
Outputs:
- result: bfloat16 [131072, 128], P('seq')
- grad_inputs: float32 [131072, 128], P('seq')
- grad_gains: float32 [2, 2, 128], replicated
- grad_shifts: float32 [2, 2, 128], replicated
- grad_qkv: float32 [2, 128, 384], replicated
- grad_qv_bias: float32 [2, 256], replicated
- grad_out: float32 [2, 128, 128], replicated
- grad_out_bias: float32 [2, 128], replicated
- grad_gate: float32 [2, 128], replicated
- grad_up: float32 [2, 128, 256], replicated
- grad_up_bias: float32 [2, 256], replicated
- grad_down: float32 [2, 256, 128], replicated
- grad_down_bias: float32 [2, 128], replicated
The draws below stay inside these ranges and needn't reach their ends.
Inputs may be any that keep to these rules, and one draw needn't show every extreme that they name: `segment_ids`: in each sequence the ids never fall; each of the 8 ids covers 1 to 64 tokens.
All inputs are finite; a program needn't handle non-finite values.
Results may differ from the reference program's by a relative error of at most 0.02.
Values sent between devices are 32-bit elements; how exact they have to be, the bound alone decides.
No kernel may reach another device: no remote copies, remote signals or barrier semaphores. Data moves between devices by JAX's collectives and lax.ppermute only.
A program may use at most 128 MiB of HBM per device.

```python
import math
import jax
import jax.numpy as jnp
import numpy as np
from jax import lax

D = 128
HEADS = 8
FF = 256
LAYERS = 2
LEN = 256
ROWS_SEQ = 8
ROW_MOST = 64
SEQS = 512
TOKENS = 131072


def shard_levels(rng, extent, cuts, least, high):
    loudness, own = 1.0, jax.random.fold_in(rng, 6)
    for axis_at, blocks in cuts:
        steps = jnp.exp(jax.random.uniform(jax.random.fold_in(own, axis_at), (blocks,), jnp.float32, least / len(cuts), high / len(cuts)))
        loudness = loudness * jnp.repeat(steps, extent[axis_at] // blocks).reshape([-1 if axis == axis_at else 1 for axis in range(len(extent))])
    return loudness


def split_up(count, total, limit, skew):
    loads = [(1 << 20) // math.isqrt(grade ** skew) + 1 for grade in range(2, count + 1)]
    rest, holding = total - limit - (count - 1), [1] * (count - 1)
    while rest > 0:
        movable = [i for i in range(count - 1) if holding[i] < limit]
        mass, remaining = sum([loads[i] for i in movable]), rest
        for i in movable:
            more = min(limit - holding[i], max(1, remaining * loads[i] // mass), rest)
            holding[i] = holding[i] + more
            rest = rest - more
    return np.array([limit] + holding)


def uneven_parts(key, amount, total, reach, slope):
    if amount == 2:
        one = jax.random.randint(key, (), max(1, total - reach), min(reach, total - 1) + 1)
        return jnp.stack([one, total - one])
    lengths = jnp.asarray(split_up(amount, total, reach, slope), jnp.int32)
    twos = (amount - 1) // 2
    giver, taker = lengths[1:1 + 2 * twos:2], lengths[2:2 + 2 * twos:2]
    margin = jnp.minimum(giver - 1, reach - taker)
    shifted = jax.random.randint(jax.random.fold_in(key, 1), (twos,), 0, 1 << 20) % (margin + 1)
    lengths = lengths.at[1:1 + 2 * twos:2].set(giver - shifted).at[2:2 + 2 * twos:2].set(taker + shifted)
    return lengths[jax.random.permutation(jax.random.fold_in(key, 2), amount)]


def noise(own_key, dims, deviation, reach, split=(), dtype=jnp.bfloat16):
    values = deviation * jax.random.normal(own_key, dims, jnp.float32)
    if split:
        values = values * shard_levels(own_key, dims, split, -0.22, 0.18)
    return jnp.clip(values, -reach, reach).astype(dtype)


def setup_inputs(seed: int = 0) -> dict:
    streams_of = jax.random.split(jax.random.key(seed), 15)
    inputs = noise(streams_of[0], (TOKENS, D), 1.0, 6.0, ((0, 32),))
    segment_ids = jax.vmap(lambda own: jnp.searchsorted(jnp.cumsum(uneven_parts(own, ROWS_SEQ, LEN, ROW_MOST, 1)), jnp.arange(LEN), side="right"))(jax.random.split(streams_of[1], SEQS)).reshape((SEQS, LEN)).astype(jnp.int32)
    cotangent = noise(streams_of[2], (TOKENS, D), 1.0, 6.0, ((0, 32),))
    norm_gains = jnp.clip(1.0 + 0.1 * jax.random.normal(streams_of[3], (LAYERS, 2, D), jnp.float32), 0.5, 1.5)
    norm_shifts = noise(streams_of[4], (LAYERS, 2, D), 0.3, 3.0, (), jnp.float32)
    w_qkv = noise(streams_of[5], (LAYERS, D, 3 * D), D ** -0.5, 0.5)
    qv_bias = noise(streams_of[6], (LAYERS, 2 * D), 0.3, 3.0, (), jnp.float32)
    w_out = noise(streams_of[7], (LAYERS, D, D), (D // 32) ** -0.5, 3.0)
    out_bias = noise(streams_of[8], (LAYERS, D), 0.3, 3.0, (), jnp.float32)
    w_gate = noise(streams_of[9], (LAYERS, D), D ** -0.5, 0.5)
    w_up = noise(streams_of[10], (LAYERS, D, FF), D ** -0.5, 0.5)
    up_bias = noise(streams_of[11], (LAYERS, FF), 0.3, 3.0, (), jnp.float32)
    w_down = noise(streams_of[12], (LAYERS, FF, D), (FF // 4) ** -0.5, 0.75)
    down_bias = noise(streams_of[13], (LAYERS, D), 0.3, 3.0, (), jnp.float32)
    return {"inputs": inputs, "segment_ids": segment_ids, "cotangent": cotangent, "norm_gains": norm_gains, "norm_shifts": norm_shifts, "w_qkv": w_qkv, "qv_bias": qv_bias, "w_out": w_out, "out_bias": out_bias, "w_gate": w_gate, "w_up": w_up, "up_bias": up_bias, "w_down": w_down, "down_bias": down_bias}


@jax.custom_vjp
def low(v):
    return lax.optimization_barrier(v.astype(jnp.bfloat16)).astype(jnp.float32)

@jax.custom_vjp
def low_back(v):
    return v

def low_keep(v):
    return (low(v), None)

def low_pass(kept, grad):
    return (grad,)

def back_keep(v):
    return (v, None)

def back_low(kept, grad):
    return (low(grad),)
low.defvjp(low_keep, low_pass)
low_back.defvjp(back_keep, back_low)
HIGHEST_PRECISION = lax.Precision.HIGHEST
MASKED_SCORE = -1000000000.0

def both_ways(operand):
    return low(low_back(operand))

def norm_rows(operand, gain_row, shift_row):
    average = lax.optimization_barrier(jnp.mean(operand, axis=-1, keepdims=True))
    centered = operand - average
    variance = lax.optimization_barrier(jnp.mean(centered * centered, axis=-1, keepdims=True))
    return centered * lax.rsqrt(variance + 1e-05) * gain_row + shift_row

def attend(query_rows, key_rows, value_rows, segment_row):
    token_count = query_rows.shape[0]
    head_size = query_rows.shape[1] // HEADS
    shape = (token_count, HEADS, head_size)
    scores = jnp.einsum('qhe,khe->hqk', query_rows.reshape(shape), key_rows.reshape(shape), precision=HIGHEST_PRECISION) * head_size ** (-0.5)
    scores = low_back(scores)
    allowed = segment_row[:, None] == segment_row[None, :]
    scores = jnp.where(allowed[None], scores, MASKED_SCORE)
    weights = low(jax.nn.softmax(scores, axis=-1))
    mixed_rows = jnp.einsum('hqk,khe->qhe', weights, value_rows.reshape(shape), precision=HIGHEST_PRECISION)
    return mixed_rows.reshape(token_count, HEADS * head_size)

def layer_forward(hidden, segments, weights):
    gain_pair, shift_pair, qkv_matrix, qv_row, out_matrix, out_row, gate_row, up_matrix, up_row, down_matrix, down_row = weights
    width = hidden.shape[1]
    normed = low(norm_rows(hidden, gain_pair[0], shift_pair[0]))
    projected = jnp.dot(normed, qkv_matrix, precision=HIGHEST_PRECISION)
    query_rows = both_ways(projected[:, :width] + qv_row[:width])
    key_rows = both_ways(projected[:, width:2 * width])
    value_rows = both_ways(projected[:, 2 * width:] + qv_row[width:])
    seq_count, length = segments.shape
    shaped = lambda operand: operand.reshape(seq_count, length, width)
    mixed_rows = jax.vmap(attend)(shaped(query_rows), shaped(key_rows), shaped(value_rows), segments)
    mixed_rows = both_ways(mixed_rows.reshape(seq_count * length, width))
    branch = low_back(jnp.dot(mixed_rows, out_matrix, precision=HIGHEST_PRECISION) + out_row)
    middle = hidden + branch
    normed_two = low(norm_rows(middle, gain_pair[1], shift_pair[1]))
    gate_value = jax.nn.sigmoid(jnp.dot(normed_two, gate_row, precision=HIGHEST_PRECISION))
    inner_rows = low_back(jnp.dot(normed_two, up_matrix, precision=HIGHEST_PRECISION) + up_row)
    active = both_ways(jax.nn.gelu(inner_rows * gate_value[:, None]))
    branch_two = low_back(jnp.dot(active, down_matrix, precision=HIGHEST_PRECISION) + down_row)
    return middle + branch_two

def reference(inputs, segment_ids, cotangent, norm_gains, norm_shifts, w_qkv, qv_bias, w_out, out_bias, w_gate, w_up, up_bias, w_down, down_bias):
    parameters = tuple((entry.astype(jnp.float32) for entry in (norm_gains, norm_shifts, w_qkv, qv_bias, w_out, out_bias, w_gate, w_up, up_bias, w_down, down_bias)))
    seq_total, length = segment_ids.shape
    width = inputs.shape[1]
    group_size = min(seq_total, max(1, 4096 // length))
    group_count = seq_total // group_size
    hidden_all = inputs.astype(jnp.float32).reshape(group_count, group_size * length, width)
    cot_all = cotangent.astype(jnp.float32).reshape(group_count, group_size * length, width)
    segs_all = segment_ids.reshape(group_count, group_size, length)

    def forward(hidden, segments, weights_all):
        for layer_index in range(LAYERS):
            hidden = layer_forward(hidden, segments, tuple((entry[layer_index] for entry in weights_all)))
        return hidden

    def group_step(totals, block_items):
        hidden, segments, cot_rows = block_items
        output, pullback = jax.vjp(lambda rows_in, weights_all: forward(rows_in, segments, weights_all), hidden, parameters)
        grad_rows, grad_params = pullback(cot_rows)
        totals = tuple((total_entry + grad_entry for total_entry, grad_entry in zip(totals, grad_params)))
        return (totals, (output, grad_rows))
    zeros_start = tuple((jnp.zeros_like(entry) for entry in parameters))
    totals, (outputs, grad_rows) = lax.scan(group_step, zeros_start, (hidden_all, segs_all, cot_all))
    return (outputs.reshape(-1, width).astype(jnp.bfloat16), grad_rows.reshape(-1, width), totals[0], totals[1], totals[2], totals[3], totals[4], totals[5], totals[6], totals[7], totals[8], totals[9], totals[10])
```

```python
import jax
import jax.numpy as jnp
from jax import lax
from jax.experimental import pallas as pl
from jax.experimental.pallas import tpu as pltpu
from jax.sharding import PartitionSpec as P

HEADS = 8
LAYERS = 2
WIDTH = 128
FF = 256
LEN = 256
HALF = 128
WINDOW = 192
FAR = -1.0e9
GELU_A = 0.7978845608028654
GELU_B = 0.044715
F32 = jnp.float32
BF16 = jnp.bfloat16

GAIN_ONE, SHIFT_ONE, GAIN_TWO, SHIFT_TWO, OUT_BIAS, DOWN_BIAS, Q_BIAS, V_BIAS, GATE, UP_LOW, UP_HIGH = range(11)
COLUMNS = 11
S_GAIN_ONE, S_SHIFT_ONE, S_GAIN_TWO, S_SHIFT_TWO, S_OUT, S_DOWN, S_V, S_GATE, S_UP_LOW, S_UP_HIGH = range(10)
SUMS = 10
R_QKV, R_OUT, R_UP, R_DOWN, R_SMALL, ROWS = 0, 384, 512, 768, 1024, 1056


def dot(left, right):
    return lax.dot_general(left, right, (((1,), (0,)), ((), ())), preferred_element_type=F32)


def dot_t(left, right):
    return lax.dot_general(left, right, (((1,), (1,)), ((), ())), preferred_element_type=F32)


def both(column):
    return jnp.concatenate([column, column], axis=1)


def fold(value):
    return value[:, :HALF] + value[:, HALF:]


def zeros(rows, lanes=LEN):
    return jnp.zeros((rows, lanes), BF16)


def split_three(value):
    high = value.astype(BF16)
    rest = value - high.astype(F32)
    middle = rest.astype(BF16)
    low = (rest - middle.astype(F32)).astype(BF16)
    return high, middle, low


def norm_parts(value):
    average = jnp.sum(value, axis=0, keepdims=True) * (1.0 / WIDTH)
    centered = value - average
    variance = jnp.sum(centered * centered, axis=0, keepdims=True) * (1.0 / WIDTH)
    scale = lax.rsqrt(variance + 1e-05)
    return centered * scale, scale


def pair_block(rows, pair, block):
    lanes = slice(block * HALF, (block + 1) * HALF)
    first = rows[32 * pair : 32 * pair + 16, lanes]
    second = rows[32 * pair + 16 : 32 * pair + 32, lanes]
    gap = zeros(16, HALF)
    return jnp.concatenate(
        [jnp.concatenate([first, gap], axis=1), jnp.concatenate([gap, second], axis=1)], axis=0
    )


def place(pair, block, extra):
    lanes = block.shape[1]
    if pair % 2 == 0:
        features = [block, zeros(32, lanes)]
    else:
        features = [zeros(32, lanes), block]
    if extra is None:
        other = [zeros(64, lanes)]
    else:
        other = [extra, zeros(64 - extra.shape[0], lanes)]
    return jnp.concatenate(features + other if pair < 2 else other + features, axis=0)


def token_rows(rows, extra_low, extra_high):
    low = jnp.concatenate([rows[:64], extra_low, zeros(64 - extra_low.shape[0])], axis=0)
    high = jnp.concatenate([extra_high, zeros(64 - extra_high.shape[0]), rows[64:]], axis=0)
    return low.T, high.T


def skewed(units):
    running, waiting = [], list(units)
    while running or waiting:
        if waiting:
            running.insert(0, waiting.pop(0))
        running = [unit for unit in running if next(unit, "end") != "end"]
        yield


def together(parts):
    running = list(parts)
    while running:
        running = [part for part in running if next(part, "end") != "end"]


def window_of(block):
    return slice(0, WINDOW) if block == 0 else slice(LEN - WINDOW, LEN)


def segment_masks(segments):
    ids = lax.broadcasted_iota(jnp.int32, (16, LEN), 0)
    same = ids == segments
    one_hot = jnp.where(same, 1.0, 0.0).astype(BF16)
    other = jnp.where(same | (ids >= 8), 0.0, FAR).astype(BF16)
    return one_hot, other


def forward_unit(block, pair, keys_rows, query, values, marks, mixed_ref, total_ref):
    window = window_of(block)
    lanes = slice(block * HALF, (block + 1) * HALF)
    weights = place(pair, pair_block(query, pair, block), both(marks[:, lanes]))
    scores = dot(keys_rows[window], weights)
    yield
    peak = jnp.max(scores, axis=0, keepdims=True)
    powers = jnp.exp(scores - peak).astype(BF16)
    yield
    ones = jnp.ones((16, WINDOW), BF16)
    mixed = dot(jnp.concatenate([values[32 * pair : 32 * pair + 32, window], ones], axis=0), powers)
    yield
    total = mixed[32:33]
    scale = 1.0 / total
    mixed_ref[32 * pair : 32 * pair + 16, lanes] = mixed[:16, :HALF] * scale[:, :HALF]
    mixed_ref[32 * pair + 16 : 32 * pair + 32, lanes] = mixed[16:32, HALF:] * scale[:, HALF:]
    log_total = peak + jnp.log(total)
    total_ref[2 * pair : 2 * pair + 1, lanes] = log_total[:, :HALF]
    total_ref[2 * pair + 1 : 2 * pair + 2, lanes] = log_total[:, HALF:]


def attention_forward(query, keys, values, one_hot, other, mixed_ref, total_ref):
    low, high = token_rows(keys, other, other)
    yield
    yield from skewed(
        forward_unit(block, pair, low if pair < 2 else high, query, values, one_hot, mixed_ref, total_ref)
        for block in range(2)
        for pair in range(4)
    )


def forward_layer(layer, hidden, segments, weights, columns, mixed_ref, total_ref):
    qkv_t, out_t, up_t, down_t = weights
    column = lambda which: both(columns[layer, which])
    xhat, unused = norm_parts(hidden)
    normed = (xhat * column(GAIN_ONE) + column(SHIFT_ONE)).astype(BF16)
    yield
    projected = dot(qkv_t[layer], normed)
    yield
    query = (projected[:WIDTH] + column(Q_BIAS)).astype(BF16)
    keys = projected[WIDTH : 2 * WIDTH].astype(BF16)
    values = (projected[2 * WIDTH :] + column(V_BIAS)).astype(BF16)
    one_hot, other = segments
    yield from attention_forward(query, keys, values, one_hot, other, mixed_ref, total_ref)
    mixed = mixed_ref[...].astype(BF16)
    middle = hidden + (dot(out_t[layer], mixed) + column(OUT_BIAS))
    yield
    xhat_two, unused = norm_parts(middle)
    normed_two = (xhat_two * column(GAIN_TWO) + column(SHIFT_TWO)).astype(BF16)
    yield
    inner = dot(up_t[layer], normed_two)
    yield
    logit = inner[FF : FF + 1]
    inner = inner[:FF] + jnp.concatenate([column(UP_LOW), column(UP_HIGH)], axis=0)
    gated = inner * jax.nn.sigmoid(logit)
    power = jnp.tanh(GELU_A * gated * (1.0 + GELU_B * (gated * gated)))
    active = (0.5 * gated * (1.0 + power)).astype(BF16)
    yield
    output = middle + (dot(down_t[layer], active) + column(DOWN_BIAS))
    return output, (normed, query, keys, values, mixed, middle, normed_two, inner, logit)


def norm_backward(gradient, xhat, scale, gain):
    inner = gradient * gain
    first = jnp.sum(inner, axis=0, keepdims=True) * (1.0 / WIDTH)
    second = jnp.sum(inner * xhat, axis=0, keepdims=True) * (1.0 / WIDTH)
    return scale * (inner - first - xhat * second)


def backward_unit(
    block, pair, query_rows, grad_rows, query, keys, values, grad_mixed, other, pattern, dk_ref, dv_ref, results
):
    window = window_of(block)
    lanes = slice(block * HALF, (block + 1) * HALF)
    key_block = pair_block(keys, pair, block)
    value_block = pair_block(values, pair, block)
    ones = pattern[pair]
    key_weights = place(pair, key_block, jnp.concatenate([both(other[:, lanes]), ones], axis=0))
    value_weights = place(pair, value_block, jnp.concatenate([zeros(16), ones], axis=0))
    scores = dot(query_rows[window], key_weights)
    grad_probs = dot(grad_rows[window], value_weights)
    yield
    probs = jnp.exp(scores)
    grad_scores = (probs * grad_probs).astype(BF16)
    probs = probs.astype(BF16)
    yield
    rows = slice(32 * pair, 32 * pair + 32)
    grad_values = dot(grad_mixed[rows, window], probs)
    grad_keys = dot(query[rows, window], grad_scores)
    parts = [key_block]
    if pair > 0:
        parts = [zeros(32 * pair)] + parts
    if pair < 3:
        parts = parts + [zeros(96 - 32 * pair)]
    grad_query = dot_t(grad_scores, jnp.concatenate(parts, axis=0))
    results[block] = grad_query if pair == 0 else results[block] + grad_query
    yield
    first, second = slice(32 * pair, 32 * pair + 16), slice(32 * pair + 16, 32 * pair + 32)
    dv_ref[first, lanes] = grad_values[:16, :HALF]
    dv_ref[second, lanes] = grad_values[16:, HALF:]
    dk_ref[first, lanes] = grad_keys[:16, :HALF]
    dk_ref[second, lanes] = grad_keys[16:, HALF:]


def attention_backward(query, keys, values, mixed, log_total, grad_mixed, one_hot, other, pattern, dk_ref, dv_ref):
    product = grad_mixed.astype(F32) * mixed.astype(F32)
    deltas = [
        jnp.sum(product[16 * head : 16 * head + 16], axis=0, keepdims=True) for head in range(HEADS)
    ]
    delta = jnp.concatenate(deltas, axis=0)
    gap = jnp.zeros((4, LEN), F32)

    def extras(value):
        parts = [part.astype(F32) for part in split_three(-value)]
        low = jnp.concatenate([part[:4] for part in parts] + [gap], axis=0).astype(BF16)
        high = jnp.concatenate([part[4:] for part in parts] + [gap], axis=0).astype(BF16)
        return low, high

    total_low, total_high = extras(log_total)
    delta_low, delta_high = extras(delta)
    query_low, query_high = token_rows(
        query, jnp.concatenate([one_hot, total_low], axis=0), jnp.concatenate([one_hot, total_high], axis=0)
    )
    grad_low, grad_high = token_rows(
        grad_mixed, jnp.concatenate([zeros(16), delta_low], axis=0), jnp.concatenate([zeros(16), delta_high], axis=0)
    )
    yield
    results = {}
    yield from skewed(
        backward_unit(
            block, pair, query_low if pair < 2 else query_high, grad_low if pair < 2 else grad_high, query, keys,
            values, grad_mixed, other, pattern, dk_ref, dv_ref, results,
        )
        for block in range(2)
        for pair in range(4)
    )
    windows = [results[0], results[1]]
    edge = LEN - WINDOW
    grad_query = jnp.concatenate(
        [windows[0][:edge], windows[0][edge:] + windows[1][: WINDOW - edge], windows[1][WINDOW - edge :]], axis=0
    )
    return (grad_query * 0.25).astype(BF16)


def backward_layer(layer, gradient, hidden, segments, kept, log_total, raw, columns, pattern, totals, dk_ref, dv_ref):
    w_qkv, w_out, w_up, w_down = raw
    normed, query, keys, values, mixed, middle, normed_two, inner, logit = kept
    qkv_total, out_total, up_total, down_total, sums, query_sum = totals
    column = lambda which: both(columns[layer, which])
    branch = gradient.astype(BF16)
    sums[S_DOWN] += fold(branch.astype(F32))
    grad_active = dot(w_down[layer], branch).astype(BF16).astype(F32)
    yield
    gate = jax.nn.sigmoid(logit)
    gated = inner * gate
    square = gated * gated
    power = jnp.tanh(GELU_A * gated * (1.0 + GELU_B * square))
    half_up = 0.5 + 0.5 * power
    active = (gated * half_up).astype(BF16)
    slope = half_up + gated * (half_up * (1.0 - power)) * (GELU_A + (3.0 * GELU_A * GELU_B) * square)
    grad_gated = grad_active * slope
    grad_logit = jnp.sum(grad_gated * inner, axis=0, keepdims=True) * (gate * (1.0 - gate))
    grad_inner = (grad_gated * gate).astype(BF16)
    yield
    down_total[...] += dot_t(branch, active)
    up_total[...] += dot_t(normed_two, grad_inner)
    inner_sum = fold(grad_inner.astype(F32))
    sums[S_UP_LOW] += inner_sum[:HALF]
    sums[S_UP_HIGH] += inner_sum[HALF:]
    sums[S_GATE] += fold(normed_two.astype(F32) * grad_logit)
    grad_two = dot(w_up[layer], grad_inner) + column(GATE) * grad_logit
    yield
    xhat, scale = norm_parts(middle)
    sums[S_GAIN_TWO] += fold(grad_two * xhat)
    sums[S_SHIFT_TWO] += fold(grad_two)
    grad_middle = gradient + norm_backward(grad_two, xhat, scale, column(GAIN_TWO))
    attended = grad_middle.astype(BF16)
    sums[S_OUT] += fold(attended.astype(F32))
    yield
    out_total[...] += dot_t(mixed, attended)
    grad_mixed = dot(w_out[layer], attended).astype(BF16)
    one_hot, other = segments
    yield
    grad_query = yield from attention_backward(
        query, keys, values, mixed, log_total, grad_mixed, one_hot, other, pattern, dk_ref, dv_ref
    )
    yield
    grad_keys = dk_ref[...].astype(BF16)
    grad_values = dv_ref[...].astype(BF16)
    grad_kv = jnp.concatenate([grad_keys, grad_values], axis=0)
    qkv_total[:, :WIDTH] += dot(normed, grad_query)
    qkv_total[:, WIDTH:] += dot_t(normed, grad_kv)
    query_sum[...] += jnp.sum(grad_query.astype(F32).reshape(LEN // 8, 8, WIDTH), axis=0)
    sums[S_V] += fold(grad_values.astype(F32))
    grad_one = dot_t(w_qkv[layer][:, :WIDTH], grad_query) + dot(w_qkv[layer][:, WIDTH:], grad_kv)
    yield
    xhat, scale = norm_parts(hidden)
    sums[S_GAIN_ONE] += fold(grad_one * xhat)
    sums[S_SHIFT_ONE] += fold(grad_one)
    return grad_middle + norm_backward(grad_one, xhat, scale, column(GAIN_ONE))


def spread(row):
    return jnp.broadcast_to(row, (WIDTH, WIDTH)).T


def fill_columns(layer, columns, gains, shifts, qv_bias, out_bias, w_gate, up_bias, down_bias):
    columns[layer, GAIN_ONE] = spread(gains[layer, 0:1])
    columns[layer, GAIN_TWO] = spread(gains[layer, 1:2])
    columns[layer, SHIFT_ONE] = spread(shifts[layer, 0:1])
    columns[layer, SHIFT_TWO] = spread(shifts[layer, 1:2])
    columns[layer, OUT_BIAS] = spread(out_bias[layer : layer + 1])
    columns[layer, DOWN_BIAS] = spread(down_bias[layer : layer + 1])
    columns[layer, Q_BIAS] = spread(qv_bias[layer : layer + 1, :WIDTH]) * 0.25
    columns[layer, V_BIAS] = spread(qv_bias[layer : layer + 1, WIDTH:])
    columns[layer, GATE] = spread(w_gate[layer : layer + 1].astype(F32))
    columns[layer, UP_LOW] = spread(up_bias[layer : layer + 1, :WIDTH])
    columns[layer, UP_HIGH] = spread(up_bias[layer : layer + 1, WIDTH:])


def clear_totals(totals):
    for ref in totals:
        ref[...] = jnp.zeros_like(ref)


def write_totals(totals, grads_ref):
    qkv_total, out_total, up_total, down_total, sums, query_sum = totals
    for part in range(3):
        rows = slice(R_QKV + part * WIDTH, R_QKV + (part + 1) * WIDTH)
        grads_ref[rows] = qkv_total[:, part * WIDTH : (part + 1) * WIDTH]
    grads_ref[R_OUT : R_OUT + WIDTH] = out_total[...]
    for part in range(2):
        lanes = slice(part * WIDTH, (part + 1) * WIDTH)
        grads_ref[R_UP + part * WIDTH : R_UP + (part + 1) * WIDTH] = up_total[:, lanes]
        grads_ref[R_DOWN + part * WIDTH : R_DOWN + (part + 1) * WIDTH] = down_total[:, lanes].T
    rows = [jnp.sum(sums[which].T, axis=0, keepdims=True) for which in range(SUMS)]
    rows.append(jnp.sum(query_sum[...], axis=0, keepdims=True))
    rows.append(jnp.zeros((ROWS - R_SMALL - len(rows), WIDTH), F32))
    grads_ref[R_SMALL:ROWS] = jnp.concatenate(rows, axis=0)


def first_kernel(
    per_step,
    x_ref, seg_ref, cot_ref, gains, shifts, w_qkv, qv_bias, w_out, out_bias, w_gate, w_up, up_bias, w_down, down_bias,
    pattern,
    result_ref, grad_ref, normed_ref, qkv_ref, mixed_ref, total_ref, middle_ref, normed_two_ref, inner_ref, logit_ref,
    grads_ref,
    columns, qkv_t, out_t, up_t, down_t, mixed_scratch, total_scratch, dk_ref, dv_ref, *totals,
):
    @pl.when(pl.program_id(0) == 0)
    def start():
        clear_totals(totals)
        for layer in range(LAYERS):
            fill_columns(layer, columns, gains, shifts, qv_bias, out_bias, w_gate, up_bias, down_bias)
            qkv_t[layer, :WIDTH] = (w_qkv[layer][:, :WIDTH] * jnp.asarray(0.25, BF16)).T
            qkv_t[layer, WIDTH:] = w_qkv[layer][:, WIDTH:].T
            out_t[layer] = w_out[layer].T
            up_t[layer, :FF] = w_up[layer].T
            up_t[layer, FF:] = jnp.concatenate(
                [w_gate[layer : layer + 1].astype(F32), jnp.zeros((15, WIDTH), F32)], axis=0
            ).astype(BF16)
            down_t[layer] = w_down[layer].T

    weights = (qkv_t, out_t, up_t, down_t)
    raw = (w_qkv, w_out, w_up, w_down)
    def sequence(item):
        tokens = slice(item * LEN, (item + 1) * LEN)
        segments = segment_masks(seg_ref[0, item : item + 1])
        hidden = x_ref[tokens].astype(F32).T
        middle_hidden, kept = yield from forward_layer(
            0, hidden, segments, weights, columns, mixed_scratch.at[item], total_scratch.at[item]
        )
        normed, query, keys, values, mixed, middle, normed_two, inner, logit = kept
        normed_ref[item] = normed
        qkv_ref[item, :WIDTH] = query
        qkv_ref[item, WIDTH : 2 * WIDTH] = keys
        qkv_ref[item, 2 * WIDTH :] = values
        mixed_ref[item] = mixed
        total_ref[item] = total_scratch[item]
        middle_ref[item] = middle
        normed_two_ref[item] = normed_two
        inner_ref[item] = inner
        logit_ref[item] = jnp.broadcast_to(logit, (8, LEN))
        output, kept = yield from forward_layer(
            1, middle_hidden, segments, weights, columns, mixed_scratch.at[item], total_scratch.at[item]
        )
        result_ref[tokens] = output.T.astype(BF16)
        gradient = cot_ref[tokens].astype(F32).T
        grad_ref[item] = yield from backward_layer(
            1, gradient, middle_hidden, segments, kept, total_scratch[item], raw, columns, pattern, totals,
            dk_ref.at[item], dv_ref.at[item],
        )

    together([sequence(item) for item in range(per_step)])

    @pl.when(pl.program_id(0) == pl.num_programs(0) - 1)
    def finish():
        write_totals(totals, grads_ref)


def second_kernel(
    per_step,
    x_ref, seg_ref, grad_ref, gains, shifts, w_qkv, qv_bias, w_out, out_bias, w_gate, w_up, up_bias, w_down, down_bias,
    pattern, normed_ref, qkv_ref, mixed_ref, total_ref, middle_ref, normed_two_ref, inner_ref, logit_ref,
    grad_inputs_ref, grads_ref,
    columns, dk_ref, dv_ref, *totals,
):
    @pl.when(pl.program_id(0) == 0)
    def start():
        clear_totals(totals)
        fill_columns(0, columns, gains, shifts, qv_bias, out_bias, w_gate, up_bias, down_bias)

    raw = (w_qkv, w_out, w_up, w_down)
    def sequence(item):
        tokens = slice(item * LEN, (item + 1) * LEN)
        segments = segment_masks(seg_ref[0, item : item + 1])
        hidden = x_ref[tokens].astype(F32).T
        kept = (
            normed_ref[item], qkv_ref[item, :WIDTH], qkv_ref[item, WIDTH : 2 * WIDTH], qkv_ref[item, 2 * WIDTH :],
            mixed_ref[item], middle_ref[item], normed_two_ref[item], inner_ref[item], logit_ref[item, 0:1],
        )
        gradient = yield from backward_layer(
            0, grad_ref[item], hidden, segments, kept, total_ref[item], raw, columns, pattern, totals,
            dk_ref.at[item], dv_ref.at[item],
        )
        grad_inputs_ref[tokens] = gradient.T

    together([sequence(item) for item in range(per_step)])

    @pl.when(pl.program_id(0) == pl.num_programs(0) - 1)
    def finish():
        write_totals(totals, grads_ref)


def totals_scratch():
    return [
        pltpu.VMEM((WIDTH, 3 * WIDTH), F32),
        pltpu.VMEM((WIDTH, WIDTH), F32),
        pltpu.VMEM((WIDTH, FF), F32),
        pltpu.VMEM((WIDTH, FF), F32),
        pltpu.VMEM((SUMS, WIDTH, WIDTH), F32),
        pltpu.VMEM((8, WIDTH), F32),
    ]


def head_pattern():
    rows = lax.broadcasted_iota(jnp.int32, (4, 16, LEN), 1)
    pairs = lax.broadcasted_iota(jnp.int32, (4, 16, LEN), 0)
    lanes = lax.broadcasted_iota(jnp.int32, (4, 16, LEN), 2)
    head = (pairs % 2) * 2 + lanes // HALF
    return ((rows < 12) & (rows % 4 == head)).astype(BF16)


def local_part(inputs, segment_ids, cotangent, *parameters, per_step=4):
    seqs = segment_ids.shape[0]
    per_step = min(per_step, seqs)
    steps = seqs // per_step
    segments = segment_ids.reshape(steps, per_step, LEN)
    pattern = head_pattern()
    tokens = pl.BlockSpec((per_step * LEN, WIDTH), lambda i: (i, 0))
    segment_spec = pl.BlockSpec((1, per_step, LEN), lambda i: (i, 0, 0))

    def whole(array):
        zero = (0,) * array.ndim
        return pl.BlockSpec(array.shape, lambda i: zero)

    def kept(rows):
        return pl.BlockSpec((per_step, rows, LEN), lambda i: (i, 0, 0))

    kept_shapes = [
        (WIDTH, BF16), (3 * WIDTH, BF16), (WIDTH, BF16), (HEADS, F32), (WIDTH, F32), (WIDTH, BF16), (FF, F32), (8, F32),
    ]
    kept_specs = [kept(rows) for rows, unused in kept_shapes]
    grads_spec = pl.BlockSpec((ROWS, WIDTH), lambda i: (0, 0))
    grads_shape = jax.ShapeDtypeStruct((ROWS, WIDTH), F32)
    params = pltpu.CompilerParams(vmem_limit_bytes=56 * 1024 * 1024)
    first = pl.pallas_call(
        lambda *refs: first_kernel(per_step, *refs),
        grid=(steps,),
        in_specs=[tokens, segment_spec, tokens] + [whole(entry) for entry in parameters] + [whole(pattern)],
        out_specs=[tokens, kept(WIDTH)] + kept_specs + [grads_spec],
        out_shape=[
            jax.ShapeDtypeStruct(inputs.shape, BF16),
            jax.ShapeDtypeStruct((seqs, WIDTH, LEN), F32),
        ]
        + [jax.ShapeDtypeStruct((seqs, rows, LEN), dtype) for rows, dtype in kept_shapes]
        + [grads_shape],
        scratch_shapes=[
            pltpu.VMEM((LAYERS, COLUMNS, WIDTH, WIDTH), F32),
            pltpu.VMEM((LAYERS, 3 * WIDTH, WIDTH), BF16),
            pltpu.VMEM((LAYERS, WIDTH, WIDTH), BF16),
            pltpu.VMEM((LAYERS, FF + 16, WIDTH), BF16),
            pltpu.VMEM((LAYERS, WIDTH, FF), BF16),
            pltpu.VMEM((per_step, WIDTH, LEN), F32),
            pltpu.VMEM((per_step, HEADS, LEN), F32),
            pltpu.VMEM((per_step, WIDTH, LEN), F32),
            pltpu.VMEM((per_step, WIDTH, LEN), F32),
        ]
        + totals_scratch(),
        compiler_params=params,
        name="forward_and_last_backward",
    )(inputs, segments, cotangent, *parameters, pattern)
    result, gradient, saved, grads_one = first[0], first[1], first[2:-1], first[-1]
    grad_inputs, grads_zero = pl.pallas_call(
        lambda *refs: second_kernel(per_step, *refs),
        grid=(steps,),
        in_specs=[tokens, segment_spec, kept(WIDTH)]
        + [whole(entry) for entry in parameters]
        + [whole(pattern)]
        + kept_specs,
        out_specs=[tokens, grads_spec],
        out_shape=[jax.ShapeDtypeStruct(inputs.shape, F32), grads_shape],
        scratch_shapes=[
            pltpu.VMEM((1, COLUMNS, WIDTH, WIDTH), F32),
            pltpu.VMEM((per_step, WIDTH, LEN), F32),
            pltpu.VMEM((per_step, WIDTH, LEN), F32),
        ]
        + totals_scratch(),
        compiler_params=params,
        name="first_backward",
    )(inputs, segments, gradient, *parameters, pattern, *saved)
    return result, grad_inputs, grads_zero, grads_one


def unpack(grads):
    small = grads[:, R_SMALL:]
    gains = jnp.stack([small[:, S_GAIN_ONE], small[:, S_GAIN_TWO]], axis=1)
    shifts = jnp.stack([small[:, S_SHIFT_ONE], small[:, S_SHIFT_TWO]], axis=1)
    qkv = jnp.concatenate([grads[:, R_QKV + i * WIDTH : R_QKV + (i + 1) * WIDTH] for i in range(3)], axis=2)
    up = jnp.concatenate([grads[:, R_UP + i * WIDTH : R_UP + (i + 1) * WIDTH] for i in range(2)], axis=2)
    return (
        gains,
        shifts,
        qkv,
        jnp.concatenate([small[:, SUMS], small[:, S_V]], axis=1),
        grads[:, R_OUT : R_OUT + WIDTH],
        small[:, S_OUT],
        small[:, S_GATE],
        up,
        jnp.concatenate([small[:, S_UP_LOW], small[:, S_UP_HIGH]], axis=1),
        grads[:, R_DOWN : R_DOWN + FF],
        small[:, S_DOWN],
    )


def all_sum(zero, one, size):
    me = lax.axis_index("seq")
    bits = size.bit_length() - 1

    def swap(value, bit):
        return lax.ppermute(value, "seq", [(i, i ^ (1 << bit)) for i in range(size)])

    halves = (zero, one)
    sides = []
    for bit in range(bits):
        side = (me >> bit) & 1
        if bit >= 3:
            current = current + swap(current, bit)
            continue
        sides.append(side)
        mine = jnp.where(side == 0, halves[0], halves[1])
        others = jnp.where(side == 0, halves[1], halves[0])
        current = mine + swap(others, bit)
        middle = current.shape[0] // 2
        halves = (current[:middle], current[middle:])
    for bit in reversed(range(min(bits, 3))):
        others = swap(current, bit)
        first = jnp.where(sides[bit] == 0, current, others)
        second = jnp.where(sides[bit] == 0, others, current)
        current = jnp.concatenate([first, second], axis=0)
    return current.reshape(LAYERS, ROWS, WIDTH)


def body(size, *arguments):
    result, grad_inputs, grads_zero, grads_one = local_part(*arguments)
    if size & (size - 1) or size < 2:
        grads = lax.psum(jnp.stack([grads_zero, grads_one]), "seq")
    else:
        grads = all_sum(grads_zero, grads_one, size)
    return (result, grad_inputs) + unpack(grads)


def solution(mesh):
    rows = P("seq", None)
    return jax.shard_map(
        lambda *arguments: body(mesh.shape["seq"], *arguments),
        mesh=mesh,
        in_specs=(rows, rows, rows) + (P(),) * 11,
        out_specs=(rows, rows) + (P(),) * 11,
        check_vma=False,
    )
```

```python
import jax
import jax.numpy as jnp
from jax import lax
from jax.experimental import pallas as pl
from jax.experimental.pallas import tpu as pltpu
from jax.sharding import PartitionSpec as P

HEADS = 8
LAYERS = 2
WIDTH = 128
FF = 256
LEN = 256
HALF = 128
CHUNK = 64
QUARTER = 64
WINDOWS = ((0, 128), (0, 192), (64, 256), (128, 256))
PLACES = ((0, 128), (256, 448), (640, 832), (1024, 1152))
POWER_ROWS = 1280
FAR = -1.0e9
GELU_A = 0.7978845608028654
GELU_B = 0.044715
F32 = jnp.float32
BF16 = jnp.bfloat16

GAIN_ONE, SHIFT_ONE, GAIN_TWO, SHIFT_TWO, OUT_BIAS, DOWN_BIAS, Q_BIAS, V_BIAS, GATE, UP_LOW, UP_HIGH = range(11)
COLUMNS = 11
S_GAIN_ONE, S_SHIFT_ONE, S_GAIN_TWO, S_SHIFT_TWO, S_DOWN, S_GATE = range(6)
SUMS = 6
S_OUT, S_Q, S_K, S_V, S_UP_LOW, S_UP_HIGH, SMALL = range(6, 13)
R_QKV, R_OUT, R_UP, R_DOWN, R_SMALL, ROWS = 0, 384, 512, 768, 1024, 1056


def dot(left, right):
    return lax.dot_general(left, right, (((1,), (0,)), ((), ())), preferred_element_type=F32)


def both(column):
    return jnp.concatenate([column, column], axis=1)


def fold(value):
    return value[:, :HALF] + value[:, HALF:]


def zeros(rows, lanes=LEN):
    return jnp.zeros((rows, lanes), BF16)


def ones(rows, lanes=LEN):
    return jnp.ones((rows, lanes), BF16)


def split_three(value):
    high = value.astype(BF16)
    rest = value - high.astype(F32)
    middle = rest.astype(BF16)
    low = (rest - middle.astype(F32)).astype(BF16)
    return high, middle, low


def norm_parts(value):
    average = jnp.sum(value, axis=0, keepdims=True) * (1.0 / WIDTH)
    centered = value - average
    variance = jnp.sum(centered * centered, axis=0, keepdims=True) * (1.0 / WIDTH)
    scale = lax.rsqrt(variance + 1e-05)
    return centered * scale, scale


def lane_mask(rows, which):
    row = lax.broadcasted_iota(jnp.int32, (rows, HALF), 0)
    lane = lax.broadcasted_iota(jnp.int32, (rows, HALF), 1)
    return jnp.where(which(row, lane < QUARTER), 1.0, 0.0).astype(BF16)


def turned(rows):
    return jnp.concatenate(
        [rows[:, 64:128], rows[:, :64], rows[:, 192:256], rows[:, 128:192]], axis=1
    )


def make_masks():
    low = lane_mask(16, lambda row, left: left)
    high = lane_mask(16, lambda row, left: ~left)
    heads = [
        lane_mask(16, lambda row, left, head=head: (row % 4 == head) & (left if head % 2 == 0 else ~left))
        for head in range(4)
    ]
    return low, high, heads


def halves_of(rows, masks):
    low, high, unused = masks
    count = rows.shape[0] // 16
    low_all = jnp.concatenate([both(low)] * count, axis=0)
    high_all = jnp.concatenate([both(high)] * count, axis=0)
    other = turned(rows)
    return ((rows * low_all, other * high_all), (other * low_all, rows * high_all))


def head_block(variants, block, group):
    lanes = slice((block // 2) * HALF, (block // 2 + 1) * HALF)
    gap = zeros(16, HALF)
    pieces = []
    for head in range(4):
        first = QUARTER * group + 16 * head
        piece = variants[block % 2][head % 2][first : first + 16, lanes]
        pieces.append(jnp.concatenate([piece, gap] if head < 2 else [gap, piece], axis=1))
    return jnp.concatenate(pieces, axis=0)


def with_extra(features, extra):
    return jnp.concatenate([features, extra], axis=0)


def spread_marks(rows, masks, block):
    low, high, unused = masks
    lanes = slice((block // 2) * HALF, (block // 2 + 1) * HALF)
    here, there = rows[:, lanes], turned(rows)[:, lanes]
    once = here * low + there * high if block % 2 == 0 else there * low + here * high
    return both(once)


def spread_rows(rows, masks, block):
    unused, unused, heads = masks
    lanes = slice((block // 2) * HALF, (block // 2 + 1) * HALF)
    here, there = rows[:, lanes], turned(rows)[:, lanes]
    if block % 2 == 1:
        here, there = there, here
    return jnp.concatenate([here * heads[0] + there * heads[1], here * heads[2] + there * heads[3]], axis=1)


def join_blocks(even, odd, head):
    left = lax.broadcasted_iota(jnp.int32, even.shape, 1) < QUARTER
    if head % 2 == 0:
        return jnp.where(left, even, pltpu.roll(odd, QUARTER, 1))
    return jnp.where(left, pltpu.roll(even, QUARTER, 1), odd)


def token_rows(rows, extra):
    return [
        jnp.concatenate([rows[QUARTER * group : QUARTER * group + QUARTER], extra], axis=0).T for group in range(2)
    ]


def skewed(units):
    running, waiting = [], list(units)
    while running or waiting:
        if waiting:
            running.insert(0, waiting.pop(0))
        running = [unit for unit in running if next(unit, "end") != "end"]
        yield


def together(parts):
    running = list(parts)
    while running:
        running = [part for part in running if next(part, "end") != "end"]


def segment_masks(segments):
    ids = lax.broadcasted_iota(jnp.int32, (16, LEN), 0)
    same = ids == segments
    one_hot = jnp.where(same, 1.0, 0.0).astype(BF16)
    other = jnp.where(same | (ids >= 8), 0.0, FAR).astype(BF16)
    return one_hot, other


def forward_unit(block, group, keys_rows, variants, values, marks, power_ref, mixed_ref, scale_ref, results):
    first, last = WINDOWS[block]
    weights = with_extra(head_block(variants, block, group), marks[block])
    scores = dot(keys_rows[first:last], weights)
    yield
    peak = jnp.max(scores, axis=0, keepdims=True)
    powers = jnp.exp(scores - peak).astype(BF16)
    start = PLACES[block][group]
    power_ref[start : start + last - first] = powers
    yield
    rows = values[QUARTER * group : QUARTER * group + QUARTER, first:last]
    mixed = dot(jnp.concatenate([rows, ones(16, last - first)], axis=0), powers)
    yield
    scale = 1.0 / mixed[QUARTER : QUARTER + 8]
    results[block, group] = (mixed, scale)
    if block % 2 == 0:
        return
    even, even_scale = results[block - 1, group]
    lanes = slice((block // 2) * HALF, (block // 2 + 1) * HALF)
    for head in range(4):
        tile = slice((head // 2) * HALF, (head // 2 + 1) * HALF)
        rows = slice(16 * head, 16 * head + 16)
        factor = join_blocks(even_scale[:, tile], scale[:, tile], head)
        joined = join_blocks(even[rows, tile], mixed[rows, tile], head)
        place = QUARTER * group + 16 * head
        mixed_ref[place : place + 16, lanes] = joined * jnp.concatenate([factor, factor], axis=0)
        place = 8 * (4 * group + head)
        scale_ref[place : place + 8, lanes] = factor


def attention_forward(query, keys, values, segments, masks, power_ref, mixed_ref, scale_ref):
    one_hot, other = segments
    rows = token_rows(keys, other)
    variants = halves_of(query, masks)
    marks = [spread_marks(one_hot, masks, block) for block in range(4)]
    yield
    results = {}
    yield from skewed(
        forward_unit(block, group, rows[group], variants, values, marks, power_ref, mixed_ref, scale_ref, results)
        for block in (0, 1, 2, 3)
        for group in range(2)
    )


def forward_layer(layer, hidden, segments, masks, weights, columns, power_ref, mixed_ref, scale_ref):
    qkv_t, out_t, up_t, down_t = weights
    column = lambda which: both(columns[layer, which])
    xhat, unused = norm_parts(hidden)
    normed = (xhat * column(GAIN_ONE) + column(SHIFT_ONE)).astype(BF16)
    yield
    projected = dot(qkv_t[layer], normed)
    yield
    query = (projected[:WIDTH] + column(Q_BIAS)).astype(BF16)
    keys = projected[WIDTH : 2 * WIDTH].astype(BF16)
    values = (projected[2 * WIDTH :] + column(V_BIAS)).astype(BF16)
    yield from attention_forward(query, keys, values, segments, masks, power_ref, mixed_ref, scale_ref)
    mixed = mixed_ref[...].astype(BF16)
    middle = hidden + (dot(out_t[layer], mixed) + column(OUT_BIAS))
    yield
    xhat_two, unused = norm_parts(middle)
    normed_two = (xhat_two * column(GAIN_TWO) + column(SHIFT_TWO)).astype(BF16)
    yield
    inner = dot(up_t[layer], normed_two)
    yield
    logit = inner[FF : FF + 1]
    inner = inner[:FF] + jnp.concatenate([column(UP_LOW), column(UP_HIGH)], axis=0)
    gate = jax.nn.sigmoid(logit)
    parts = []
    for start in range(0, FF, CHUNK):
        gated = inner[start : start + CHUNK] * gate
        power = jnp.tanh(gated * (GELU_A + (GELU_A * GELU_B) * (gated * gated)))
        parts.append((gated * (0.5 + 0.5 * power)).astype(BF16))
        yield
    active = jnp.concatenate(parts, axis=0)
    output = middle + (dot(down_t[layer], active) + column(DOWN_BIAS))
    return output, (normed, query, keys, values, mixed, middle, normed_two, inner, logit)


def norm_backward(gradient, xhat, scale, gain):
    inner = gradient * gain
    first = jnp.sum(inner, axis=0, keepdims=True) * (1.0 / WIDTH)
    second = jnp.sum(inner * xhat, axis=0, keepdims=True) * (1.0 / WIDTH)
    return scale * (inner - first - xhat * second)


def backward_unit(block, values_rows, query_variants, grad_variants, keys, deltas, power_ref, results, dq_ref):
    first, last = WINDOWS[block]
    query_blocks = [head_block(query_variants, block, group) for group in range(2)]
    grad_blocks = [head_block(grad_variants, block, group) for group in range(2)]
    products = [
        dot(values_rows[group][first:last], with_extra(grad_blocks[group], deltas[block][group]))
        for group in range(2)
    ]
    yield
    powers, grad_scores = [], []
    for group in range(2):
        start = PLACES[block][group]
        powers.append(power_ref[start : start + last - first])
        grad_scores.append((powers[group].astype(F32) * products[group]).astype(BF16))
        yield
    mixed = [
        dot(keys[QUARTER * group : QUARTER * group + QUARTER, first:last], grad_scores[group]) for group in range(2)
    ]

    def together_rows(blocks):
        gap = zeros(QUARTER)
        low = jnp.concatenate([blocks[0], gap], axis=0)
        high = jnp.concatenate([gap, blocks[1]], axis=0)
        return jnp.concatenate([low, high], axis=1)

    grad_keys = dot(jnp.concatenate(grad_scores, axis=1), together_rows(query_blocks).T)
    grad_values = dot(jnp.concatenate(powers, axis=1), together_rows(grad_blocks).T)
    results[block] = (grad_keys, grad_values, mixed)
    yield
    if block % 2 == 0:
        return
    lanes = slice((block // 2) * HALF, (block // 2 + 1) * HALF)
    for group in range(2):
        even, odd = results[block - 1][2][group], mixed[group]
        for head in range(4):
            tile = slice((head // 2) * HALF, (head // 2 + 1) * HALF)
            rows = slice(16 * head, 16 * head + 16)
            place = QUARTER * group + 16 * head
            dq_ref[place : place + 16, lanes] = join_blocks(even[rows, tile], odd[rows, tile], head)


def attention_backward(query, keys, values, mixed, scale, grad_mixed, masks, power_ref, dq_ref):
    factors = [scale[8 * head : 8 * head + 8] for head in range(HEADS)]
    grad = (grad_mixed * jnp.concatenate([row for factor in factors for row in (factor, factor)], axis=0)).astype(BF16)
    product = grad.astype(F32) * mixed.astype(F32)
    delta = jnp.concatenate(
        [jnp.sum(product[16 * head : 16 * head + 16], axis=0, keepdims=True) for head in range(HEADS)], axis=0
    )
    yield
    parts = [part.astype(F32) for part in split_three(-delta)]
    gap = jnp.zeros((4, LEN), F32)
    extras = [
        jnp.concatenate([part[4 * group : 4 * group + 4] for part in parts] + [gap], axis=0).astype(BF16)
        for group in range(2)
    ]
    deltas = [[spread_rows(extras[group], masks, block) for group in range(2)] for block in range(4)]
    query_variants = halves_of(query, masks)
    grad_variants = halves_of(grad, masks)
    rows = token_rows(values, ones(16))
    yield
    results = {}
    yield from skewed(
        backward_unit(block, rows, query_variants, grad_variants, keys, deltas, power_ref, results, dq_ref)
        for block in range(4)
    )

    def collect(which):
        parts = [results[block][which] for block in range(4)]
        return jnp.concatenate(
            [
                parts[0][:64] + parts[1][:64],
                parts[0][64:] + parts[1][64:128] + parts[2][:64],
                parts[1][128:] + parts[2][64:128] + parts[3][:64],
                parts[2][128:] + parts[3][64:],
            ],
            axis=0,
        ).astype(BF16)

    return (dq_ref[...] * 0.25).astype(BF16), collect(0), collect(1)


def backward_layer(
    layer, gradient, hidden, masks, kept, power_ref, scale_ref, raw, columns, totals, dq_ref
):
    w_qkv, w_out, w_up, w_down = raw
    normed, query, keys, values, mixed, middle, normed_two, inner, logit = kept
    qkv_total, out_total, up_total, down_total, sums = totals
    column = lambda which: both(columns[layer, which])
    branch = gradient.astype(BF16)
    sums[S_DOWN] += fold(branch.astype(F32))
    grad_active = dot(w_down[layer], branch)
    yield
    gate = jax.nn.sigmoid(logit)
    actives, inners = [], []
    logit_sum = jnp.zeros((1, LEN), F32)
    for start in range(0, FF, CHUNK):
        rows = slice(start, start + CHUNK)
        gated = inner[rows] * gate
        square = gated * gated
        power = jnp.tanh(gated * (GELU_A + (GELU_A * GELU_B) * square))
        half_up = 0.5 + 0.5 * power
        active = gated * half_up
        slope = half_up + (active * (1.0 - power)) * (GELU_A + (3.0 * GELU_A * GELU_B) * square)
        grad_gated = grad_active[rows].astype(BF16).astype(F32) * slope
        logit_sum = logit_sum + jnp.sum(grad_gated * inner[rows], axis=0, keepdims=True)
        actives.append(active.astype(BF16))
        inners.append((grad_gated * gate).astype(BF16))
        yield
    grad_logit = logit_sum * (gate * (1.0 - gate))
    active = jnp.concatenate(actives, axis=0)
    grad_inner = jnp.concatenate(inners, axis=0)
    grad_two = dot(w_up[layer], grad_inner) + column(GATE) * grad_logit
    down_total[...] += dot(branch, active.T)
    up_total[...] += dot(jnp.concatenate([normed_two, ones(16)], axis=0), grad_inner.T)
    sums[S_GATE] += fold(normed_two.astype(F32) * grad_logit)
    yield
    xhat, scale = norm_parts(middle)
    sums[S_GAIN_TWO] += fold(grad_two * xhat)
    sums[S_SHIFT_TWO] += fold(grad_two)
    grad_middle = gradient + norm_backward(grad_two, xhat, scale, column(GAIN_TWO))
    attended = grad_middle.astype(BF16)
    yield
    grad_mixed = dot(w_out[layer], attended)
    out_total[...] += dot(jnp.concatenate([mixed, ones(16)], axis=0), attended.T)
    yield
    grad_query, grad_keys, grad_values = yield from attention_backward(
        query, keys, values, mixed, scale_ref[...], grad_mixed, masks, power_ref, dq_ref
    )
    yield
    grad_rows = jnp.concatenate([grad_query.T, grad_keys, grad_values], axis=1)
    qkv_total[...] += dot(jnp.concatenate([normed, ones(16)], axis=0), grad_rows)
    grad_one = dot(w_qkv[layer], jnp.concatenate([grad_query, grad_keys.T, grad_values.T], axis=0))
    yield
    xhat, scale = norm_parts(hidden)
    sums[S_GAIN_ONE] += fold(grad_one * xhat)
    sums[S_SHIFT_ONE] += fold(grad_one)
    return grad_middle + norm_backward(grad_one, xhat, scale, column(GAIN_ONE))


def spread(row):
    return jnp.broadcast_to(row, (WIDTH, WIDTH)).T


def fill_columns(layer, columns, gains, shifts, qv_bias, out_bias, w_gate, up_bias, down_bias):
    columns[layer, GAIN_ONE] = spread(gains[layer, 0:1])
    columns[layer, GAIN_TWO] = spread(gains[layer, 1:2])
    columns[layer, SHIFT_ONE] = spread(shifts[layer, 0:1])
    columns[layer, SHIFT_TWO] = spread(shifts[layer, 1:2])
    columns[layer, OUT_BIAS] = spread(out_bias[layer : layer + 1])
    columns[layer, DOWN_BIAS] = spread(down_bias[layer : layer + 1])
    columns[layer, Q_BIAS] = spread(qv_bias[layer : layer + 1, :WIDTH]) * 0.25
    columns[layer, V_BIAS] = spread(qv_bias[layer : layer + 1, WIDTH:])
    columns[layer, GATE] = spread(w_gate[layer : layer + 1].astype(F32))
    columns[layer, UP_LOW] = spread(up_bias[layer : layer + 1, :WIDTH])
    columns[layer, UP_HIGH] = spread(up_bias[layer : layer + 1, WIDTH:])


def clear_totals(totals):
    for ref in totals:
        ref[...] = jnp.zeros_like(ref)


def write_totals(totals, grads_ref):
    qkv_total, out_total, up_total, down_total, sums = totals
    for part in range(3):
        rows = slice(R_QKV + part * WIDTH, R_QKV + (part + 1) * WIDTH)
        grads_ref[rows] = qkv_total[:WIDTH, part * WIDTH : (part + 1) * WIDTH]
    grads_ref[R_OUT : R_OUT + WIDTH] = out_total[:WIDTH]
    for part in range(2):
        lanes = slice(part * WIDTH, (part + 1) * WIDTH)
        grads_ref[R_UP + part * WIDTH : R_UP + (part + 1) * WIDTH] = up_total[:WIDTH, lanes]
        grads_ref[R_DOWN + part * WIDTH : R_DOWN + (part + 1) * WIDTH] = down_total[:, lanes].T
    rows = [jnp.sum(sums[which].T, axis=0, keepdims=True) for which in range(SUMS)]
    rows.append(out_total[WIDTH : WIDTH + 1])
    rows.extend(qkv_total[WIDTH : WIDTH + 1, part * WIDTH : (part + 1) * WIDTH] for part in range(3))
    rows.extend(up_total[WIDTH : WIDTH + 1, part * WIDTH : (part + 1) * WIDTH] for part in range(2))
    rows.append(jnp.zeros((ROWS - R_SMALL - len(rows), WIDTH), F32))
    grads_ref[R_SMALL:ROWS] = jnp.concatenate(rows, axis=0)


def kernel(
    per_step, steps,
    x_ref, seg_ref, cot_ref, gains, shifts, w_qkv, qv_bias, w_out, out_bias, w_gate, w_up, up_bias, w_down, down_bias,
    result_ref, grad_inputs_ref, grads_ref,
    columns, qkv_t, out_t, up_t, down_t, mixed_scratch, dq_ref, power_last, scale_last,
    grad_kept, normed_kept, qkv_kept, mixed_kept, scale_kept, middle_kept, normed_two_kept, inner_kept, logit_kept,
    power_kept, *totals,
):
    step = pl.program_id(0)
    totals_zero, totals_one = totals[: len(totals) // 2], totals[len(totals) // 2 :]

    @pl.when(step == 0)
    def start():
        clear_totals(totals)
        for layer in range(LAYERS):
            fill_columns(layer, columns, gains, shifts, qv_bias, out_bias, w_gate, up_bias, down_bias)
            qkv_t[layer, :WIDTH] = (w_qkv[layer][:, :WIDTH] * jnp.asarray(0.25, BF16)).T
            qkv_t[layer, WIDTH:] = w_qkv[layer][:, WIDTH:].T
            out_t[layer] = w_out[layer].T
            up_t[layer, :FF] = w_up[layer].T
            up_t[layer, FF:] = jnp.concatenate(
                [w_gate[layer : layer + 1].astype(F32), jnp.zeros((15, WIDTH), F32)], axis=0
            ).astype(BF16)
            down_t[layer] = w_down[layer].T

    masks = make_masks()
    weights = (qkv_t, out_t, up_t, down_t)
    raw = (w_qkv, w_out, w_up, w_down)

    def upward(item):
        tokens = slice(item * LEN, (item + 1) * LEN)
        place = step * per_step + item
        segments = segment_masks(seg_ref[0, item : item + 1])
        hidden = x_ref[tokens].astype(F32).T
        middle_hidden, kept = yield from forward_layer(
            0, hidden, segments, masks, weights, columns, power_kept.at[place], mixed_scratch.at[item],
            scale_kept.at[place],
        )
        normed, query, keys, values, mixed, middle, normed_two, inner, logit = kept
        normed_kept[place] = normed
        qkv_kept[place, :WIDTH] = query
        qkv_kept[place, WIDTH : 2 * WIDTH] = keys
        qkv_kept[place, 2 * WIDTH :] = values
        mixed_kept[place] = mixed
        middle_kept[place] = middle
        normed_two_kept[place] = normed_two
        inner_kept[place] = inner
        logit_kept[place] = jnp.broadcast_to(logit, (8, LEN))
        output, kept = yield from forward_layer(
            1, middle_hidden, segments, masks, weights, columns, power_last.at[item], mixed_scratch.at[item],
            scale_last.at[item],
        )
        result_ref[tokens] = output.T.astype(BF16)
        gradient = cot_ref[tokens].astype(F32).T
        grad_kept[place] = yield from backward_layer(
            1, gradient, middle_hidden, masks, kept, power_last.at[item], scale_last.at[item], raw, columns,
            totals_one, dq_ref.at[item],
        )

    def downward(item):
        tokens = slice(item * LEN, (item + 1) * LEN)
        place = (step - steps) * per_step + item
        hidden = x_ref[tokens].astype(F32).T
        kept = (
            normed_kept[place], qkv_kept[place, :WIDTH], qkv_kept[place, WIDTH : 2 * WIDTH],
            qkv_kept[place, 2 * WIDTH :], mixed_kept[place], middle_kept[place], normed_two_kept[place],
            inner_kept[place], logit_kept[place, 0:1],
        )
        gradient = yield from backward_layer(
            0, grad_kept[place], hidden, masks, kept, power_kept.at[place], scale_kept.at[place], raw, columns,
            totals_zero, dq_ref.at[item],
        )
        grad_inputs_ref[tokens] = gradient.T

    @pl.when(step < steps)
    def first_half():
        together([upward(item) for item in range(per_step)])

    @pl.when(step >= steps)
    def second_half():
        together([downward(item) for item in range(per_step)])

    @pl.when(step == 2 * steps - 1)
    def finish():
        write_totals(totals_zero, grads_ref.at[0])
        write_totals(totals_one, grads_ref.at[1])


def totals_scratch():
    return [
        pltpu.VMEM((WIDTH + 16, 3 * WIDTH), F32),
        pltpu.VMEM((WIDTH + 16, WIDTH), F32),
        pltpu.VMEM((WIDTH + 16, FF), F32),
        pltpu.VMEM((WIDTH, FF), F32),
        pltpu.VMEM((SUMS, WIDTH, WIDTH), F32),
    ]


def local_part(inputs, segment_ids, cotangent, *parameters, per_step=4):
    seqs = segment_ids.shape[0]
    per_step = min(per_step, seqs)
    steps = seqs // per_step
    segments = segment_ids.reshape(steps, per_step, LEN)
    rows = (per_step * LEN, WIDTH)

    def whole(array):
        zero = (0,) * array.ndim
        return pl.BlockSpec(array.shape, lambda i: zero)

    def kept(rows, dtype, count=seqs):
        return pltpu.VMEM((count, rows, LEN), dtype)

    return pl.pallas_call(
        lambda *refs: kernel(per_step, steps, *refs),
        grid=(2 * steps,),
        in_specs=[
            pl.BlockSpec(rows, lambda i: (i % steps, 0)),
            pl.BlockSpec((1, per_step, LEN), lambda i: (i % steps, 0, 0)),
            pl.BlockSpec(rows, lambda i: (jnp.minimum(i, steps - 1), 0)),
        ]
        + [whole(entry) for entry in parameters],
        out_specs=[
            pl.BlockSpec(rows, lambda i: (jnp.minimum(i, steps - 1), 0)),
            pl.BlockSpec(rows, lambda i: (jnp.maximum(i - steps, 0), 0)),
            pl.BlockSpec((LAYERS, ROWS, WIDTH), lambda i: (0, 0, 0)),
        ],
        out_shape=[
            jax.ShapeDtypeStruct(inputs.shape, BF16),
            jax.ShapeDtypeStruct(inputs.shape, F32),
            jax.ShapeDtypeStruct((LAYERS, ROWS, WIDTH), F32),
        ],
        scratch_shapes=[
            pltpu.VMEM((LAYERS, COLUMNS, WIDTH, WIDTH), F32),
            pltpu.VMEM((LAYERS, 3 * WIDTH, WIDTH), BF16),
            pltpu.VMEM((LAYERS, WIDTH, WIDTH), BF16),
            pltpu.VMEM((LAYERS, FF + 16, WIDTH), BF16),
            pltpu.VMEM((LAYERS, WIDTH, FF), BF16),
            kept(WIDTH, F32, per_step),
            kept(WIDTH, F32, per_step),
            kept(POWER_ROWS, BF16, per_step),
            kept(8 * HEADS, F32, per_step),
            kept(WIDTH, F32),
            kept(WIDTH, BF16),
            kept(3 * WIDTH, BF16),
            kept(WIDTH, BF16),
            kept(8 * HEADS, F32),
            kept(WIDTH, F32),
            kept(WIDTH, BF16),
            kept(FF, F32),
            kept(8, F32),
            kept(POWER_ROWS, BF16),
        ]
        + totals_scratch()
        + totals_scratch(),
        compiler_params=pltpu.CompilerParams(vmem_limit_bytes=60 * 1024 * 1024),
        name="layers",
    )(inputs, segments, cotangent, *parameters)


def unpack(grads):
    small = grads[:, R_SMALL:]
    gains = jnp.stack([small[:, S_GAIN_ONE], small[:, S_GAIN_TWO]], axis=1)
    shifts = jnp.stack([small[:, S_SHIFT_ONE], small[:, S_SHIFT_TWO]], axis=1)
    qkv = jnp.concatenate([grads[:, R_QKV + i * WIDTH : R_QKV + (i + 1) * WIDTH] for i in range(3)], axis=2)
    up = jnp.concatenate([grads[:, R_UP + i * WIDTH : R_UP + (i + 1) * WIDTH] for i in range(2)], axis=2)
    return (
        gains,
        shifts,
        qkv,
        jnp.concatenate([small[:, S_Q], small[:, S_V]], axis=1),
        grads[:, R_OUT : R_OUT + WIDTH],
        small[:, S_OUT],
        small[:, S_GATE],
        up,
        jnp.concatenate([small[:, S_UP_LOW], small[:, S_UP_HIGH]], axis=1),
        grads[:, R_DOWN : R_DOWN + FF],
        small[:, S_DOWN],
    )


def all_sum(grads, size):
    me = lax.axis_index("seq")
    bits = size.bit_length() - 1

    def swap(value, bit):
        return lax.ppermute(value, "seq", [(i, i ^ (1 << bit)) for i in range(size)])

    halves = (grads[0], grads[1])
    sides = []
    for bit in range(bits):
        side = (me >> bit) & 1
        if bit >= 3:
            current = current + swap(current, bit)
            continue
        sides.append(side)
        mine = jnp.where(side == 0, halves[0], halves[1])
        others = jnp.where(side == 0, halves[1], halves[0])
        current = mine + swap(others, bit)
        middle = current.shape[0] // 2
        halves = (current[:middle], current[middle:])
    for bit in reversed(range(min(bits, 3))):
        others = swap(current, bit)
        first = jnp.where(sides[bit] == 0, current, others)
        second = jnp.where(sides[bit] == 0, others, current)
        current = jnp.concatenate([first, second], axis=0)
    return current.reshape(LAYERS, ROWS, WIDTH)


def body(size, *arguments):
    result, grad_inputs, grads = local_part(*arguments)
    if size & (size - 1) or size < 2:
        grads = lax.psum(grads, "seq")
    else:
        grads = all_sum(grads, size)
    return (result, grad_inputs) + unpack(grads)


def solution(mesh):
    rows = P("seq", None)
    return jax.shard_map(
        lambda *arguments: body(mesh.shape["seq"], *arguments),
        mesh=mesh,
        in_specs=(rows, rows, rows) + (P(),) * 11,
        out_specs=(rows, rows) + (P(),) * 11,
        check_vma=False,
    )
```

```python
import jax
import jax.numpy as jnp
from jax import lax
from jax.experimental import pallas as pl
from jax.experimental.pallas import tpu as pltpu
from jax.sharding import PartitionSpec as P

HEADS = 8
LAYERS = 2
WIDTH = 128
FF = 256
LEN = 256
HALF = 128
CHUNK = 64
QUARTER = 64
WINDOWS = ((0, 128), (0, 192), (64, 256), (128, 256))
PLACES = ((0, 128), (256, 448), (640, 832), (1024, 1152))
POWER_ROWS = 1280
FAR = -1.0e9
GELU_A = 0.7978845608028654
GELU_B = 0.044715
F32 = jnp.float32
BF16 = jnp.bfloat16

GAIN_ONE, SHIFT_ONE, GAIN_TWO, SHIFT_TWO, OUT_BIAS, DOWN_BIAS, Q_BIAS, V_BIAS, GATE, UP_LOW, UP_HIGH = range(11)
COLUMNS = 11
S_GAIN_ONE, S_SHIFT_ONE, S_GAIN_TWO, S_SHIFT_TWO, S_DOWN, S_GATE = range(6)
SUMS = 6
S_OUT, S_Q, S_K, S_V, S_UP_LOW, S_UP_HIGH, SMALL = range(6, 13)
R_QKV, R_OUT, R_UP, R_DOWN, R_SMALL, ROWS = 0, 384, 512, 768, 1024, 1056


def dot(left, right):
    return lax.dot_general(left, right, (((1,), (0,)), ((), ())), preferred_element_type=F32)


def both(column):
    return jnp.concatenate([column, column], axis=1)


def fold(value):
    return value[:, :HALF] + value[:, HALF:]


def zeros(rows, lanes=LEN):
    return jnp.zeros((rows, lanes), BF16)


def ones(rows, lanes=LEN):
    return jnp.ones((rows, lanes), BF16)


def split_three(value):
    high = value.astype(BF16)
    rest = value - high.astype(F32)
    middle = rest.astype(BF16)
    low = (rest - middle.astype(F32)).astype(BF16)
    return high, middle, low


def norm_parts(value):
    average = jnp.sum(value, axis=0, keepdims=True) * (1.0 / WIDTH)
    centered = value - average
    variance = jnp.sum(centered * centered, axis=0, keepdims=True) * (1.0 / WIDTH)
    scale = lax.rsqrt(variance + 1e-05)
    return centered * scale, scale


def lane_mask(rows, which):
    row = lax.broadcasted_iota(jnp.int32, (rows, HALF), 0)
    lane = lax.broadcasted_iota(jnp.int32, (rows, HALF), 1)
    return jnp.where(which(row, lane < QUARTER), 1.0, 0.0).astype(BF16)


def turned(rows):
    return jnp.concatenate(
        [rows[:, 64:128], rows[:, :64], rows[:, 192:256], rows[:, 128:192]], axis=1
    )


def make_masks():
    low = lane_mask(16, lambda row, left: left)
    high = lane_mask(16, lambda row, left: ~left)
    heads = [
        lane_mask(16, lambda row, left, head=head: (row % 4 == head) & (left if head % 2 == 0 else ~left))
        for head in range(4)
    ]
    return low, high, heads


def halves_of(rows, masks):
    low, high, unused = masks
    count = rows.shape[0] // 16
    low_all = jnp.concatenate([both(low)] * count, axis=0)
    high_all = jnp.concatenate([both(high)] * count, axis=0)
    other = turned(rows)
    return ((rows * low_all, other * high_all), (other * low_all, rows * high_all))


def head_block(variants, block, group):
    lanes = slice((block // 2) * HALF, (block // 2 + 1) * HALF)
    gap = zeros(16, HALF)
    pieces = []
    for head in range(4):
        first = QUARTER * group + 16 * head
        piece = variants[block % 2][head % 2][first : first + 16, lanes]
        pieces.append(jnp.concatenate([piece, gap] if head < 2 else [gap, piece], axis=1))
    return jnp.concatenate(pieces, axis=0)


def with_extra(features, extra):
    return jnp.concatenate([features, extra], axis=0)


def spread_marks(rows, masks, block):
    low, high, unused = masks
    lanes = slice((block // 2) * HALF, (block // 2 + 1) * HALF)
    here, there = rows[:, lanes], turned(rows)[:, lanes]
    once = here * low + there * high if block % 2 == 0 else there * low + here * high
    return both(once)


def spread_rows(rows, masks, block):
    unused, unused, heads = masks
    lanes = slice((block // 2) * HALF, (block // 2 + 1) * HALF)
    here, there = rows[:, lanes], turned(rows)[:, lanes]
    if block % 2 == 1:
        here, there = there, here
    return jnp.concatenate([here * heads[0] + there * heads[1], here * heads[2] + there * heads[3]], axis=1)


def join_blocks(even, odd, head):
    left = lax.broadcasted_iota(jnp.int32, even.shape, 1) < QUARTER
    if head % 2 == 0:
        return jnp.where(left, even, pltpu.roll(odd, QUARTER, 1))
    return jnp.where(left, pltpu.roll(even, QUARTER, 1), odd)


def token_rows(rows, extra):
    return [
        jnp.concatenate([rows[QUARTER * group : QUARTER * group + QUARTER], extra], axis=0).T for group in range(2)
    ]


def skewed(units):
    running, waiting = [], list(units)
    while running or waiting:
        if waiting:
            running.insert(0, waiting.pop(0))
        running = [unit for unit in running if next(unit, "end") != "end"]
        yield


def together(parts):
    running = list(parts)
    while running:
        running = [part for part in running if next(part, "end") != "end"]


def segment_masks(segments):
    ids = lax.broadcasted_iota(jnp.int32, (16, LEN), 0)
    same = ids == segments
    one_hot = jnp.where(same, 1.0, 0.0).astype(BF16)
    other = jnp.where(same | (ids >= 8), 0.0, FAR).astype(BF16)
    return one_hot, other


def forward_unit(block, group, keys_rows, variants, values, marks, power_ref, mixed_ref, scale_ref, results):
    first, last = WINDOWS[block]
    weights = with_extra(head_block(variants, block, group), marks[block])
    scores = dot(keys_rows[first:last], weights)
    yield
    peak = jnp.max(scores, axis=0, keepdims=True)
    powers = jnp.exp(scores - peak).astype(BF16)
    start = PLACES[block][group]
    power_ref[start : start + last - first] = powers
    yield
    rows = values[QUARTER * group : QUARTER * group + QUARTER, first:last]
    mixed = dot(jnp.concatenate([rows, ones(16, last - first)], axis=0), powers)
    yield
    scale = 1.0 / mixed[QUARTER : QUARTER + 8]
    results[block, group] = (mixed, scale)
    if block % 2 == 0:
        return
    even, even_scale = results[block - 1, group]
    lanes = slice((block // 2) * HALF, (block // 2 + 1) * HALF)
    for head in range(4):
        tile = slice((head // 2) * HALF, (head // 2 + 1) * HALF)
        rows = slice(16 * head, 16 * head + 16)
        factor = join_blocks(even_scale[:, tile], scale[:, tile], head)
        joined = join_blocks(even[rows, tile], mixed[rows, tile], head)
        place = QUARTER * group + 16 * head
        mixed_ref[place : place + 16, lanes] = joined * jnp.concatenate([factor, factor], axis=0)
        place = 8 * (4 * group + head)
        scale_ref[place : place + 8, lanes] = factor


def attention_forward(query, keys, values, segments, masks, power_ref, mixed_ref, scale_ref):
    one_hot, other = segments
    rows = token_rows(keys, other)
    variants = halves_of(query, masks)
    marks = [spread_marks(one_hot, masks, block) for block in range(4)]
    yield
    results = {}
    yield from skewed(
        forward_unit(block, group, rows[group], variants, values, marks, power_ref, mixed_ref, scale_ref, results)
        for block in (0, 1, 2, 3)
        for group in range(2)
    )


def forward_layer(layer, hidden, segments, masks, weights, columns, power_ref, mixed_ref, scale_ref):
    qkv_t, out_t, up_t, down_t = weights
    column = lambda which: both(columns[layer, which])
    xhat, unused = norm_parts(hidden)
    normed = (xhat * column(GAIN_ONE) + column(SHIFT_ONE)).astype(BF16)
    yield
    projected = dot(qkv_t[layer], normed)
    yield
    query = (projected[:WIDTH] + column(Q_BIAS)).astype(BF16)
    keys = projected[WIDTH : 2 * WIDTH].astype(BF16)
    values = (projected[2 * WIDTH :] + column(V_BIAS)).astype(BF16)
    yield from attention_forward(query, keys, values, segments, masks, power_ref, mixed_ref, scale_ref)
    mixed = mixed_ref[...]
    middle = hidden + (dot(out_t[layer], mixed.astype(BF16)) + column(OUT_BIAS))
    yield
    xhat_two, unused = norm_parts(middle)
    normed_two = (xhat_two * column(GAIN_TWO) + column(SHIFT_TWO)).astype(BF16)
    yield
    inner = dot(up_t[layer], normed_two)
    yield
    logit = inner[FF : FF + 1]
    inner = inner[:FF] + jnp.concatenate([column(UP_LOW), column(UP_HIGH)], axis=0)
    gate = jax.nn.sigmoid(logit)
    parts = []
    for start in range(0, FF, CHUNK):
        gated = inner[start : start + CHUNK] * gate
        power = jnp.tanh(gated * (GELU_A + (GELU_A * GELU_B) * (gated * gated)))
        parts.append((gated * (0.5 + 0.5 * power)).astype(BF16))
        yield
    active = jnp.concatenate(parts, axis=0)
    output = middle + (dot(down_t[layer], active) + column(DOWN_BIAS))
    return output, (normed, query, keys, values, mixed, middle, normed_two, inner, logit)


def norm_backward(gradient, xhat, scale, gain):
    inner = gradient * gain
    first = jnp.sum(inner, axis=0, keepdims=True) * (1.0 / WIDTH)
    second = jnp.sum(inner * xhat, axis=0, keepdims=True) * (1.0 / WIDTH)
    return scale * (inner - first - xhat * second)


def backward_unit(block, values_rows, query_variants, grad_variants, keys, deltas, power_ref, results, dq_ref):
    first, last = WINDOWS[block]
    query_blocks = [head_block(query_variants, block, group) for group in range(2)]
    grad_blocks = [head_block(grad_variants, block, group) for group in range(2)]
    products = [
        dot(values_rows[group][first:last], with_extra(grad_blocks[group], deltas[block][group]))
        for group in range(2)
    ]
    yield
    powers, grad_scores = [], []
    for group in range(2):
        start = PLACES[block][group]
        powers.append(power_ref[start : start + last - first])
        grad_scores.append((powers[group].astype(F32) * products[group]).astype(BF16))
        yield
    mixed = [
        dot(keys[QUARTER * group : QUARTER * group + QUARTER, first:last], grad_scores[group]) for group in range(2)
    ]

    def together_rows(blocks):
        gap = zeros(QUARTER)
        low = jnp.concatenate([blocks[0], gap], axis=0)
        high = jnp.concatenate([gap, blocks[1]], axis=0)
        return jnp.concatenate([low, high], axis=1)

    grad_keys = dot(jnp.concatenate(grad_scores, axis=1), together_rows(query_blocks).T)
    grad_values = dot(jnp.concatenate(powers, axis=1), together_rows(grad_blocks).T)
    results[block] = (grad_keys, grad_values, mixed)
    yield
    if block % 2 == 0:
        return
    lanes = slice((block // 2) * HALF, (block // 2 + 1) * HALF)
    for group in range(2):
        even, odd = results[block - 1][2][group], mixed[group]
        for head in range(4):
            tile = slice((head // 2) * HALF, (head // 2 + 1) * HALF)
            rows = slice(16 * head, 16 * head + 16)
            place = QUARTER * group + 16 * head
            dq_ref[place : place + 16, lanes] = join_blocks(even[rows, tile], odd[rows, tile], head)


def attention_backward(query, keys, values, mixed, scale, grad_mixed, masks, power_ref, dq_ref):
    factors = [scale[8 * head : 8 * head + 8] for head in range(HEADS)]
    grad = (grad_mixed * jnp.concatenate([row for factor in factors for row in (factor, factor)], axis=0)).astype(BF16)
    product = grad.astype(F32) * mixed
    delta = jnp.concatenate(
        [jnp.sum(product[16 * head : 16 * head + 16], axis=0, keepdims=True) for head in range(HEADS)], axis=0
    )
    yield
    parts = [part.astype(F32) for part in split_three(-delta)]
    gap = jnp.zeros((4, LEN), F32)
    extras = [
        jnp.concatenate([part[4 * group : 4 * group + 4] for part in parts] + [gap], axis=0).astype(BF16)
        for group in range(2)
    ]
    deltas = [[spread_rows(extras[group], masks, block) for group in range(2)] for block in range(4)]
    query_variants = halves_of(query, masks)
    grad_variants = halves_of(grad, masks)
    rows = token_rows(values, ones(16))
    yield
    results = {}
    yield from skewed(
        backward_unit(block, rows, query_variants, grad_variants, keys, deltas, power_ref, results, dq_ref)
        for block in range(4)
    )

    def collect(which):
        parts = [results[block][which] for block in range(4)]
        return jnp.concatenate(
            [
                parts[0][:64] + parts[1][:64],
                parts[0][64:] + parts[1][64:128] + parts[2][:64],
                parts[1][128:] + parts[2][64:128] + parts[3][:64],
                parts[2][128:] + parts[3][64:],
            ],
            axis=0,
        ).astype(BF16)

    return (dq_ref[...] * 0.25).astype(BF16), collect(0), collect(1)


def backward_layer(
    layer, gradient, hidden, masks, kept, power_ref, scale_ref, raw, columns, totals, dq_ref
):
    w_qkv, w_out, w_up, w_down = raw
    normed, query, keys, values, mixed, middle, normed_two, inner, logit = kept
    qkv_total, out_total, up_total, down_total, sums = totals
    column = lambda which: both(columns[layer, which])
    branch = gradient.astype(BF16)
    sums[S_DOWN] += fold(branch.astype(F32))
    grad_active = dot(w_down[layer], branch)
    yield
    gate = jax.nn.sigmoid(logit)
    actives, inners = [], []
    logit_sum = jnp.zeros((1, LEN), F32)
    for start in range(0, FF, CHUNK):
        rows = slice(start, start + CHUNK)
        gated = inner[rows] * gate
        square = gated * gated
        power = jnp.tanh(gated * (GELU_A + (GELU_A * GELU_B) * square))
        half_up = 0.5 + 0.5 * power
        active = gated * half_up
        slope = half_up + (active * (1.0 - power)) * (GELU_A + (3.0 * GELU_A * GELU_B) * square)
        grad_gated = grad_active[rows].astype(BF16).astype(F32) * slope
        logit_sum = logit_sum + jnp.sum(grad_gated * inner[rows], axis=0, keepdims=True)
        actives.append(active.astype(BF16))
        inners.append((grad_gated * gate).astype(BF16))
        yield
    grad_logit = logit_sum * (gate * (1.0 - gate))
    active = jnp.concatenate(actives, axis=0)
    grad_inner = jnp.concatenate(inners, axis=0)
    grad_two = dot(w_up[layer], grad_inner) + column(GATE) * grad_logit
    down_total[...] += dot(branch, active.T)
    up_total[...] += dot(jnp.concatenate([normed_two, ones(16)], axis=0), grad_inner.T)
    sums[S_GATE] += fold(normed_two.astype(F32) * grad_logit)
    yield
    xhat, scale = norm_parts(middle)
    sums[S_GAIN_TWO] += fold(grad_two * xhat)
    sums[S_SHIFT_TWO] += fold(grad_two)
    grad_middle = gradient + norm_backward(grad_two, xhat, scale, column(GAIN_TWO))
    attended = grad_middle.astype(BF16)
    yield
    grad_mixed = dot(w_out[layer], attended)
    out_total[...] += dot(jnp.concatenate([mixed.astype(BF16), ones(16)], axis=0), attended.T)
    yield
    grad_query, grad_keys, grad_values = yield from attention_backward(
        query, keys, values, mixed, scale_ref[...], grad_mixed, masks, power_ref, dq_ref
    )
    yield
    grad_rows = jnp.concatenate([grad_query.T, grad_keys, grad_values], axis=1)
    qkv_total[...] += dot(jnp.concatenate([normed, ones(16)], axis=0), grad_rows)
    grad_one = dot(w_qkv[layer], jnp.concatenate([grad_query, grad_keys.T, grad_values.T], axis=0))
    yield
    xhat, scale = norm_parts(hidden)
    sums[S_GAIN_ONE] += fold(grad_one * xhat)
    sums[S_SHIFT_ONE] += fold(grad_one)
    return grad_middle + norm_backward(grad_one, xhat, scale, column(GAIN_ONE))


def spread(row):
    return jnp.broadcast_to(row, (WIDTH, WIDTH)).T


def fill_columns(layer, columns, gains, shifts, qv_bias, out_bias, w_gate, up_bias, down_bias):
    columns[layer, GAIN_ONE] = spread(gains[layer, 0:1])
    columns[layer, GAIN_TWO] = spread(gains[layer, 1:2])
    columns[layer, SHIFT_ONE] = spread(shifts[layer, 0:1])
    columns[layer, SHIFT_TWO] = spread(shifts[layer, 1:2])
    columns[layer, OUT_BIAS] = spread(out_bias[layer : layer + 1])
    columns[layer, DOWN_BIAS] = spread(down_bias[layer : layer + 1])
    columns[layer, Q_BIAS] = spread(qv_bias[layer : layer + 1, :WIDTH]) * 0.25
    columns[layer, V_BIAS] = spread(qv_bias[layer : layer + 1, WIDTH:])
    columns[layer, GATE] = spread(w_gate[layer : layer + 1].astype(F32))
    columns[layer, UP_LOW] = spread(up_bias[layer : layer + 1, :WIDTH])
    columns[layer, UP_HIGH] = spread(up_bias[layer : layer + 1, WIDTH:])


def clear_totals(totals):
    for ref in totals:
        ref[...] = jnp.zeros_like(ref)


def write_totals(totals, grads_ref):
    qkv_total, out_total, up_total, down_total, sums = totals
    for part in range(3):
        rows = slice(R_QKV + part * WIDTH, R_QKV + (part + 1) * WIDTH)
        grads_ref[rows] = qkv_total[:WIDTH, part * WIDTH : (part + 1) * WIDTH]
    grads_ref[R_OUT : R_OUT + WIDTH] = out_total[:WIDTH]
    for part in range(2):
        lanes = slice(part * WIDTH, (part + 1) * WIDTH)
        grads_ref[R_UP + part * WIDTH : R_UP + (part + 1) * WIDTH] = up_total[:WIDTH, lanes]
        grads_ref[R_DOWN + part * WIDTH : R_DOWN + (part + 1) * WIDTH] = down_total[:, lanes].T
    rows = [jnp.sum(sums[which].T, axis=0, keepdims=True) for which in range(SUMS)]
    rows.append(out_total[WIDTH : WIDTH + 1])
    rows.extend(qkv_total[WIDTH : WIDTH + 1, part * WIDTH : (part + 1) * WIDTH] for part in range(3))
    rows.extend(up_total[WIDTH : WIDTH + 1, part * WIDTH : (part + 1) * WIDTH] for part in range(2))
    rows.append(jnp.zeros((ROWS - R_SMALL - len(rows), WIDTH), F32))
    grads_ref[R_SMALL:ROWS] = jnp.concatenate(rows, axis=0)


def kernel(
    per_step, steps,
    x_ref, seg_ref, cot_ref, gains, shifts, w_qkv, qv_bias, w_out, out_bias, w_gate, w_up, up_bias, w_down, down_bias,
    result_ref, grad_inputs_ref, grads_ref,
    columns, qkv_t, out_t, up_t, down_t, mixed_scratch, dq_ref, power_last, scale_last,
    grad_kept, normed_kept, qkv_kept, mixed_kept, scale_kept, middle_kept, normed_two_kept, inner_kept, logit_kept,
    power_kept, *totals,
):
    step = pl.program_id(0)
    totals_zero, totals_one = totals[: len(totals) // 2], totals[len(totals) // 2 :]

    @pl.when(step == 0)
    def start():
        clear_totals(totals)
        for layer in range(LAYERS):
            fill_columns(layer, columns, gains, shifts, qv_bias, out_bias, w_gate, up_bias, down_bias)
            qkv_t[layer, :WIDTH] = (w_qkv[layer][:, :WIDTH] * jnp.asarray(0.25, BF16)).T
            qkv_t[layer, WIDTH:] = w_qkv[layer][:, WIDTH:].T
            out_t[layer] = w_out[layer].T
            up_t[layer, :FF] = w_up[layer].T
            up_t[layer, FF:] = jnp.concatenate(
                [w_gate[layer : layer + 1].astype(F32), jnp.zeros((15, WIDTH), F32)], axis=0
            ).astype(BF16)
            down_t[layer] = w_down[layer].T

    masks = make_masks()
    weights = (qkv_t, out_t, up_t, down_t)
    raw = (w_qkv, w_out, w_up, w_down)

    def upward(item):
        tokens = slice(item * LEN, (item + 1) * LEN)
        place = step * per_step + item
        segments = segment_masks(seg_ref[pl.ds(place, 1)])
        hidden = x_ref[tokens].astype(F32).T
        middle_hidden, kept = yield from forward_layer(
            0, hidden, segments, masks, weights, columns, power_kept.at[place], mixed_scratch.at[item],
            scale_kept.at[place],
        )
        normed, query, keys, values, mixed, middle, normed_two, inner, logit = kept
        normed_kept[place] = normed
        qkv_kept[place, :WIDTH] = query
        qkv_kept[place, WIDTH : 2 * WIDTH] = keys
        qkv_kept[place, 2 * WIDTH :] = values
        mixed_kept[place] = mixed
        middle_kept[place] = middle
        normed_two_kept[place] = normed_two
        inner_kept[place] = inner
        logit_kept[place] = jnp.broadcast_to(logit, (8, LEN))
        output, kept = yield from forward_layer(
            1, middle_hidden, segments, masks, weights, columns, power_last.at[item], mixed_scratch.at[item],
            scale_last.at[item],
        )
        result_ref[tokens] = output.T.astype(BF16)
        gradient = cot_ref[tokens].astype(F32).T
        grad_kept[place] = yield from backward_layer(
            1, gradient, middle_hidden, masks, kept, power_last.at[item], scale_last.at[item], raw, columns,
            totals_one, dq_ref.at[item],
        )

    def downward(item):
        tokens = slice(item * LEN, (item + 1) * LEN)
        place = (step - steps) * per_step + item
        hidden = x_ref[tokens].astype(F32).T
        kept = (
            normed_kept[place], qkv_kept[place, :WIDTH], qkv_kept[place, WIDTH : 2 * WIDTH],
            qkv_kept[place, 2 * WIDTH :], mixed_kept[place], middle_kept[place], normed_two_kept[place],
            inner_kept[place], logit_kept[place, 0:1],
        )
        gradient = yield from backward_layer(
            0, grad_kept[place], hidden, masks, kept, power_kept.at[place], scale_kept.at[place], raw, columns,
            totals_zero, dq_ref.at[item],
        )
        grad_inputs_ref[tokens] = gradient.T

    @pl.when(step < steps)
    def first_half():
        together([upward(item) for item in range(per_step)])

    @pl.when(step >= steps)
    def second_half():
        together([downward(item) for item in range(per_step)])

    @pl.when(step == 2 * steps - 1)
    def finish():
        write_totals(totals_zero, grads_ref.at[0])
        write_totals(totals_one, grads_ref.at[1])


def totals_scratch():
    return [
        pltpu.VMEM((WIDTH + 16, 3 * WIDTH), F32),
        pltpu.VMEM((WIDTH + 16, WIDTH), F32),
        pltpu.VMEM((WIDTH + 16, FF), F32),
        pltpu.VMEM((WIDTH, FF), F32),
        pltpu.VMEM((SUMS, WIDTH, WIDTH), F32),
    ]


def local_part(inputs, segment_ids, cotangent, *parameters, per_step=4):
    seqs = segment_ids.shape[0]
    per_step = min(per_step, seqs)
    steps = seqs // per_step
    rows = (per_step * LEN, WIDTH)

    def whole(array):
        zero = (0,) * array.ndim
        return pl.BlockSpec(array.shape, lambda i: zero)

    def kept(rows, dtype, count=seqs):
        return pltpu.VMEM((count, rows, LEN), dtype)

    return pl.pallas_call(
        lambda *refs: kernel(per_step, steps, *refs),
        grid=(2 * steps,),
        in_specs=[
            pl.BlockSpec(rows, lambda i: (i % steps, 0)),
            whole(segment_ids),
            pl.BlockSpec(rows, lambda i: (jnp.minimum(i, steps - 1), 0)),
        ]
        + [whole(entry) for entry in parameters],
        out_specs=[
            pl.BlockSpec(rows, lambda i: (jnp.minimum(i, steps - 1), 0)),
            pl.BlockSpec(rows, lambda i: (jnp.maximum(i - steps, 0), 0)),
            pl.BlockSpec((LAYERS, ROWS, WIDTH), lambda i: (0, 0, 0)),
        ],
        out_shape=[
            jax.ShapeDtypeStruct(inputs.shape, BF16),
            jax.ShapeDtypeStruct(inputs.shape, F32),
            jax.ShapeDtypeStruct((LAYERS, ROWS, WIDTH), F32),
        ],
        scratch_shapes=[
            pltpu.VMEM((LAYERS, COLUMNS, WIDTH, WIDTH), F32),
            pltpu.VMEM((LAYERS, 3 * WIDTH, WIDTH), BF16),
            pltpu.VMEM((LAYERS, WIDTH, WIDTH), BF16),
            pltpu.VMEM((LAYERS, FF + 16, WIDTH), BF16),
            pltpu.VMEM((LAYERS, WIDTH, FF), BF16),
            kept(WIDTH, F32, per_step),
            kept(WIDTH, F32, per_step),
            kept(POWER_ROWS, BF16, per_step),
            kept(8 * HEADS, F32, per_step),
            kept(WIDTH, F32),
            kept(WIDTH, BF16),
            kept(3 * WIDTH, BF16),
            kept(WIDTH, F32),
            kept(8 * HEADS, F32),
            kept(WIDTH, F32),
            kept(WIDTH, BF16),
            kept(FF, F32),
            kept(8, F32),
            kept(POWER_ROWS, BF16),
        ]
        + totals_scratch()
        + totals_scratch(),
        compiler_params=pltpu.CompilerParams(vmem_limit_bytes=60 * 1024 * 1024),
        name="layers",
    )(inputs, segment_ids, cotangent, *parameters)


def unpack_kernel(
    where_ref, near_ref, far_ref,
    gains_ref, shifts_ref, qkv_ref, qv_bias_ref, out_ref, out_bias_ref, gate_ref, up_ref, up_bias_ref, down_ref,
    down_bias_ref,
    grads,
):
    core, part = where_ref[0], where_ref[1]
    quarter = ROWS // 4
    for mask in range(4):
        place = pl.ds(pl.multiple_of((part ^ mask) * quarter, 8), quarter)
        rows = slice(mask * quarter, (mask + 1) * quarter)
        grads[core, place] = near_ref[rows]
        grads[1 - core, place] = far_ref[rows]
    for layer in range(LAYERS):
        for part in range(3):
            lanes = slice(part * WIDTH, (part + 1) * WIDTH)
            qkv_ref[layer, :, lanes] = grads[layer, R_QKV + part * WIDTH : R_QKV + (part + 1) * WIDTH]
        out_ref[layer] = grads[layer, R_OUT : R_OUT + WIDTH]
        for part in range(2):
            lanes = slice(part * WIDTH, (part + 1) * WIDTH)
            up_ref[layer, :, lanes] = grads[layer, R_UP + part * WIDTH : R_UP + (part + 1) * WIDTH]
        down_ref[layer] = grads[layer, R_DOWN : R_DOWN + FF]
        one = slice(layer, layer + 1)

        def row(which):
            return grads[layer, R_SMALL + which : R_SMALL + which + 1]

        gains_ref[layer, 0:1], gains_ref[layer, 1:2] = row(S_GAIN_ONE), row(S_GAIN_TWO)
        shifts_ref[layer, 0:1], shifts_ref[layer, 1:2] = row(S_SHIFT_ONE), row(S_SHIFT_TWO)
        qv_bias_ref[one, :WIDTH], qv_bias_ref[one, WIDTH:] = row(S_Q), row(S_V)
        out_bias_ref[one], gate_ref[one], down_bias_ref[one] = row(S_OUT), row(S_GATE), row(S_DOWN)
        up_bias_ref[one, :WIDTH], up_bias_ref[one, WIDTH:] = row(S_UP_LOW), row(S_UP_HIGH)


def unpack(where, near, far):
    shapes = [
        (LAYERS, 2, WIDTH), (LAYERS, 2, WIDTH), (LAYERS, WIDTH, 3 * WIDTH), (LAYERS, 2 * WIDTH), (LAYERS, WIDTH, WIDTH),
        (LAYERS, WIDTH), (LAYERS, WIDTH), (LAYERS, WIDTH, FF), (LAYERS, FF), (LAYERS, FF, WIDTH), (LAYERS, WIDTH),
    ]
    return pl.pallas_call(
        unpack_kernel,
        in_specs=[pl.BlockSpec(memory_space=pltpu.SMEM), pl.BlockSpec(), pl.BlockSpec()],
        out_shape=[jax.ShapeDtypeStruct(shape, F32) for shape in shapes],
        scratch_shapes=[pltpu.VMEM((LAYERS, ROWS, WIDTH), F32)],
        compiler_params=pltpu.CompilerParams(vmem_limit_bytes=16 * 1024 * 1024),
        name="unpack",
    )(where, near, far)


def all_sum(grads, size):
    me = lax.axis_index("seq")
    bits = size.bit_length() - 1
    core, part = me & 1, (me >> 1) & 3

    def swap(value, mask):
        return lax.ppermute(value, "seq", [(i, i ^ mask) for i in range(size)])

    def pick(value, index):
        return lax.dynamic_index_in_dim(value, index, 0, keepdims=False)

    layer = pick(grads, core) + swap(pick(grads, 1 - core), 1)
    quarters = layer.reshape(4, ROWS // 4, WIDTH)
    others = [swap(pick(quarters, part ^ mask), 2 * mask) for mask in (1, 2, 3)]
    mine = pick(quarters, part) + others[0] + others[1] + others[2]
    for bit in range(3, bits):
        mine = mine + swap(mine, 1 << bit)
    near = jnp.concatenate([mine] + [swap(mine, 2 * mask) for mask in (1, 2, 3)], axis=0)
    return jnp.stack([core, part]).astype(jnp.int32), near, swap(near, 1)


def body(size, *arguments):
    result, grad_inputs, grads = local_part(*arguments)
    if size & (size - 1) or size < 8:
        grads = lax.psum(grads, "seq")
        summed = (jnp.zeros((2,), jnp.int32), grads[0], grads[1])
    else:
        summed = all_sum(grads, size)
    return (result, grad_inputs) + tuple(unpack(*summed))


def solution(mesh):
    rows = P("seq", None)
    return jax.shard_map(
        lambda *arguments: body(mesh.shape["seq"], *arguments),
        mesh=mesh,
        in_specs=(rows, rows, rows) + (P(),) * 11,
        out_specs=(rows, rows) + (P(),) * 11,
        check_vma=False,
    )
```

```python
import jax
import jax.numpy as jnp
from jax import lax
from jax.experimental import pallas as pl
from jax.experimental.pallas import tpu as pltpu
from jax.sharding import PartitionSpec as P

HEADS = 8
LAYERS = 2
WIDTH = 128
FF = 256
LEN = 256
HALF = 128
CHUNK = 128
QUARTER = 64
WINDOWS = ((0, 128), (0, 192), (64, 256), (128, 256))
PLACES = ((0, 128), (256, 448), (640, 832), (1024, 1152))
POWER_ROWS = 1280
FAR = -1.0e9
GELU_A = 0.7978845608028654
GELU_B = 0.044715
F32 = jnp.float32
BF16 = jnp.bfloat16

GAIN_ONE, SHIFT_ONE, GAIN_TWO, SHIFT_TWO, DOWN_BIAS, GATE = range(6)
COLUMNS = 6
EXTENDED = WIDTH + 16
S_DOWN, S_GATE = range(2)
SUMS = 2
S_LOGIT = 2
S_OUT, S_Q, S_K, S_V, S_UP_LOW, S_UP_HIGH, S_SHIFT_ONE, S_SHIFT_TWO, S_GAIN_ONE, S_GAIN_TWO = range(2, 12)
R_QKV, R_OUT, R_UP, R_DOWN, R_SMALL, ROWS = 0, 384, 512, 768, 1024, 1056


def dot(left, right):
    return lax.dot_general(left, right, (((1,), (0,)), ((), ())), preferred_element_type=F32)


def both(column):
    return jnp.concatenate([column, column], axis=1)


def fold(value):
    return value[:, :HALF] + value[:, HALF:]


def zeros(rows, lanes=LEN):
    return jnp.zeros((rows, lanes), BF16)


def ones(rows, lanes=LEN):
    return jnp.ones((rows, lanes), BF16)


def split_three(value):
    high = value.astype(BF16)
    rest = value - high.astype(F32)
    middle = rest.astype(BF16)
    low = (rest - middle.astype(F32)).astype(BF16)
    return high, middle, low


def norm_parts(value):
    average = jnp.sum(value, axis=0, keepdims=True) * (1.0 / WIDTH)
    centered = value - average
    variance = jnp.sum(centered * centered, axis=0, keepdims=True) * (1.0 / WIDTH)
    scale = lax.rsqrt(variance + 1e-05)
    return centered * scale, scale


def lane_mask(rows, which):
    row = lax.broadcasted_iota(jnp.int32, (rows, HALF), 0)
    lane = lax.broadcasted_iota(jnp.int32, (rows, HALF), 1)
    return jnp.where(which(row, lane < QUARTER), 1.0, 0.0).astype(BF16)


def turned(rows):
    return jnp.concatenate(
        [rows[:, 64:128], rows[:, :64], rows[:, 192:256], rows[:, 128:192]], axis=1
    )


def make_masks():
    low = lane_mask(16, lambda row, left: left)
    high = lane_mask(16, lambda row, left: ~left)
    heads = [
        lane_mask(16, lambda row, left, head=head: (row % 4 == head) & (left if head % 2 == 0 else ~left))
        for head in range(4)
    ]
    return low, high, heads


def halves_of(rows, masks):
    low, high, unused = masks
    count = rows.shape[0] // 16
    low_all = jnp.concatenate([both(low)] * count, axis=0)
    high_all = jnp.concatenate([both(high)] * count, axis=0)
    other = turned(rows)
    return ((rows * low_all, other * high_all), (other * low_all, rows * high_all))


def head_block(variants, block, group):
    lanes = slice((block // 2) * HALF, (block // 2 + 1) * HALF)
    gap = zeros(16, HALF)
    pieces = []
    for head in range(4):
        first = QUARTER * group + 16 * head
        piece = variants[block % 2][head % 2][first : first + 16, lanes]
        pieces.append(jnp.concatenate([piece, gap] if head < 2 else [gap, piece], axis=1))
    return jnp.concatenate(pieces, axis=0)


def with_extra(features, extra):
    return jnp.concatenate([features, extra], axis=0)


def spread_marks(rows, masks, block):
    low, high, unused = masks
    lanes = slice((block // 2) * HALF, (block // 2 + 1) * HALF)
    here, there = rows[:, lanes], turned(rows)[:, lanes]
    once = here * low + there * high if block % 2 == 0 else there * low + here * high
    return both(once)


def spread_rows(rows, masks, block):
    unused, unused, heads = masks
    lanes = slice((block // 2) * HALF, (block // 2 + 1) * HALF)
    here, there = rows[:, lanes], turned(rows)[:, lanes]
    if block % 2 == 1:
        here, there = there, here
    return jnp.concatenate([here * heads[0] + there * heads[1], here * heads[2] + there * heads[3]], axis=1)


def join_blocks(even, odd, head):
    left = lax.broadcasted_iota(jnp.int32, even.shape, 1) < QUARTER
    if head % 2 == 0:
        return jnp.where(left, even, pltpu.roll(odd, QUARTER, 1))
    return jnp.where(left, pltpu.roll(even, QUARTER, 1), odd)


def token_rows(rows, extra):
    return [
        jnp.concatenate([rows[QUARTER * group : QUARTER * group + QUARTER], extra], axis=0).T for group in range(2)
    ]


def skewed(units):
    running, waiting = [], list(units)
    while running or waiting:
        if waiting:
            running.append(waiting.pop(0))
        running = [unit for unit in running if next(unit, "end") != "end"]
        yield


def together(parts):
    running, waiting = [], list(parts)
    while running or waiting:
        if waiting:
            running.append(waiting.pop(0))
        running = [part for part in running if next(part, "end") != "end"]


def segment_masks(segments):
    ids = lax.broadcasted_iota(jnp.int32, (16, LEN), 0)
    same = ids == segments
    one_hot = jnp.where(same, 1.0, 0.0).astype(BF16)
    other = jnp.where(same | (ids >= 8), 0.0, FAR).astype(BF16)
    return one_hot, other


def forward_unit(block, group, keys_rows, variants, values, marks, power_ref, mixed_ref, scale_ref, results):
    first, last = WINDOWS[block]
    weights = with_extra(head_block(variants, block, group), marks[block])
    scores = dot(keys_rows[first:last], weights)
    yield
    peak = jnp.max(scores, axis=0, keepdims=True)
    powers = jnp.exp(scores - peak).astype(BF16)
    start = PLACES[block][group]
    power_ref[start : start + last - first] = powers
    yield
    rows = values[QUARTER * group : QUARTER * group + QUARTER, first:last]
    mixed = dot(jnp.concatenate([rows, ones(16, last - first)], axis=0), powers)
    yield
    scale = 1.0 / mixed[QUARTER : QUARTER + 8]
    results[block, group] = (mixed, scale)
    if block % 2 == 0:
        return
    even, even_scale = results[block - 1, group]
    lanes = slice((block // 2) * HALF, (block // 2 + 1) * HALF)
    for head in range(4):
        tile = slice((head // 2) * HALF, (head // 2 + 1) * HALF)
        rows = slice(16 * head, 16 * head + 16)
        factor = join_blocks(even_scale[:, tile], scale[:, tile], head)
        joined = join_blocks(even[rows, tile], mixed[rows, tile], head)
        place = QUARTER * group + 16 * head
        mixed_ref[place : place + 16, lanes] = joined * jnp.concatenate([factor, factor], axis=0)
        place = 8 * (4 * group + head)
        scale_ref[place : place + 8, lanes] = factor


def attention_forward(query, keys, values, segments, masks, power_ref, mixed_ref, scale_ref):
    one_hot, other = segments
    rows = token_rows(keys, other)
    variants = halves_of(query, masks)
    marks = [spread_marks(one_hot, masks, block) for block in range(4)]
    yield
    results = {}
    yield from skewed(
        forward_unit(block, group, rows[group], variants, values, marks, power_ref, mixed_ref, scale_ref, results)
        for block in (0, 1, 2, 3)
        for group in range(2)
    )


def forward_layer(
    layer, hidden, segments, masks, weights, columns, power_ref, mixed_ref, scale_ref, gated_ref, twice_ref
):
    qkv_t, out_t, up_t, down_t = weights
    column = lambda which: both(columns[layer, which])
    xhat, spread_one = norm_parts(hidden)
    normed = (xhat * column(GAIN_ONE) + column(SHIFT_ONE)).astype(BF16)
    yield
    projected = dot(qkv_t[layer][:, :EXTENDED], jnp.concatenate([normed, ones(16)], axis=0))
    yield
    query = projected[:WIDTH].astype(BF16)
    keys = projected[WIDTH : 2 * WIDTH].astype(BF16)
    values = projected[2 * WIDTH :].astype(BF16)
    yield from attention_forward(query, keys, values, segments, masks, power_ref, mixed_ref, scale_ref)
    mixed = mixed_ref[...]
    middle = hidden + dot(out_t[layer][:, :EXTENDED], jnp.concatenate([mixed.astype(BF16), ones(16)], axis=0))
    yield
    xhat_two, spread_two = norm_parts(middle)
    normed_two = (xhat_two * column(GAIN_TWO) + column(SHIFT_TWO)).astype(BF16)
    yield
    inner = dot(up_t[layer][:, :EXTENDED], jnp.concatenate([normed_two, ones(16)], axis=0))
    yield
    logit = inner[FF : FF + 1]
    gate = jax.nn.sigmoid(logit)
    parts = []
    for start in range(0, FF, CHUNK):
        gated = inner[start : start + CHUNK] * gate
        twice_up = 1.0 + jnp.tanh(gated * (GELU_A + (GELU_A * GELU_B) * (gated * gated)))
        gated_ref[start : start + CHUNK] = gated
        twice_ref[start : start + CHUNK] = twice_up
        parts.append((gated * twice_up).astype(BF16))
        yield
    active = jnp.concatenate(parts, axis=0)
    output = middle + (dot(down_t[layer], active) + column(DOWN_BIAS))
    rows = jnp.concatenate([spread_one, spread_two, gate, jnp.zeros((5, LEN), F32)], axis=0)
    return output, (normed, query, keys, values, mixed, xhat, xhat_two, normed_two, rows)


def norm_backward(gradient, xhat, scale, gain):
    inner = gradient * gain
    first = jnp.sum(inner, axis=0, keepdims=True) * (1.0 / WIDTH)
    second = jnp.sum(inner * xhat, axis=0, keepdims=True) * (1.0 / WIDTH)
    return scale * (inner - first - xhat * second)


def backward_unit(block, values_rows, query_variants, grad_variants, keys, deltas, power_ref, results, dq_ref):
    first, last = WINDOWS[block]
    query_blocks = [head_block(query_variants, block, group) for group in range(2)]
    grad_blocks = [head_block(grad_variants, block, group) for group in range(2)]
    products = [
        dot(values_rows[group][first:last], with_extra(grad_blocks[group], deltas[block][group]))
        for group in range(2)
    ]
    yield
    powers, grad_scores = [], []
    for group in range(2):
        start = PLACES[block][group]
        powers.append(power_ref[start : start + last - first])
        grad_scores.append((powers[group].astype(F32) * products[group]).astype(BF16))
        yield
    mixed = [
        dot(keys[QUARTER * group : QUARTER * group + QUARTER, first:last], grad_scores[group]) for group in range(2)
    ]

    def together_rows(blocks):
        gap = zeros(QUARTER)
        low = jnp.concatenate([blocks[0], gap], axis=0)
        high = jnp.concatenate([gap, blocks[1]], axis=0)
        return jnp.concatenate([low, high], axis=1)

    grad_keys = dot(jnp.concatenate(grad_scores, axis=1), together_rows(query_blocks).T)
    grad_values = dot(jnp.concatenate(powers, axis=1), together_rows(grad_blocks).T)
    results[block] = (grad_keys, grad_values, mixed)
    yield
    if block % 2 == 0:
        return
    lanes = slice((block // 2) * HALF, (block // 2 + 1) * HALF)
    for group in range(2):
        even, odd = results[block - 1][2][group], mixed[group]
        for head in range(4):
            tile = slice((head // 2) * HALF, (head // 2 + 1) * HALF)
            rows = slice(16 * head, 16 * head + 16)
            place = QUARTER * group + 16 * head
            dq_ref[place : place + 16, lanes] = join_blocks(even[rows, tile], odd[rows, tile], head)


def attention_backward(query, keys, values, mixed, scale, grad_mixed, masks, power_ref, dq_ref):
    factors = [scale[8 * head : 8 * head + 8] for head in range(HEADS)]
    grad = (grad_mixed * jnp.concatenate([row for factor in factors for row in (factor, factor)], axis=0)).astype(BF16)
    product = grad.astype(F32) * mixed
    delta = jnp.concatenate(
        [jnp.sum(product[16 * head : 16 * head + 16], axis=0, keepdims=True) for head in range(HEADS)], axis=0
    )
    yield
    parts = [part.astype(F32) for part in split_three(-delta)]
    gap = jnp.zeros((4, LEN), F32)
    extras = [
        jnp.concatenate([part[4 * group : 4 * group + 4] for part in parts] + [gap], axis=0).astype(BF16)
        for group in range(2)
    ]
    deltas = [[spread_rows(extras[group], masks, block) for group in range(2)] for block in range(4)]
    query_variants = halves_of(query, masks)
    grad_variants = halves_of(grad, masks)
    rows = token_rows(values, ones(16))
    yield
    results = {}
    yield from skewed(
        backward_unit(block, rows, query_variants, grad_variants, keys, deltas, power_ref, results, dq_ref)
        for block in range(4)
    )

    def collect(which):
        parts = [results[block][which] for block in range(4)]
        return jnp.concatenate(
            [
                parts[0][:64] + parts[1][:64],
                parts[0][64:] + parts[1][64:128] + parts[2][:64],
                parts[1][128:] + parts[2][64:128] + parts[3][:64],
                parts[2][128:] + parts[3][64:],
            ],
            axis=0,
        ).astype(BF16)

    return (dq_ref[...] * 0.25).astype(BF16), collect(0), collect(1)


def backward_layer(
    layer, gradient, masks, kept, power_ref, scale_ref, gated_ref, twice_ref, raw, columns, totals, dq_ref
):
    w_qkv, w_out, w_up, w_down = raw
    normed, query, keys, values, mixed, xhat, xhat_two, normed_two, rows = kept
    spread_one, spread_two, gate = rows[0:1], rows[1:2], rows[2:3]
    qkv_total, out_total, up_total, down_total, sums = totals
    column = lambda which: both(columns[layer, which])
    branch = gradient.astype(BF16)
    sums[S_DOWN] += fold(gradient)
    grad_active = dot(w_down[layer], branch)
    yield
    actives, inners = [], []
    logit_sum = jnp.zeros((1, LEN), F32)
    for start in range(0, FF, CHUNK):
        rows = slice(start, start + CHUNK)
        gated = gated_ref[rows]
        twice_up = twice_ref[rows]
        active = gated * twice_up
        curve = GELU_A + (3.0 * GELU_A * GELU_B) * (gated * gated)
        slope = twice_up + (active * (2.0 - twice_up)) * curve
        grad_gated = grad_active[rows] * slope
        logit_sum = logit_sum + jnp.sum(grad_gated * gated, axis=0, keepdims=True)
        actives.append(active.astype(BF16))
        inners.append((grad_gated * gate).astype(BF16))
        yield
    grad_logit = logit_sum * (1.0 - gate)
    active = jnp.concatenate(actives, axis=0)
    grad_inner = jnp.concatenate(inners, axis=0)
    grad_two = dot(w_up[layer], grad_inner) + column(GATE) * grad_logit
    down_total[...] += dot(branch, active.T)
    up_total[...] += dot(jnp.concatenate([normed_two, ones(16)], axis=0), grad_inner.T)
    sums[S_GATE] += fold(normed_two.astype(F32) * grad_logit)
    sums[S_LOGIT, 0:1] += fold(grad_logit)
    yield
    grad_middle = gradient + norm_backward(grad_two, xhat_two, spread_two, column(GAIN_TWO))
    attended = grad_middle.astype(BF16)
    yield
    grad_mixed = dot(w_out[layer], attended)
    out_total[...] += dot(jnp.concatenate([mixed.astype(BF16), ones(16)], axis=0), attended.T)
    yield
    grad_query, grad_keys, grad_values = yield from attention_backward(
        query, keys, values, mixed, scale_ref[...], grad_mixed, masks, power_ref, dq_ref
    )
    yield
    grad_rows = jnp.concatenate([grad_query.T, grad_keys, grad_values], axis=1)
    qkv_total[...] += dot(jnp.concatenate([normed, ones(16)], axis=0), grad_rows)
    grad_one = dot(w_qkv[layer], jnp.concatenate([grad_query, grad_keys.T, grad_values.T], axis=0))
    yield
    return grad_middle + norm_backward(grad_one, xhat, spread_one, column(GAIN_ONE))


def spread(row):
    return jnp.broadcast_to(row, (WIDTH, WIDTH)).T


def bias_lanes(row):
    parts = [part.astype(F32) for part in split_three(row)]
    return jnp.concatenate(parts + [jnp.zeros((13, WIDTH), F32)], axis=0).T.astype(BF16)


def fill_columns(layer, columns, gains, shifts, w_gate, down_bias):
    columns[layer, GAIN_ONE] = spread(gains[layer, 0:1])
    columns[layer, GAIN_TWO] = spread(gains[layer, 1:2])
    columns[layer, SHIFT_ONE] = spread(shifts[layer, 0:1])
    columns[layer, SHIFT_TWO] = spread(shifts[layer, 1:2])
    columns[layer, DOWN_BIAS] = spread(down_bias[layer : layer + 1])
    columns[layer, GATE] = spread(w_gate[layer : layer + 1].astype(F32))


def clear_totals(totals):
    for ref in totals:
        ref[...] = jnp.zeros_like(ref)


def through(weights, row):
    parts = jnp.concatenate(split_three(row), axis=0)
    return jnp.sum(lax.dot_general(parts, weights, (((1,), (1,)), ((), ())), preferred_element_type=F32), axis=0, keepdims=True)


def across(value):
    parts = [value[:, start : start + WIDTH] for start in range(0, value.shape[1], WIDTH)]
    total = parts[0]
    for part in parts[1:]:
        total = total + part
    return jnp.sum(total.T, axis=0, keepdims=True)


def write_totals(totals, grads_ref, w_qkv, w_gate, w_up, gains, shifts):
    qkv_total, out_total, up_total, down_total, sums = totals
    for part in range(3):
        rows = slice(R_QKV + part * WIDTH, R_QKV + (part + 1) * WIDTH)
        grads_ref[rows] = qkv_total[:WIDTH, part * WIDTH : (part + 1) * WIDTH]
    grads_ref[R_OUT : R_OUT + WIDTH] = out_total[:WIDTH]
    for part in range(2):
        lanes = slice(part * WIDTH, (part + 1) * WIDTH)
        grads_ref[R_UP + part * WIDTH : R_UP + (part + 1) * WIDTH] = up_total[:WIDTH, lanes]
        grads_ref[R_DOWN + part * WIDTH : R_DOWN + (part + 1) * WIDTH] = down_total[:, lanes].T * 0.5
    rows = [jnp.sum(sums[which].T, axis=0, keepdims=True) for which in range(SUMS)]
    rows.append(out_total[WIDTH : WIDTH + 1])
    rows.extend(qkv_total[WIDTH : WIDTH + 1, part * WIDTH : (part + 1) * WIDTH] for part in range(3))
    rows.extend(up_total[WIDTH : WIDTH + 1, part * WIDTH : (part + 1) * WIDTH] for part in range(2))
    rows.append(through(w_qkv, qkv_total[WIDTH : WIDTH + 1]))
    logit = jnp.sum(sums[S_LOGIT, 0:1], axis=1, keepdims=True)
    rows.append(through(w_up, up_total[WIDTH : WIDTH + 1]) + logit * w_gate.astype(F32))
    moments = (
        across(qkv_total[:WIDTH] * w_qkv.astype(F32)),
        across(up_total[:WIDTH] * w_up.astype(F32)) + rows[S_GATE] * w_gate.astype(F32),
    )
    for which, moment in enumerate(moments):
        norm = slice(which, which + 1)
        rows.append((moment - shifts[norm] * rows[S_SHIFT_ONE + which]) / gains[norm])
    rows.append(jnp.zeros((ROWS - R_SMALL - len(rows), WIDTH), F32))
    grads_ref[R_SMALL:ROWS] = jnp.concatenate(rows, axis=0)


def kernel(
    per_step, steps,
    x_ref, seg_ref, cot_ref, gains, shifts, w_qkv, qv_bias, w_out, out_bias, w_gate, w_up, up_bias, w_down, down_bias,
    result_ref, grad_inputs_ref, grads_ref,
    columns, qkv_t, out_t, up_t, down_t, half_down, mixed_scratch, dq_ref, power_last, scale_last, gated_last, twice_last,
    grad_kept, normed_kept, qkv_kept, mixed_kept, scale_kept, xhat_kept, xhat_two_kept, normed_two_kept, rows_kept,
    power_kept, gated_kept, twice_kept, *totals,
):
    step = pl.program_id(0)
    totals_zero, totals_one = totals[: len(totals) // 2], totals[len(totals) // 2 :]

    @pl.when(step == 0)
    def start():
        clear_totals(totals)
        for layer in range(LAYERS):
            fill_columns(layer, columns, gains, shifts, w_gate, down_bias)
            for ref in (qkv_t, out_t, up_t):
                ref[layer, :, WIDTH:] = zeros(ref.shape[1], WIDTH)
            qkv_t[layer, :WIDTH, :WIDTH] = (w_qkv[layer][:, :WIDTH] * jnp.asarray(0.25, BF16)).T
            qkv_t[layer, WIDTH:, :WIDTH] = w_qkv[layer][:, WIDTH:].T
            biases = qv_bias[layer : layer + 1]
            qkv_t[layer, :WIDTH, WIDTH:EXTENDED] = bias_lanes(biases[:, :WIDTH] * 0.25)
            qkv_t[layer, 2 * WIDTH :, WIDTH:EXTENDED] = bias_lanes(biases[:, WIDTH:])
            out_t[layer, :, :WIDTH] = w_out[layer].T
            out_t[layer, :, WIDTH:EXTENDED] = bias_lanes(out_bias[layer : layer + 1])
            up_t[layer, :FF, :WIDTH] = w_up[layer].T
            up_t[layer, FF:, :WIDTH] = jnp.concatenate(
                [w_gate[layer : layer + 1].astype(F32), jnp.zeros((15, WIDTH), F32)], axis=0
            ).astype(BF16)
            biases = up_bias[layer : layer + 1]
            up_t[layer, :WIDTH, WIDTH:EXTENDED] = bias_lanes(biases[:, :WIDTH])
            up_t[layer, WIDTH:FF, WIDTH:EXTENDED] = bias_lanes(biases[:, WIDTH:])
            half_down[layer] = w_down[layer] * jnp.asarray(0.5, BF16)
            down_t[layer] = half_down[layer].T

    masks = make_masks()
    weights = (qkv_t, out_t, up_t, down_t)
    raw = (w_qkv, w_out, w_up, half_down)

    def upward(item):
        tokens = slice(item * LEN, (item + 1) * LEN)
        place = step * per_step + item
        segments = segment_masks(seg_ref[pl.ds(place, 1)])
        hidden = x_ref[tokens].astype(F32).T
        middle_hidden, kept = yield from forward_layer(
            0, hidden, segments, masks, weights, columns, power_kept.at[place], mixed_scratch.at[item],
            scale_kept.at[place], gated_kept.at[place], twice_kept.at[place],
        )
        normed, query, keys, values, mixed, xhat, xhat_two, normed_two, rows = kept
        normed_kept[place] = normed
        qkv_kept[place, :WIDTH] = query
        qkv_kept[place, WIDTH : 2 * WIDTH] = keys
        qkv_kept[place, 2 * WIDTH :] = values
        mixed_kept[place] = mixed
        xhat_kept[place] = xhat
        xhat_two_kept[place] = xhat_two
        normed_two_kept[place] = normed_two
        rows_kept[place] = rows
        output, kept = yield from forward_layer(
            1, middle_hidden, segments, masks, weights, columns, power_last.at[item], mixed_scratch.at[item],
            scale_last.at[item], gated_last.at[item], twice_last.at[item],
        )
        result_ref[tokens] = output.T.astype(BF16)
        gradient = cot_ref[tokens].astype(F32).T
        grad_kept[place] = yield from backward_layer(
            1, gradient, masks, kept, power_last.at[item], scale_last.at[item], gated_last.at[item],
            twice_last.at[item], raw, columns, totals_one, dq_ref.at[item],
        )

    def downward(item):
        tokens = slice(item * LEN, (item + 1) * LEN)
        place = (step - steps) * per_step + item
        kept = (
            normed_kept[place], qkv_kept[place, :WIDTH], qkv_kept[place, WIDTH : 2 * WIDTH],
            qkv_kept[place, 2 * WIDTH :], mixed_kept[place], xhat_kept[place], xhat_two_kept[place],
            normed_two_kept[place], rows_kept[place],
        )
        gradient = yield from backward_layer(
            0, grad_kept[place], masks, kept, power_kept.at[place], scale_kept.at[place], gated_kept.at[place],
            twice_kept.at[place], raw, columns, totals_zero, dq_ref.at[item],
        )
        grad_inputs_ref[tokens] = gradient.T

    @pl.when(step < steps)
    def first_half():
        together([upward(item) for item in range(per_step)])

    @pl.when(step >= steps)
    def second_half():
        together([downward(item) for item in range(per_step)])

    @pl.when(step == 2 * steps - 1)
    def finish():
        for layer, part in enumerate((totals_zero, totals_one)):
            write_totals(
                part, grads_ref.at[layer], w_qkv[layer], w_gate[layer : layer + 1], w_up[layer], gains[layer],
                shifts[layer],
            )


def totals_scratch():
    return [
        pltpu.VMEM((WIDTH + 16, 3 * WIDTH), F32),
        pltpu.VMEM((WIDTH + 16, WIDTH), F32),
        pltpu.VMEM((WIDTH + 16, FF), F32),
        pltpu.VMEM((WIDTH, FF), F32),
        pltpu.VMEM((SUMS + 1, WIDTH, WIDTH), F32),
    ]


def local_part(inputs, segment_ids, cotangent, *parameters, per_step=4):
    seqs = segment_ids.shape[0]
    per_step = min(per_step, seqs)
    steps = seqs // per_step
    rows = (per_step * LEN, WIDTH)

    def whole(array):
        zero = (0,) * array.ndim
        return pl.BlockSpec(array.shape, lambda i: zero)

    def kept(rows, dtype, count=seqs):
        return pltpu.VMEM((count, rows, LEN), dtype)

    return pl.pallas_call(
        lambda *refs: kernel(per_step, steps, *refs),
        grid=(2 * steps,),
        in_specs=[
            pl.BlockSpec(rows, lambda i: (jnp.minimum(i, steps - 1), 0)),
            whole(segment_ids),
            pl.BlockSpec(rows, lambda i: (jnp.minimum(i, steps - 1), 0)),
        ]
        + [whole(entry) for entry in parameters],
        out_specs=[
            pl.BlockSpec(rows, lambda i: (jnp.minimum(i, steps - 1), 0)),
            pl.BlockSpec(rows, lambda i: (jnp.maximum(i - steps, 0), 0)),
            pl.BlockSpec((LAYERS, ROWS, WIDTH), lambda i: (0, 0, 0)),
        ],
        out_shape=[
            jax.ShapeDtypeStruct(inputs.shape, BF16),
            jax.ShapeDtypeStruct(inputs.shape, F32),
            jax.ShapeDtypeStruct((LAYERS, ROWS, WIDTH), F32),
        ],
        scratch_shapes=[
            pltpu.VMEM((LAYERS, COLUMNS, WIDTH, WIDTH), F32),
            pltpu.VMEM((LAYERS, 3 * WIDTH, 2 * WIDTH), BF16),
            pltpu.VMEM((LAYERS, WIDTH, 2 * WIDTH), BF16),
            pltpu.VMEM((LAYERS, FF + 16, 2 * WIDTH), BF16),
            pltpu.VMEM((LAYERS, WIDTH, FF), BF16),
            pltpu.VMEM((LAYERS, FF, WIDTH), BF16),
            kept(WIDTH, F32, per_step),
            kept(WIDTH, F32, per_step),
            kept(POWER_ROWS, BF16, per_step),
            kept(8 * HEADS, F32, per_step),
            kept(FF, F32, per_step),
            kept(FF, F32, per_step),
            kept(WIDTH, F32),
            kept(WIDTH, BF16),
            kept(3 * WIDTH, BF16),
            kept(WIDTH, F32),
            kept(8 * HEADS, F32),
            kept(WIDTH, F32),
            kept(WIDTH, F32),
            kept(WIDTH, BF16),
            kept(8, F32),
            kept(POWER_ROWS, BF16),
            kept(FF, F32),
            kept(FF, F32),
        ]
        + totals_scratch()
        + totals_scratch(),
        compiler_params=pltpu.CompilerParams(vmem_limit_bytes=60 * 1024 * 1024),
        name="layers",
    )(inputs, segment_ids, cotangent, *parameters)


def unpack_kernel(
    where_ref, near_ref, far_ref,
    gains_ref, shifts_ref, qkv_ref, qv_bias_ref, out_ref, out_bias_ref, gate_ref, up_ref, up_bias_ref, down_ref,
    down_bias_ref,
    grads,
):
    core, part = where_ref[0], where_ref[1]
    quarter = ROWS // 4
    for mask in range(4):
        place = pl.ds(pl.multiple_of((part ^ mask) * quarter, 8), quarter)
        rows = slice(mask * quarter, (mask + 1) * quarter)
        grads[core, place] = near_ref[rows]
        grads[1 - core, place] = far_ref[rows]
    for layer in range(LAYERS):
        for part in range(3):
            lanes = slice(part * WIDTH, (part + 1) * WIDTH)
            qkv_ref[layer, :, lanes] = grads[layer, R_QKV + part * WIDTH : R_QKV + (part + 1) * WIDTH]
        out_ref[layer] = grads[layer, R_OUT : R_OUT + WIDTH]
        for part in range(2):
            lanes = slice(part * WIDTH, (part + 1) * WIDTH)
            up_ref[layer, :, lanes] = grads[layer, R_UP + part * WIDTH : R_UP + (part + 1) * WIDTH]
        down_ref[layer] = grads[layer, R_DOWN : R_DOWN + FF]
        one = slice(layer, layer + 1)

        def row(which):
            return grads[layer, R_SMALL + which : R_SMALL + which + 1]

        gains_ref[layer, 0:1], gains_ref[layer, 1:2] = row(S_GAIN_ONE), row(S_GAIN_TWO)
        shifts_ref[layer, 0:1], shifts_ref[layer, 1:2] = row(S_SHIFT_ONE), row(S_SHIFT_TWO)
        qv_bias_ref[one, :WIDTH], qv_bias_ref[one, WIDTH:] = row(S_Q), row(S_V)
        out_bias_ref[one], gate_ref[one], down_bias_ref[one] = row(S_OUT), row(S_GATE), row(S_DOWN)
        up_bias_ref[one, :WIDTH], up_bias_ref[one, WIDTH:] = row(S_UP_LOW), row(S_UP_HIGH)


def unpack(where, near, far):
    shapes = [
        (LAYERS, 2, WIDTH), (LAYERS, 2, WIDTH), (LAYERS, WIDTH, 3 * WIDTH), (LAYERS, 2 * WIDTH), (LAYERS, WIDTH, WIDTH),
        (LAYERS, WIDTH), (LAYERS, WIDTH), (LAYERS, WIDTH, FF), (LAYERS, FF), (LAYERS, FF, WIDTH), (LAYERS, WIDTH),
    ]
    return pl.pallas_call(
        unpack_kernel,
        in_specs=[pl.BlockSpec(memory_space=pltpu.SMEM), pl.BlockSpec(), pl.BlockSpec()],
        out_shape=[jax.ShapeDtypeStruct(shape, F32) for shape in shapes],
        scratch_shapes=[pltpu.VMEM((LAYERS, ROWS, WIDTH), F32)],
        compiler_params=pltpu.CompilerParams(vmem_limit_bytes=16 * 1024 * 1024),
        name="unpack",
    )(where, near, far)


def all_sum(grads, size):
    me = lax.axis_index("seq")
    bits = size.bit_length() - 1
    core, part = me & 1, (me >> 1) & 3

    def swap(value, mask):
        return lax.ppermute(value, "seq", [(i, i ^ mask) for i in range(size)])

    def pick(value, index):
        return lax.dynamic_index_in_dim(value, index, 0, keepdims=False)

    layer = pick(grads, core) + swap(pick(grads, 1 - core), 1)
    quarters = layer.reshape(4, ROWS // 4, WIDTH)
    others = [swap(pick(quarters, part ^ mask), 2 * mask) for mask in (1, 2, 3)]
    mine = pick(quarters, part) + others[0] + others[1] + others[2]
    for bit in range(3, bits):
        mine = mine + swap(mine, 1 << bit)
    near = jnp.concatenate([mine] + [swap(mine, 2 * mask) for mask in (1, 2, 3)], axis=0)
    return jnp.stack([core, part]).astype(jnp.int32), near, swap(near, 1)


def body(size, *arguments):
    result, grad_inputs, grads = local_part(*arguments)
    if size & (size - 1) or size < 8:
        grads = lax.psum(grads, "seq")
        summed = (jnp.zeros((2,), jnp.int32), grads[0], grads[1])
    else:
        summed = all_sum(grads, size)
    return (result, grad_inputs) + tuple(unpack(*summed))


def solution(mesh):
    rows = P("seq", None)
    return jax.shard_map(
        lambda *arguments: body(mesh.shape["seq"], *arguments),
        mesh=mesh,
        in_specs=(rows, rows, rows) + (P(),) * 11,
        out_specs=(rows, rows) + (P(),) * 11,
        check_vma=False,
    )
```

```python
import jax
import jax.numpy as jnp
from jax import lax
from jax.experimental import pallas as pl
from jax.experimental.pallas import tpu as pltpu
from jax.sharding import PartitionSpec as P

HEADS = 8
LAYERS = 2
WIDTH = 128
FF = 256
LEN = 256
HALF = 128
CHUNK = 256
AHEAD = 44
QUARTER = 64
WINDOWS = ((0, 128), (0, 192), (64, 256), (128, 256))
PLACES = ((0, 128), (256, 448), (640, 832), (1024, 1152))
POWER_ROWS = 1280
FAR = -1.0e9
GELU_A = 0.7978845608028654
GELU_B = 0.044715
F32 = jnp.float32
BF16 = jnp.bfloat16

GAIN_ONE, SHIFT_ONE, GAIN_TWO, SHIFT_TWO, DOWN_BIAS, GATE = range(6)
COLUMNS = 6
EXTENDED = WIDTH + 16
S_DOWN, S_GATE = range(2)
SUMS = 2
S_LOGIT = 2
S_OUT, S_Q, S_K, S_V, S_UP_LOW, S_UP_HIGH, S_SHIFT_ONE, S_SHIFT_TWO, S_GAIN_ONE, S_GAIN_TWO = range(2, 12)
R_QKV, R_OUT, R_UP, R_DOWN, R_SMALL, ROWS = 0, 384, 512, 768, 1024, 1056


def dot(left, right):
    return lax.dot_general(left, right, (((1,), (0,)), ((), ())), preferred_element_type=F32)


def both(column):
    return jnp.concatenate([column, column], axis=1)


def fold(value):
    return value[:, :HALF] + value[:, HALF:]


def zeros(rows, lanes=LEN):
    return jnp.zeros((rows, lanes), BF16)


def ones(rows, lanes=LEN):
    return jnp.ones((rows, lanes), BF16)


def split_three(value):
    high = value.astype(BF16)
    rest = value - high.astype(F32)
    middle = rest.astype(BF16)
    low = (rest - middle.astype(F32)).astype(BF16)
    return high, middle, low


def norm_parts(value):
    average = jnp.sum(value, axis=0, keepdims=True) * (1.0 / WIDTH)
    centered = value - average
    variance = jnp.sum(centered * centered, axis=0, keepdims=True) * (1.0 / WIDTH)
    scale = lax.rsqrt(variance + 1e-05)
    return centered * scale, scale


def lane_mask(rows, which):
    row = lax.broadcasted_iota(jnp.int32, (rows, HALF), 0)
    lane = lax.broadcasted_iota(jnp.int32, (rows, HALF), 1)
    return jnp.where(which(row, lane < QUARTER), 1.0, 0.0).astype(BF16)


def turned(rows):
    return jnp.concatenate(
        [rows[:, 64:128], rows[:, :64], rows[:, 192:256], rows[:, 128:192]], axis=1
    )


def make_masks():
    low = lane_mask(16, lambda row, left: left)
    high = lane_mask(16, lambda row, left: ~left)
    heads = [
        lane_mask(16, lambda row, left, head=head: (row % 4 == head) & (left if head % 2 == 0 else ~left))
        for head in range(4)
    ]
    return low, high, heads


def halves_of(rows, masks):
    low, high, unused = masks
    count = rows.shape[0] // 16
    low_all = jnp.concatenate([both(low)] * count, axis=0)
    high_all = jnp.concatenate([both(high)] * count, axis=0)
    other = turned(rows)
    return ((rows * low_all, other * high_all), (other * low_all, rows * high_all))


def head_block(variants, block, group):
    lanes = slice((block // 2) * HALF, (block // 2 + 1) * HALF)
    gap = zeros(16, HALF)
    pieces = []
    for head in range(4):
        first = QUARTER * group + 16 * head
        piece = variants[block % 2][head % 2][first : first + 16, lanes]
        pieces.append(jnp.concatenate([piece, gap] if head < 2 else [gap, piece], axis=1))
    return jnp.concatenate(pieces, axis=0)


def with_extra(features, extra):
    return jnp.concatenate([features, extra], axis=0)


def spread_marks(rows, masks, block):
    low, high, unused = masks
    lanes = slice((block // 2) * HALF, (block // 2 + 1) * HALF)
    here, there = rows[:, lanes], turned(rows)[:, lanes]
    once = here * low + there * high if block % 2 == 0 else there * low + here * high
    return both(once)


def spread_rows(rows, masks, block):
    unused, unused, heads = masks
    lanes = slice((block // 2) * HALF, (block // 2 + 1) * HALF)
    here, there = rows[:, lanes], turned(rows)[:, lanes]
    if block % 2 == 1:
        here, there = there, here
    return jnp.concatenate([here * heads[0] + there * heads[1], here * heads[2] + there * heads[3]], axis=1)


def join_blocks(even, odd, head):
    left = lax.broadcasted_iota(jnp.int32, even.shape, 1) < QUARTER
    if head % 2 == 0:
        return jnp.where(left, even, pltpu.roll(odd, QUARTER, 1))
    return jnp.where(left, pltpu.roll(even, QUARTER, 1), odd)


def token_rows(rows, extra):
    return [
        jnp.concatenate([rows[QUARTER * group : QUARTER * group + QUARTER], extra], axis=0).T for group in range(2)
    ]


def skewed(units):
    running, waiting = [], list(units)
    while running or waiting:
        if waiting:
            running.append(waiting.pop(0))
        running = [unit for unit in running if next(unit, "end") != "end"]
        yield


def together(parts, late=(), wait=0):
    running, waiting, turn = [], list(parts), 0
    while running or waiting:
        if waiting:
            running.append(waiting.pop(0))
        if turn >= wait and late:
            running.append(late.pop(0))
        running = [part for part in running if next(part, "end") != "end"]
        turn += 1
    assert not late


def segment_masks(segments):
    ids = lax.broadcasted_iota(jnp.int32, (16, LEN), 0)
    same = ids == segments
    one_hot = jnp.where(same, 1.0, 0.0).astype(BF16)
    other = jnp.where(same | (ids >= 8), 0.0, FAR).astype(BF16)
    return one_hot, other


def forward_unit(block, group, keys_rows, variants, values, marks, power_ref, mixed_ref, scale_ref, results):
    first, last = WINDOWS[block]
    weights = with_extra(head_block(variants, block, group), marks[block])
    scores = dot(keys_rows[first:last], weights)
    yield
    peak = jnp.max(scores, axis=0, keepdims=True)
    powers = jnp.exp(scores - peak).astype(BF16)
    start = PLACES[block][group]
    power_ref[start : start + last - first] = powers
    yield
    rows = values[QUARTER * group : QUARTER * group + QUARTER, first:last]
    mixed = dot(jnp.concatenate([rows, ones(16, last - first)], axis=0), powers)
    yield
    scale = 1.0 / mixed[QUARTER : QUARTER + 8]
    results[block, group] = (mixed, scale)
    if block % 2 == 0:
        return
    even, even_scale = results[block - 1, group]
    lanes = slice((block // 2) * HALF, (block // 2 + 1) * HALF)
    for head in range(4):
        tile = slice((head // 2) * HALF, (head // 2 + 1) * HALF)
        rows = slice(16 * head, 16 * head + 16)
        factor = join_blocks(even_scale[:, tile], scale[:, tile], head)
        joined = join_blocks(even[rows, tile], mixed[rows, tile], head)
        place = QUARTER * group + 16 * head
        mixed_ref[place : place + 16, lanes] = joined * jnp.concatenate([factor, factor], axis=0)
        place = 8 * (4 * group + head)
        scale_ref[place : place + 8, lanes] = factor


def attention_forward(query, keys, values, segments, masks, power_ref, mixed_ref, scale_ref):
    one_hot, other = segments
    rows = token_rows(keys, other)
    variants = halves_of(query, masks)
    marks = [spread_marks(one_hot, masks, block) for block in range(4)]
    yield
    results = {}
    yield from skewed(
        forward_unit(block, group, rows[group], variants, values, marks, power_ref, mixed_ref, scale_ref, results)
        for block in (0, 1, 2, 3)
        for group in range(2)
    )


def project(layer, hidden, weights, columns):
    column = lambda which: both(columns[layer, which])
    xhat, spread_one = norm_parts(hidden)
    normed = (xhat * column(GAIN_ONE) + column(SHIFT_ONE)).astype(BF16)
    yield
    projected = dot(weights[0][layer][:, :EXTENDED], jnp.concatenate([normed, ones(16)], axis=0))
    yield
    return xhat, spread_one, normed, projected.astype(BF16)


def forward_layer(layer, hidden, projected, segments, masks, weights, columns, power_ref, mixed_ref, scale_ref):
    unused, out_t, up_t, unused = weights
    column = lambda which: both(columns[layer, which])
    query, keys, values = (projected[part * WIDTH : (part + 1) * WIDTH] for part in range(3))
    yield from attention_forward(query, keys, values, segments, masks, power_ref, mixed_ref, scale_ref)
    mixed = mixed_ref[...]
    middle = hidden + dot(out_t[layer][:, :EXTENDED], jnp.concatenate([mixed.astype(BF16), ones(16)], axis=0))
    yield
    xhat_two, spread_two = norm_parts(middle)
    normed_two = (xhat_two * column(GAIN_TWO) + column(SHIFT_TWO)).astype(BF16)
    yield
    inner = dot(up_t[layer][:, :EXTENDED], jnp.concatenate([normed_two, ones(16)], axis=0))
    yield
    gate = jax.nn.sigmoid(inner[FF : FF + 1])
    return middle, inner[:FF], mixed, xhat_two, spread_two, normed_two, gate


def gated_unit(inner, gate):
    gated = inner * gate
    return gated, 1.0 + jnp.tanh(gated * (GELU_A + (GELU_A * GELU_B) * (gated * gated)))


def feed_forward(layer, middle, inner, gate, weights, columns, gated_ref, twice_ref):
    parts = []
    for start in range(0, FF, CHUNK):
        rows = slice(start, start + CHUNK)
        gated, twice_up = gated_unit(inner[rows], gate)
        gated_ref[rows] = gated
        twice_ref[rows] = twice_up
        parts.append((gated * twice_up).astype(BF16))
        yield
    return feed_output(layer, middle, jnp.concatenate(parts, axis=0), weights, columns)


def feed_output(layer, middle, active, weights, columns):
    return middle + (dot(weights[3][layer], active) + both(columns[layer, DOWN_BIAS]))


def norm_backward(gradient, xhat, scale, gain):
    inner = gradient * gain
    first = jnp.sum(inner, axis=0, keepdims=True) * (1.0 / WIDTH)
    second = jnp.sum(inner * xhat, axis=0, keepdims=True) * (1.0 / WIDTH)
    return scale * (inner - first - xhat * second)


def backward_unit(block, values_rows, query_variants, grad_variants, keys, deltas, power_ref, results, dq_ref, turned_ref):
    first, last = WINDOWS[block]
    query_blocks = [head_block(query_variants, block, group) for group in range(2)]
    grad_blocks = [head_block(grad_variants, block, group) for group in range(2)]
    products = [
        dot(values_rows[group][first:last], with_extra(grad_blocks[group], deltas[block][group]))
        for group in range(2)
    ]
    yield
    powers, grad_scores = [], []
    for group in range(2):
        start = PLACES[block][group]
        powers.append(power_ref[start : start + last - first])
        grad_scores.append((powers[group].astype(F32) * products[group]).astype(BF16))
        yield
    mixed = [
        dot(keys[QUARTER * group : QUARTER * group + QUARTER, first:last], grad_scores[group]) for group in range(2)
    ]

    def together_rows(blocks):
        gap = zeros(QUARTER)
        low = jnp.concatenate([blocks[0], gap], axis=0)
        high = jnp.concatenate([gap, blocks[1]], axis=0)
        return jnp.concatenate([low, high], axis=1)

    grad_keys = dot(jnp.concatenate(grad_scores, axis=1), together_rows(query_blocks).T)
    flipped = []
    for group in range(2):
        turned_ref[0 + 2 * block + group, :, : last - first] = powers[group].T
        flipped.append(dot(grad_blocks[group], turned_ref[0 + 2 * block + group, :, : last - first]))
    grad_values = jnp.concatenate(flipped, axis=0)
    results[block] = (grad_keys, grad_values, mixed)
    yield
    if block % 2 == 0:
        return
    lanes = slice((block // 2) * HALF, (block // 2 + 1) * HALF)
    for group in range(2):
        even, odd = results[block - 1][2][group], mixed[group]
        for head in range(4):
            tile = slice((head // 2) * HALF, (head // 2 + 1) * HALF)
            rows = slice(16 * head, 16 * head + 16)
            place = QUARTER * group + 16 * head
            dq_ref[place : place + 16, lanes] = join_blocks(even[rows, tile], odd[rows, tile], head)


def attention_backward(query, keys, values, mixed, scale, grad_mixed, masks, power_ref, dq_ref, turned_ref):
    factors = [scale[8 * head : 8 * head + 8] for head in range(HEADS)]
    grad = (grad_mixed * jnp.concatenate([row for factor in factors for row in (factor, factor)], axis=0)).astype(BF16)
    product = grad.astype(F32) * mixed
    delta = jnp.concatenate(
        [jnp.sum(product[16 * head : 16 * head + 16], axis=0, keepdims=True) for head in range(HEADS)], axis=0
    )
    yield
    parts = [part.astype(F32) for part in split_three(-delta)]
    gap = jnp.zeros((4, LEN), F32)
    extras = [
        jnp.concatenate([part[4 * group : 4 * group + 4] for part in parts] + [gap], axis=0).astype(BF16)
        for group in range(2)
    ]
    deltas = [[spread_rows(extras[group], masks, block) for group in range(2)] for block in range(4)]
    query_variants = halves_of(query, masks)
    grad_variants = halves_of(grad, masks)
    rows = token_rows(values, ones(16))
    yield
    results = {}
    yield from skewed(
        backward_unit(block, rows, query_variants, grad_variants, keys, deltas, power_ref, results, dq_ref, turned_ref)
        for block in range(4)
    )

    def collect_lanes(which):
        parts = [results[block][which] for block in range(4)]
        gap = jnp.zeros((WIDTH, QUARTER), F32)
        first = jnp.concatenate([parts[0], parts[3]], axis=1)
        second = jnp.concatenate([parts[1], gap], axis=1)
        third = jnp.concatenate([gap, parts[2]], axis=1)
        return (first + second + third).astype(BF16)

    def collect(which):
        parts = [results[block][which] for block in range(4)]
        return jnp.concatenate(
            [
                parts[0][:64] + parts[1][:64],
                parts[0][64:] + parts[1][64:128] + parts[2][:64],
                parts[1][128:] + parts[2][64:128] + parts[3][:64],
                parts[2][128:] + parts[3][64:],
            ],
            axis=0,
        ).astype(BF16)

    return (dq_ref[...] * 0.25).astype(BF16), collect(0), collect_lanes(1).T


def backward_layer(
    layer, gradient, masks, kept, power_ref, scale_ref, units, use_active, raw, columns, totals, dq_ref, turned_ref
):
    w_qkv, w_out, w_up, w_down = raw
    normed, query, keys, values, mixed, xhat, xhat_two, normed_two, rows = kept
    spread_one, spread_two, gate = rows[0:1], rows[1:2], rows[2:3]
    qkv_total, out_total, up_total, down_total, sums = totals
    column = lambda which: both(columns[layer, which])
    branch = gradient.astype(BF16)
    sums[S_DOWN] += fold(gradient)
    grad_active = dot(w_down[layer], branch)
    yield
    actives, inners = [], []
    logit_sum = jnp.zeros((1, LEN), F32)
    for start in range(0, FF, CHUNK):
        rows = slice(start, start + CHUNK)
        gated, twice_up = units(rows)
        active = gated * twice_up
        curve = GELU_A + (3.0 * GELU_A * GELU_B) * (gated * gated)
        slope = twice_up + (active * (2.0 - twice_up)) * curve
        grad_gated = grad_active[rows] * slope
        logit_sum = logit_sum + jnp.sum(grad_gated * gated, axis=0, keepdims=True)
        actives.append(active.astype(BF16))
        inners.append((grad_gated * gate).astype(BF16))
        yield
    grad_logit = logit_sum * (1.0 - gate)
    active = jnp.concatenate(actives, axis=0)
    use_active(active)
    grad_inner = jnp.concatenate(inners, axis=0)
    grad_two = dot(w_up[layer], grad_inner) + column(GATE) * grad_logit
    down_total[...] += dot(branch, active.T)
    up_total[...] += dot(jnp.concatenate([normed_two, ones(16)], axis=0), grad_inner.T)
    sums[S_GATE] += fold(normed_two.astype(F32) * grad_logit)
    sums[S_LOGIT, 0:1] += fold(grad_logit)
    yield
    grad_middle = gradient + norm_backward(grad_two, xhat_two, spread_two, column(GAIN_TWO))
    attended = grad_middle.astype(BF16)
    yield
    grad_mixed = dot(w_out[layer], attended)
    out_total[...] += dot(jnp.concatenate([mixed.astype(BF16), ones(16)], axis=0), attended.T)
    yield
    grad_query, grad_keys, grad_values = yield from attention_backward(
        query, keys, values, mixed, scale_ref[...], grad_mixed, masks, power_ref, dq_ref, turned_ref
    )
    yield
    grad_rows = jnp.concatenate([grad_query.T, grad_keys, grad_values], axis=1)
    qkv_total[...] += dot(jnp.concatenate([normed, ones(16)], axis=0), grad_rows)
    grad_one = dot(w_qkv[layer], jnp.concatenate([grad_query, grad_keys.T, grad_values.T], axis=0))
    yield
    return grad_middle + norm_backward(grad_one, xhat, spread_one, column(GAIN_ONE))


def spread(row):
    return jnp.broadcast_to(row, (WIDTH, WIDTH)).T


def bias_lanes(row):
    parts = [part.astype(F32) for part in split_three(row)]
    return jnp.concatenate(parts + [jnp.zeros((13, WIDTH), F32)], axis=0).T.astype(BF16)


def fill_columns(layer, columns, gains, shifts, w_gate, down_bias):
    columns[layer, GAIN_ONE] = spread(gains[layer, 0:1])
    columns[layer, GAIN_TWO] = spread(gains[layer, 1:2])
    columns[layer, SHIFT_ONE] = spread(shifts[layer, 0:1])
    columns[layer, SHIFT_TWO] = spread(shifts[layer, 1:2])
    columns[layer, DOWN_BIAS] = spread(down_bias[layer : layer + 1])
    columns[layer, GATE] = spread(w_gate[layer : layer + 1].astype(F32))


def clear_totals(totals):
    for ref in totals:
        ref[...] = jnp.zeros_like(ref)


def through(weights, row):
    parts = jnp.concatenate(split_three(row), axis=0)
    return jnp.sum(lax.dot_general(parts, weights, (((1,), (1,)), ((), ())), preferred_element_type=F32), axis=0, keepdims=True)


def across(value):
    parts = [value[:, start : start + WIDTH] for start in range(0, value.shape[1], WIDTH)]
    total = parts[0]
    for part in parts[1:]:
        total = total + part
    return jnp.sum(total.T, axis=0, keepdims=True)


def write_totals(totals, grads_ref, w_qkv, w_gate, w_up, gains, shifts):
    qkv_total, out_total, up_total, down_total, sums = totals
    for part in range(3):
        rows = slice(R_QKV + part * WIDTH, R_QKV + (part + 1) * WIDTH)
        grads_ref[rows] = qkv_total[:WIDTH, part * WIDTH : (part + 1) * WIDTH]
    grads_ref[R_OUT : R_OUT + WIDTH] = out_total[:WIDTH]
    for part in range(2):
        lanes = slice(part * WIDTH, (part + 1) * WIDTH)
        grads_ref[R_UP + part * WIDTH : R_UP + (part + 1) * WIDTH] = up_total[:WIDTH, lanes]
        grads_ref[R_DOWN + part * WIDTH : R_DOWN + (part + 1) * WIDTH] = down_total[:, lanes].T * 0.5
    rows = [jnp.sum(sums[which].T, axis=0, keepdims=True) for which in range(SUMS)]
    rows.append(out_total[WIDTH : WIDTH + 1])
    rows.extend(qkv_total[WIDTH : WIDTH + 1, part * WIDTH : (part + 1) * WIDTH] for part in range(3))
    rows.extend(up_total[WIDTH : WIDTH + 1, part * WIDTH : (part + 1) * WIDTH] for part in range(2))
    rows.append(through(w_qkv, qkv_total[WIDTH : WIDTH + 1]))
    logit = jnp.sum(sums[S_LOGIT, 0:1], axis=1, keepdims=True)
    rows.append(through(w_up, up_total[WIDTH : WIDTH + 1]) + logit * w_gate.astype(F32))
    moments = (
        across(qkv_total[:WIDTH] * w_qkv.astype(F32)),
        across(up_total[:WIDTH] * w_up.astype(F32)) + rows[S_GATE] * w_gate.astype(F32),
    )
    for which, moment in enumerate(moments):
        norm = slice(which, which + 1)
        rows.append((moment - shifts[norm] * rows[S_SHIFT_ONE + which]) / gains[norm])
    rows.append(jnp.zeros((ROWS - R_SMALL - len(rows), WIDTH), F32))
    grads_ref[R_SMALL:ROWS] = jnp.concatenate(rows, axis=0)


def kernel(
    per_step, steps,
    x_ref, x_next_ref, seg_ref, cot_ref, gains, shifts, w_qkv, qv_bias, w_out, out_bias, w_gate, w_up, up_bias, w_down, down_bias,
    result_ref, grad_inputs_ref, grads_ref,
    columns, qkv_t, out_t, up_t, down_t, half_down, mixed_scratch, dq_ref, turned_ref, power_last, scale_last,
    grad_kept, normed_kept, qkv_kept, mixed_kept, scale_kept, xhat_kept, xhat_two_kept, normed_two_kept, rows_kept,
    power_kept, gated_kept, twice_kept, *totals,
):
    step = pl.program_id(0)
    totals_zero, totals_one = totals[: len(totals) // 2], totals[len(totals) // 2 :]

    @pl.when(step == 0)
    def start():
        clear_totals(totals)
        for layer in range(LAYERS):
            fill_columns(layer, columns, gains, shifts, w_gate, down_bias)
            for ref in (qkv_t, out_t, up_t):
                ref[layer, :, WIDTH:] = zeros(ref.shape[1], WIDTH)
            qkv_t[layer, :WIDTH, :WIDTH] = (w_qkv[layer][:, :WIDTH] * jnp.asarray(0.25, BF16)).T
            qkv_t[layer, WIDTH:, :WIDTH] = w_qkv[layer][:, WIDTH:].T
            biases = qv_bias[layer : layer + 1]
            qkv_t[layer, :WIDTH, WIDTH:EXTENDED] = bias_lanes(biases[:, :WIDTH] * 0.25)
            qkv_t[layer, 2 * WIDTH :, WIDTH:EXTENDED] = bias_lanes(biases[:, WIDTH:])
            out_t[layer, :, :WIDTH] = w_out[layer].T
            out_t[layer, :, WIDTH:EXTENDED] = bias_lanes(out_bias[layer : layer + 1])
            up_t[layer, :FF, :WIDTH] = w_up[layer].T
            up_t[layer, FF:, :WIDTH] = jnp.concatenate(
                [w_gate[layer : layer + 1].astype(F32), jnp.zeros((15, WIDTH), F32)], axis=0
            ).astype(BF16)
            biases = up_bias[layer : layer + 1]
            up_t[layer, :WIDTH, WIDTH:EXTENDED] = bias_lanes(biases[:, :WIDTH])
            up_t[layer, WIDTH:FF, WIDTH:EXTENDED] = bias_lanes(biases[:, WIDTH:])
            half_down[layer] = w_down[layer] * jnp.asarray(0.5, BF16)
            down_t[layer] = half_down[layer].T

    masks = make_masks()
    weights = (qkv_t, out_t, up_t, down_t)
    raw = (w_qkv, w_out, w_up, half_down)

    def ahead(item, ref, group):
        place = group * per_step + item
        hidden = ref[item * LEN : (item + 1) * LEN].astype(F32).T
        xhat, spread_one, normed, projected = yield from project(0, hidden, weights, columns)
        xhat_kept[place] = xhat
        rows_kept[place, 0:1] = spread_one
        normed_kept[place] = normed
        qkv_kept[place] = projected

    def upward(item):
        tokens = slice(item * LEN, (item + 1) * LEN)
        place = step * per_step + item
        segments = segment_masks(seg_ref[pl.ds(place, 1)])
        hidden = x_ref[tokens].astype(F32).T
        middle, inner, mixed, xhat_two, spread_two, normed_two, gate = yield from forward_layer(
            0, hidden, qkv_kept[place], segments, masks, weights, columns, power_kept.at[place], mixed_scratch.at[item],
            scale_kept.at[place],
        )
        mixed_kept[place] = mixed
        xhat_two_kept[place] = xhat_two
        normed_two_kept[place] = normed_two
        rows_kept[place, 1:2] = spread_two
        rows_kept[place, 2:3] = gate
        hidden = yield from feed_forward(
            0, middle, inner, gate, weights, columns, gated_kept.at[place], twice_kept.at[place]
        )
        xhat, spread_one, normed, projected = yield from project(1, hidden, weights, columns)
        middle, inner, mixed, xhat_two, spread_two, normed_two, gate = yield from forward_layer(
            1, hidden, projected, segments, masks, weights, columns, power_last.at[item], mixed_scratch.at[item],
            scale_last.at[item],
        )
        kept = (
            normed, projected[:WIDTH], projected[WIDTH : 2 * WIDTH], projected[2 * WIDTH :], mixed, xhat, xhat_two,
            normed_two, jnp.concatenate([spread_one, spread_two, gate], axis=0),
        )

        def last_units(rows):
            return gated_unit(inner[rows], gate)

        def write_result(active):
            result_ref[tokens] = feed_output(1, middle, active, weights, columns).T.astype(BF16)

        gradient = cot_ref[tokens].astype(F32).T
        grad_kept[place] = yield from backward_layer(
            1, gradient, masks, kept, power_last.at[item], scale_last.at[item], last_units, write_result, raw, columns,
            totals_one, dq_ref.at[item], turned_ref.at[item],
        )

    def downward(item):
        tokens = slice(item * LEN, (item + 1) * LEN)
        place = (step - steps) * per_step + item
        kept = (
            normed_kept[place], qkv_kept[place, :WIDTH], qkv_kept[place, WIDTH : 2 * WIDTH],
            qkv_kept[place, 2 * WIDTH :], mixed_kept[place], xhat_kept[place], xhat_two_kept[place],
            normed_two_kept[place], rows_kept[place],
        )
        gradient = yield from backward_layer(
            0, grad_kept[place], masks, kept, power_kept.at[place], scale_kept.at[place],
            lambda rows: (gated_kept[place, rows], twice_kept[place, rows]), lambda active: None, raw, columns,
            totals_zero, dq_ref.at[item], turned_ref.at[item],
        )
        grad_inputs_ref[tokens] = gradient.T

    @pl.when(step == 0)
    def begin():
        together([ahead(item, x_ref, 0) for item in range(per_step)])

    @pl.when(step < steps)
    def first_half():
        following = lax.rem(step + 1, steps)
        together(
            [upward(item) for item in range(per_step)],
            [ahead(item, x_next_ref, following) for item in range(per_step)],
            AHEAD,
        )

    @pl.when(step >= steps)
    def second_half():
        together([downward(item) for item in range(per_step)])

    @pl.when(step == 2 * steps - 1)
    def finish():
        for layer, part in enumerate((totals_zero, totals_one)):
            write_totals(
                part, grads_ref.at[layer], w_qkv[layer], w_gate[layer : layer + 1], w_up[layer], gains[layer],
                shifts[layer],
            )


def totals_scratch():
    return [
        pltpu.VMEM((WIDTH + 16, 3 * WIDTH), F32),
        pltpu.VMEM((WIDTH + 16, WIDTH), F32),
        pltpu.VMEM((WIDTH + 16, FF), F32),
        pltpu.VMEM((WIDTH, FF), F32),
        pltpu.VMEM((SUMS + 1, WIDTH, WIDTH), F32),
    ]


def local_part(inputs, segment_ids, cotangent, *parameters, per_step=4):
    seqs = segment_ids.shape[0]
    per_step = min(per_step, seqs)
    steps = seqs // per_step
    rows = (per_step * LEN, WIDTH)

    def whole(array):
        zero = (0,) * array.ndim
        return pl.BlockSpec(array.shape, lambda i: zero)

    def kept(rows, dtype, count=seqs):
        return pltpu.VMEM((count, rows, LEN), dtype)

    return pl.pallas_call(
        lambda *refs: kernel(per_step, steps, *refs),
        grid=(2 * steps,),
        in_specs=[
            pl.BlockSpec(rows, lambda i: (jnp.minimum(i, steps - 1), 0)),
            pl.BlockSpec(rows, lambda i: (jnp.minimum(i + 1, steps) % steps, 0)),
            whole(segment_ids),
            pl.BlockSpec(rows, lambda i: (jnp.minimum(i, steps - 1), 0)),
        ]
        + [whole(entry) for entry in parameters],
        out_specs=[
            pl.BlockSpec(rows, lambda i: (jnp.minimum(i, steps - 1), 0)),
            pl.BlockSpec(rows, lambda i: (jnp.maximum(i - steps, 0), 0)),
            pl.BlockSpec((LAYERS, ROWS, WIDTH), lambda i: (0, 0, 0)),
        ],
        out_shape=[
            jax.ShapeDtypeStruct(inputs.shape, BF16),
            jax.ShapeDtypeStruct(inputs.shape, F32),
            jax.ShapeDtypeStruct((LAYERS, ROWS, WIDTH), F32),
        ],
        scratch_shapes=[
            pltpu.VMEM((LAYERS, COLUMNS, WIDTH, WIDTH), F32),
            pltpu.VMEM((LAYERS, 3 * WIDTH, 2 * WIDTH), BF16),
            pltpu.VMEM((LAYERS, WIDTH, 2 * WIDTH), BF16),
            pltpu.VMEM((LAYERS, FF + 16, 2 * WIDTH), BF16),
            pltpu.VMEM((LAYERS, WIDTH, FF), BF16),
            pltpu.VMEM((LAYERS, FF, WIDTH), BF16),
            kept(WIDTH, F32, per_step),
            kept(WIDTH, F32, per_step),
            pltpu.VMEM((per_step, 8, LEN, LEN), BF16),
            kept(POWER_ROWS, BF16, per_step),
            kept(8 * HEADS, F32, per_step),
            kept(WIDTH, F32),
            kept(WIDTH, BF16),
            kept(3 * WIDTH, BF16),
            kept(WIDTH, F32),
            kept(8 * HEADS, F32),
            kept(WIDTH, F32),
            kept(WIDTH, F32),
            kept(WIDTH, BF16),
            kept(8, F32),
            kept(POWER_ROWS, BF16),
            kept(FF, F32),
            kept(FF, F32),
        ]
        + totals_scratch()
        + totals_scratch(),
        compiler_params=pltpu.CompilerParams(vmem_limit_bytes=60 * 1024 * 1024),
        name="layers",
    )(inputs, inputs, segment_ids, cotangent, *parameters)


def unpack_kernel(
    where_ref, near_ref, far_ref,
    gains_ref, shifts_ref, qkv_ref, qv_bias_ref, out_ref, out_bias_ref, gate_ref, up_ref, up_bias_ref, down_ref,
    down_bias_ref,
    grads,
):
    core, part = where_ref[0], where_ref[1]
    quarter = ROWS // 4
    for mask in range(4):
        place = pl.ds(pl.multiple_of((part ^ mask) * quarter, 8), quarter)
        rows = slice(mask * quarter, (mask + 1) * quarter)
        grads[core, place] = near_ref[rows]
        grads[1 - core, place] = far_ref[rows]
    for layer in range(LAYERS):
        for part in range(3):
            lanes = slice(part * WIDTH, (part + 1) * WIDTH)
            qkv_ref[layer, :, lanes] = grads[layer, R_QKV + part * WIDTH : R_QKV + (part + 1) * WIDTH]
        out_ref[layer] = grads[layer, R_OUT : R_OUT + WIDTH]
        for part in range(2):
            lanes = slice(part * WIDTH, (part + 1) * WIDTH)
            up_ref[layer, :, lanes] = grads[layer, R_UP + part * WIDTH : R_UP + (part + 1) * WIDTH]
        down_ref[layer] = grads[layer, R_DOWN : R_DOWN + FF]
        one = slice(layer, layer + 1)

        def row(which):
            return grads[layer, R_SMALL + which : R_SMALL + which + 1]

        gains_ref[layer, 0:1], gains_ref[layer, 1:2] = row(S_GAIN_ONE), row(S_GAIN_TWO)
        shifts_ref[layer, 0:1], shifts_ref[layer, 1:2] = row(S_SHIFT_ONE), row(S_SHIFT_TWO)
        qv_bias_ref[one, :WIDTH], qv_bias_ref[one, WIDTH:] = row(S_Q), row(S_V)
        out_bias_ref[one], gate_ref[one], down_bias_ref[one] = row(S_OUT), row(S_GATE), row(S_DOWN)
        up_bias_ref[one, :WIDTH], up_bias_ref[one, WIDTH:] = row(S_UP_LOW), row(S_UP_HIGH)


def unpack(where, near, far):
    shapes = [
        (LAYERS, 2, WIDTH), (LAYERS, 2, WIDTH), (LAYERS, WIDTH, 3 * WIDTH), (LAYERS, 2 * WIDTH), (LAYERS, WIDTH, WIDTH),
        (LAYERS, WIDTH), (LAYERS, WIDTH), (LAYERS, WIDTH, FF), (LAYERS, FF), (LAYERS, FF, WIDTH), (LAYERS, WIDTH),
    ]
    return pl.pallas_call(
        unpack_kernel,
        in_specs=[pl.BlockSpec(memory_space=pltpu.SMEM), pl.BlockSpec(), pl.BlockSpec()],
        out_shape=[jax.ShapeDtypeStruct(shape, F32) for shape in shapes],
        scratch_shapes=[pltpu.VMEM((LAYERS, ROWS, WIDTH), F32)],
        compiler_params=pltpu.CompilerParams(vmem_limit_bytes=16 * 1024 * 1024),
        name="unpack",
    )(where, near, far)


def all_sum(grads, size):
    me = lax.axis_index("seq")
    bits = size.bit_length() - 1
    core, part = me & 1, (me >> 1) & 3

    def swap(value, mask):
        return lax.ppermute(value, "seq", [(i, i ^ mask) for i in range(size)])

    def pick(value, index):
        return lax.dynamic_index_in_dim(value, index, 0, keepdims=False)

    layer = pick(grads, core) + swap(pick(grads, 1 - core), 1)
    quarters = layer.reshape(4, ROWS // 4, WIDTH)
    others = [swap(pick(quarters, part ^ mask), 2 * mask) for mask in (1, 2, 3)]
    mine = pick(quarters, part) + others[0] + others[1] + others[2]
    for bit in range(3, bits):
        mine = mine + swap(mine, 1 << bit)
    near = jnp.concatenate([mine] + [swap(mine, 2 * mask) for mask in (1, 2, 3)], axis=0)
    return jnp.stack([core, part]).astype(jnp.int32), near, swap(near, 1)


def body(size, *arguments):
    result, grad_inputs, grads = local_part(*arguments)
    if size & (size - 1) or size < 8:
        grads = lax.psum(grads, "seq")
        summed = (jnp.zeros((2,), jnp.int32), grads[0], grads[1])
    else:
        summed = all_sum(grads, size)
    return (result, grad_inputs) + tuple(unpack(*summed))


def solution(mesh):
    rows = P("seq", None)
    return jax.shard_map(
        lambda *arguments: body(mesh.shape["seq"], *arguments),
        mesh=mesh,
        in_specs=(rows, rows, rows) + (P(),) * 11,
        out_specs=(rows, rows) + (P(),) * 11,
        check_vma=False,
    )
```

```python
import jax
import jax.numpy as jnp
from jax import lax
from jax.experimental import pallas as pl
from jax.experimental.pallas import tpu as pltpu
from jax.sharding import PartitionSpec as P

HEADS = 8
LAYERS = 2
WIDTH = 128
FF = 256
LEN = 256
HALF = 128
CHUNK = 256
AHEAD = 44
QUARTER = 64
WINDOWS = ((0, 128), (0, 192), (64, 256), (128, 256))
PLACES = ((0, 128), (256, 448), (640, 832), (1024, 1152))
POWER_ROWS = 1280
FAR = -1.0e9
GELU_A = 0.7978845608028654
GELU_B = 0.044715
F32 = jnp.float32
BF16 = jnp.bfloat16

GAIN_ONE, SHIFT_ONE, GAIN_TWO, SHIFT_TWO, DOWN_BIAS, GATE = range(6)
COLUMNS = 6
EXTENDED = WIDTH + 16
S_DOWN, S_GATE = range(2)
SUMS = 2
S_LOGIT = 2
S_OUT, S_Q, S_K, S_V, S_UP_LOW, S_UP_HIGH, S_SHIFT_ONE, S_SHIFT_TWO, S_GAIN_ONE, S_GAIN_TWO = range(2, 12)
R_QKV, R_OUT, R_UP, R_DOWN, R_SMALL, ROWS = 0, 384, 512, 768, 1024, 1056


def dot(left, right):
    return lax.dot_general(left, right, (((1,), (0,)), ((), ())), preferred_element_type=F32)


def both(column):
    return jnp.concatenate([column, column], axis=1)


def fold(value):
    return value[:, :HALF] + value[:, HALF:]


def zeros(rows, lanes=LEN):
    return jnp.zeros((rows, lanes), BF16)


def ones(rows, lanes=LEN):
    return jnp.ones((rows, lanes), BF16)


def split_three(value):
    high = value.astype(BF16)
    rest = value - high.astype(F32)
    middle = rest.astype(BF16)
    low = (rest - middle.astype(F32)).astype(BF16)
    return high, middle, low


def norm_parts(value):
    average = jnp.sum(value, axis=0, keepdims=True) * (1.0 / WIDTH)
    centered = value - average
    variance = jnp.sum(centered * centered, axis=0, keepdims=True) * (1.0 / WIDTH)
    scale = lax.rsqrt(variance + 1e-05)
    return centered * scale, scale


def lane_mask(rows, which):
    row = lax.broadcasted_iota(jnp.int32, (rows, HALF), 0)
    lane = lax.broadcasted_iota(jnp.int32, (rows, HALF), 1)
    return jnp.where(which(row, lane < QUARTER), 1.0, 0.0).astype(BF16)


def turned(rows):
    return jnp.concatenate(
        [rows[:, 64:128], rows[:, :64], rows[:, 192:256], rows[:, 128:192]], axis=1
    )


def make_masks():
    low = lane_mask(16, lambda row, left: left)
    high = lane_mask(16, lambda row, left: ~left)
    heads = [
        lane_mask(16, lambda row, left, head=head: (row % 4 == head) & (left if head % 2 == 0 else ~left))
        for head in range(4)
    ]
    return low, high, heads


def halves_of(rows, masks):
    low, high, unused = masks
    count = rows.shape[0] // 16
    low_all = jnp.concatenate([both(low)] * count, axis=0)
    high_all = jnp.concatenate([both(high)] * count, axis=0)
    other = turned(rows)
    return ((rows * low_all, other * high_all), (other * low_all, rows * high_all))


def head_block(variants, block, group):
    lanes = slice((block // 2) * HALF, (block // 2 + 1) * HALF)
    gap = zeros(16, HALF)
    pieces = []
    for head in range(4):
        first = QUARTER * group + 16 * head
        piece = variants[block % 2][head % 2][first : first + 16, lanes]
        pieces.append(jnp.concatenate([piece, gap] if head < 2 else [gap, piece], axis=1))
    return jnp.concatenate(pieces, axis=0)


def with_extra(features, extra):
    return jnp.concatenate([features, extra], axis=0)


def spread_marks(rows, masks, block):
    low, high, unused = masks
    lanes = slice((block // 2) * HALF, (block // 2 + 1) * HALF)
    here, there = rows[:, lanes], turned(rows)[:, lanes]
    once = here * low + there * high if block % 2 == 0 else there * low + here * high
    return both(once)


def spread_rows(rows, masks, block):
    unused, unused, heads = masks
    lanes = slice((block // 2) * HALF, (block // 2 + 1) * HALF)
    here, there = rows[:, lanes], turned(rows)[:, lanes]
    if block % 2 == 1:
        here, there = there, here
    return jnp.concatenate([here * heads[0] + there * heads[1], here * heads[2] + there * heads[3]], axis=1)


def join_blocks(even, odd, head):
    left = lax.broadcasted_iota(jnp.int32, even.shape, 1) < QUARTER
    if head % 2 == 0:
        return jnp.where(left, even, pltpu.roll(odd, QUARTER, 1))
    return jnp.where(left, pltpu.roll(even, QUARTER, 1), odd)


def token_rows(rows, extra):
    return [
        jnp.concatenate([rows[QUARTER * group : QUARTER * group + QUARTER], extra], axis=0).T for group in range(2)
    ]


def skewed(units):
    running, waiting = [], list(units)
    while running or waiting:
        if waiting:
            running.append(waiting.pop(0))
        running = [unit for unit in running if next(unit, "end") != "end"]
        yield


def together(parts, late=(), wait=0):
    running, waiting, turn = [], list(parts), 0
    while running or waiting:
        if waiting:
            running.append(waiting.pop(0))
        if turn >= wait and late:
            running.append(late.pop(0))
        running = [part for part in running if next(part, "end") != "end"]
        turn += 1
    assert not late


def segment_masks(segments):
    ids = lax.broadcasted_iota(jnp.int32, (16, LEN), 0)
    same = ids == segments
    one_hot = jnp.where(same, 1.0, 0.0).astype(BF16)
    other = jnp.where(same | (ids >= 8), 0.0, FAR).astype(BF16)
    return one_hot, other


def forward_unit(block, group, keys_rows, variants, values, marks, power_ref, mixed_ref, scale_ref, results):
    first, last = WINDOWS[block]
    weights = with_extra(head_block(variants, block, group), marks[block])
    scores = dot(keys_rows[first:last], weights)
    yield
    peak = jnp.max(scores, axis=0, keepdims=True)
    powers = jnp.exp(scores - peak).astype(BF16)
    start = PLACES[block][group]
    power_ref[start : start + last - first] = powers
    yield
    rows = values[QUARTER * group : QUARTER * group + QUARTER, first:last]
    mixed = dot(jnp.concatenate([rows, ones(16, last - first)], axis=0), powers)
    yield
    scale = 1.0 / mixed[QUARTER : QUARTER + 8]
    results[block, group] = (mixed, scale)
    if block % 2 == 0:
        return
    even, even_scale = results[block - 1, group]
    lanes = slice((block // 2) * HALF, (block // 2 + 1) * HALF)
    for head in range(4):
        tile = slice((head // 2) * HALF, (head // 2 + 1) * HALF)
        rows = slice(16 * head, 16 * head + 16)
        factor = join_blocks(even_scale[:, tile], scale[:, tile], head)
        joined = join_blocks(even[rows, tile], mixed[rows, tile], head)
        place = QUARTER * group + 16 * head
        mixed_ref[place : place + 16, lanes] = joined * jnp.concatenate([factor, factor], axis=0)
        place = 8 * (4 * group + head)
        scale_ref[place : place + 8, lanes] = factor


def attention_forward(query, keys, values, segments, masks, power_ref, mixed_ref, scale_ref):
    one_hot, other = segments
    rows = token_rows(keys, other)
    variants = halves_of(query, masks)
    marks = [spread_marks(one_hot, masks, block) for block in range(4)]
    yield
    results = {}
    yield from skewed(
        forward_unit(block, group, rows[group], variants, values, marks, power_ref, mixed_ref, scale_ref, results)
        for block in (0, 1, 2, 3)
        for group in range(2)
    )


def project(layer, hidden, weights, columns):
    column = lambda which: both(columns[layer, which])
    xhat, spread_one = norm_parts(hidden)
    normed = (xhat * column(GAIN_ONE) + column(SHIFT_ONE)).astype(BF16)
    yield
    projected = dot(weights[0][layer][:, :EXTENDED], jnp.concatenate([normed, ones(16)], axis=0))
    yield
    return xhat, spread_one, normed, projected.astype(BF16)


def forward_layer(layer, hidden, projected, segments, masks, weights, columns, power_ref, mixed_ref, scale_ref):
    unused, out_t, up_t, unused = weights
    column = lambda which: both(columns[layer, which])
    query, keys, values = (projected[part * WIDTH : (part + 1) * WIDTH] for part in range(3))
    yield from attention_forward(query, keys, values, segments, masks, power_ref, mixed_ref, scale_ref)
    mixed = mixed_ref[...]
    middle = hidden + dot(out_t[layer][:, :EXTENDED], jnp.concatenate([mixed.astype(BF16), ones(16)], axis=0))
    yield
    xhat_two, spread_two = norm_parts(middle)
    normed_two = (xhat_two * column(GAIN_TWO) + column(SHIFT_TWO)).astype(BF16)
    yield
    inner = dot(up_t[layer][:, :EXTENDED], jnp.concatenate([normed_two, ones(16)], axis=0))
    yield
    gate = jax.nn.sigmoid(inner[FF : FF + 1])
    return middle, inner[:FF], mixed, xhat_two, spread_two, normed_two, gate


def gated_unit(inner, gate):
    gated = inner * gate
    return gated, 1.0 + jnp.tanh(gated * (GELU_A + (GELU_A * GELU_B) * (gated * gated)))


def feed_forward(layer, middle, inner, gate, weights, columns, gated_ref, twice_ref):
    parts = []
    for start in range(0, FF, CHUNK):
        rows = slice(start, start + CHUNK)
        gated, twice_up = gated_unit(inner[rows], gate)
        gated_ref[rows] = gated
        twice_ref[rows] = twice_up
        parts.append((gated * twice_up).astype(BF16))
        yield
    return feed_output(layer, middle, jnp.concatenate(parts, axis=0), weights, columns)


def feed_output(layer, middle, active, weights, columns):
    return middle + (dot(weights[3][layer], active) + both(columns[layer, DOWN_BIAS]))


def norm_backward(gradient, xhat, scale, gain):
    inner = gradient * gain
    first = jnp.sum(inner, axis=0, keepdims=True) * (1.0 / WIDTH)
    second = jnp.sum(inner * xhat, axis=0, keepdims=True) * (1.0 / WIDTH)
    return scale * (inner - first - xhat * second)


def backward_unit(block, values_rows, query_variants, grad_variants, keys, deltas, power_ref, results, dq_ref, turned_ref):
    first, last = WINDOWS[block]
    query_blocks = [head_block(query_variants, block, group) for group in range(2)]
    grad_blocks = [head_block(grad_variants, block, group) for group in range(2)]
    products = [
        dot(values_rows[group][first:last], with_extra(grad_blocks[group], deltas[block][group]))
        for group in range(2)
    ]
    yield
    powers, grad_scores = [], []
    for group in range(2):
        start = PLACES[block][group]
        powers.append(power_ref[start : start + last - first])
        grad_scores.append((powers[group].astype(F32) * products[group]).astype(BF16))
        yield
    mixed = [
        dot(keys[QUARTER * group : QUARTER * group + QUARTER, first:last], grad_scores[group]) for group in range(2)
    ]

    def together_rows(blocks):
        gap = zeros(QUARTER)
        low = jnp.concatenate([blocks[0], gap], axis=0)
        high = jnp.concatenate([gap, blocks[1]], axis=0)
        return jnp.concatenate([low, high], axis=1)

    grad_keys = dot(jnp.concatenate(grad_scores, axis=1), together_rows(query_blocks).T)
    flipped = []
    for group in range(2):
        turned_ref[0 + 2 * block + group, :, : last - first] = powers[group].T
        flipped.append(dot(grad_blocks[group], turned_ref[0 + 2 * block + group, :, : last - first]))
    grad_values = jnp.concatenate(flipped, axis=0)
    results[block] = (grad_keys, grad_values, mixed)
    yield
    if block % 2 == 0:
        return
    lanes = slice((block // 2) * HALF, (block // 2 + 1) * HALF)
    for group in range(2):
        even, odd = results[block - 1][2][group], mixed[group]
        for head in range(4):
            tile = slice((head // 2) * HALF, (head // 2 + 1) * HALF)
            rows = slice(16 * head, 16 * head + 16)
            place = QUARTER * group + 16 * head
            dq_ref[place : place + 16, lanes] = join_blocks(even[rows, tile], odd[rows, tile], head)


def attention_backward(query, keys, values, mixed, scale, grad_mixed, masks, power_ref, dq_ref, turned_ref):
    factors = [scale[8 * head : 8 * head + 8] for head in range(HEADS)]
    grad = (grad_mixed * jnp.concatenate([row for factor in factors for row in (factor, factor)], axis=0)).astype(BF16)
    product = grad.astype(F32) * mixed
    delta = jnp.concatenate(
        [jnp.sum(product[16 * head : 16 * head + 16], axis=0, keepdims=True) for head in range(HEADS)], axis=0
    )
    yield
    parts = [part.astype(F32) for part in split_three(-delta)]
    gap = jnp.zeros((4, LEN), F32)
    extras = [
        jnp.concatenate([part[4 * group : 4 * group + 4] for part in parts] + [gap], axis=0).astype(BF16)
        for group in range(2)
    ]
    deltas = [[spread_rows(extras[group], masks, block) for group in range(2)] for block in range(4)]
    query_variants = halves_of(query, masks)
    grad_variants = halves_of(grad, masks)
    rows = token_rows(values, ones(16))
    yield
    results = {}
    yield from skewed(
        backward_unit(block, rows, query_variants, grad_variants, keys, deltas, power_ref, results, dq_ref, turned_ref)
        for block in range(4)
    )

    def collect_lanes(which):
        parts = [results[block][which] for block in range(4)]
        gap = jnp.zeros((WIDTH, QUARTER), F32)
        first = jnp.concatenate([parts[0], parts[3]], axis=1)
        second = jnp.concatenate([parts[1], gap], axis=1)
        third = jnp.concatenate([gap, parts[2]], axis=1)
        return (first + second + third).astype(BF16)

    def collect(which):
        parts = [results[block][which] for block in range(4)]
        return jnp.concatenate(
            [
                parts[0][:64] + parts[1][:64],
                parts[0][64:] + parts[1][64:128] + parts[2][:64],
                parts[1][128:] + parts[2][64:128] + parts[3][:64],
                parts[2][128:] + parts[3][64:],
            ],
            axis=0,
        ).astype(BF16)

    return (dq_ref[...] * 0.25).astype(BF16), collect(0), collect_lanes(1).T


def backward_layer(
    layer, gradient, masks, kept, power_ref, scale_ref, units, use_active, raw, columns, totals, dq_ref, turned_ref
):
    w_qkv, w_out, w_up, w_down = raw
    normed, query, keys, values, mixed, xhat, xhat_two, normed_two, rows = kept
    spread_one, spread_two, gate = rows[0:1], rows[1:2], rows[2:3]
    qkv_total, out_total, up_total, down_total, sums = totals
    column = lambda which: both(columns[layer, which])
    branch = gradient.astype(BF16)
    sums[S_DOWN] += fold(gradient)
    grad_active = dot(w_down[layer], branch)
    yield
    actives, inners = [], []
    logit_sum = jnp.zeros((1, LEN), F32)
    for start in range(0, FF, CHUNK):
        rows = slice(start, start + CHUNK)
        gated, twice_up = units(rows)
        active = gated * twice_up
        curve = GELU_A + (3.0 * GELU_A * GELU_B) * (gated * gated)
        slope = twice_up + (active * (2.0 - twice_up)) * curve
        grad_gated = grad_active[rows] * slope
        logit_sum = logit_sum + jnp.sum(grad_gated * gated, axis=0, keepdims=True)
        actives.append(active.astype(BF16))
        inners.append((grad_gated * gate).astype(BF16))
        yield
    grad_logit = logit_sum * (1.0 - gate)
    active = jnp.concatenate(actives, axis=0)
    use_active(active)
    grad_inner = jnp.concatenate(inners, axis=0)
    grad_two = dot(w_up[layer], grad_inner) + column(GATE) * grad_logit
    down_total[...] += dot(branch, active.T)
    up_total[...] += dot(jnp.concatenate([normed_two, ones(16)], axis=0), grad_inner.T)
    sums[S_GATE] += fold(normed_two.astype(F32) * grad_logit)
    sums[S_LOGIT, 0:1] += fold(grad_logit)
    yield
    grad_middle = gradient + norm_backward(grad_two, xhat_two, spread_two, column(GAIN_TWO))
    attended = grad_middle.astype(BF16)
    yield
    grad_mixed = dot(w_out[layer], attended)
    out_total[...] += dot(jnp.concatenate([mixed.astype(BF16), ones(16)], axis=0), attended.T)
    yield
    grad_query, grad_keys, grad_values = yield from attention_backward(
        query, keys, values, mixed, scale_ref[...], grad_mixed, masks, power_ref, dq_ref, turned_ref
    )
    yield
    grad_rows = jnp.concatenate([grad_query.T, grad_keys, grad_values], axis=1)
    qkv_total[...] += dot(jnp.concatenate([normed, ones(16)], axis=0), grad_rows)
    grad_one = dot(w_qkv[layer], jnp.concatenate([grad_query, grad_keys.T, grad_values.T], axis=0))
    yield
    return grad_middle + norm_backward(grad_one, xhat, spread_one, column(GAIN_ONE))


def spread(row):
    return jnp.broadcast_to(row, (WIDTH, WIDTH)).T


def bias_lanes(row):
    parts = [part.astype(F32) for part in split_three(row)]
    return jnp.concatenate(parts + [jnp.zeros((13, WIDTH), F32)], axis=0).T.astype(BF16)


def fill_columns(layer, columns, gains, shifts, w_gate, down_bias):
    columns[layer, GAIN_ONE] = spread(gains[layer, 0:1])
    columns[layer, GAIN_TWO] = spread(gains[layer, 1:2])
    columns[layer, SHIFT_ONE] = spread(shifts[layer, 0:1])
    columns[layer, SHIFT_TWO] = spread(shifts[layer, 1:2])
    columns[layer, DOWN_BIAS] = spread(down_bias[layer : layer + 1])
    columns[layer, GATE] = spread(w_gate[layer : layer + 1].astype(F32))


def clear_totals(totals):
    for ref in totals:
        ref[...] = jnp.zeros_like(ref)


def through(weights, row):
    parts = jnp.concatenate(split_three(row), axis=0)
    return jnp.sum(lax.dot_general(parts, weights, (((1,), (1,)), ((), ())), preferred_element_type=F32), axis=0, keepdims=True)


def across(value):
    parts = [value[:, start : start + WIDTH] for start in range(0, value.shape[1], WIDTH)]
    total = parts[0]
    for part in parts[1:]:
        total = total + part
    return jnp.sum(total.T, axis=0, keepdims=True)


def write_totals(totals, grads_ref, w_qkv, w_gate, w_up, gains, shifts):
    qkv_total, out_total, up_total, down_total, sums = totals
    for part in range(3):
        rows = slice(R_QKV + part * WIDTH, R_QKV + (part + 1) * WIDTH)
        grads_ref[rows] = qkv_total[:WIDTH, part * WIDTH : (part + 1) * WIDTH]
    grads_ref[R_OUT : R_OUT + WIDTH] = out_total[:WIDTH]
    for part in range(2):
        lanes = slice(part * WIDTH, (part + 1) * WIDTH)
        grads_ref[R_UP + part * WIDTH : R_UP + (part + 1) * WIDTH] = up_total[:WIDTH, lanes]
        grads_ref[R_DOWN + part * WIDTH : R_DOWN + (part + 1) * WIDTH] = down_total[:, lanes].T * 0.5
    rows = [jnp.sum(sums[which].T, axis=0, keepdims=True) for which in range(SUMS)]
    rows.append(out_total[WIDTH : WIDTH + 1])
    rows.extend(qkv_total[WIDTH : WIDTH + 1, part * WIDTH : (part + 1) * WIDTH] for part in range(3))
    rows.extend(up_total[WIDTH : WIDTH + 1, part * WIDTH : (part + 1) * WIDTH] for part in range(2))
    rows.append(through(w_qkv, qkv_total[WIDTH : WIDTH + 1]))
    logit = jnp.sum(sums[S_LOGIT, 0:1], axis=1, keepdims=True)
    rows.append(through(w_up, up_total[WIDTH : WIDTH + 1]) + logit * w_gate.astype(F32))
    moments = (
        across(qkv_total[:WIDTH] * w_qkv.astype(F32)),
        across(up_total[:WIDTH] * w_up.astype(F32)) + rows[S_GATE] * w_gate.astype(F32),
    )
    for which, moment in enumerate(moments):
        norm = slice(which, which + 1)
        rows.append((moment - shifts[norm] * rows[S_SHIFT_ONE + which]) / gains[norm])
    rows.append(jnp.zeros((ROWS - R_SMALL - len(rows), WIDTH), F32))
    grads_ref[R_SMALL:ROWS] = jnp.concatenate(rows, axis=0)


def kernel(
    per_step, steps,
    x_ref, x_next_ref, seg_ref, cot_ref, gains, shifts, w_qkv, qv_bias, w_out, out_bias, w_gate, w_up, up_bias, w_down, down_bias,
    result_ref, grad_inputs_ref, grads_ref,
    columns, qkv_t, out_t, up_t, down_t, half_down, mixed_scratch, dq_ref, turned_ref, power_last, scale_last,
    grad_kept, normed_kept, qkv_kept, mixed_kept, scale_kept, xhat_kept, xhat_two_kept, normed_two_kept, rows_kept,
    power_kept, gated_kept, twice_kept, *totals,
):
    step = pl.program_id(0)
    totals_zero, totals_one = totals[: len(totals) // 2], totals[len(totals) // 2 :]

    @pl.when(step == 0)
    def start():
        clear_totals(totals)
        for layer in range(LAYERS):
            fill_columns(layer, columns, gains, shifts, w_gate, down_bias)
            for ref in (qkv_t, out_t, up_t):
                ref[layer, :, WIDTH:] = zeros(ref.shape[1], WIDTH)
            qkv_t[layer, :WIDTH, :WIDTH] = (w_qkv[layer][:, :WIDTH] * jnp.asarray(0.25, BF16)).T
            qkv_t[layer, WIDTH:, :WIDTH] = w_qkv[layer][:, WIDTH:].T
            biases = qv_bias[layer : layer + 1]
            qkv_t[layer, :WIDTH, WIDTH:EXTENDED] = bias_lanes(biases[:, :WIDTH] * 0.25)
            qkv_t[layer, 2 * WIDTH :, WIDTH:EXTENDED] = bias_lanes(biases[:, WIDTH:])
            out_t[layer, :, :WIDTH] = w_out[layer].T
            out_t[layer, :, WIDTH:EXTENDED] = bias_lanes(out_bias[layer : layer + 1])
            up_t[layer, :FF, :WIDTH] = w_up[layer].T
            up_t[layer, FF:, :WIDTH] = jnp.concatenate(
                [w_gate[layer : layer + 1].astype(F32), jnp.zeros((15, WIDTH), F32)], axis=0
            ).astype(BF16)
            biases = up_bias[layer : layer + 1]
            up_t[layer, :WIDTH, WIDTH:EXTENDED] = bias_lanes(biases[:, :WIDTH])
            up_t[layer, WIDTH:FF, WIDTH:EXTENDED] = bias_lanes(biases[:, WIDTH:])
            half_down[layer] = w_down[layer] * jnp.asarray(0.5, BF16)
            down_t[layer] = half_down[layer].T

    masks = make_masks()
    weights = (qkv_t, out_t, up_t, down_t)
    raw = (w_qkv, w_out, w_up, half_down)

    def ahead(item, ref, group):
        place = group * per_step + item
        hidden = ref[item * LEN : (item + 1) * LEN].astype(F32).T
        xhat, spread_one, normed, projected = yield from project(0, hidden, weights, columns)
        xhat_kept[place] = xhat
        rows_kept[place, 0:1] = spread_one
        normed_kept[place] = normed
        qkv_kept[place] = projected

    def upward(item):
        tokens = slice(item * LEN, (item + 1) * LEN)
        place = step * per_step + item
        segments = segment_masks(seg_ref[pl.ds(place, 1)])
        hidden = x_ref[tokens].astype(F32).T
        middle, inner, mixed, xhat_two, spread_two, normed_two, gate = yield from forward_layer(
            0, hidden, qkv_kept[place], segments, masks, weights, columns, power_kept.at[place], mixed_scratch.at[item],
            scale_kept.at[place],
        )
        mixed_kept[place] = mixed
        xhat_two_kept[place] = xhat_two
        normed_two_kept[place] = normed_two
        rows_kept[place, 1:2] = spread_two
        rows_kept[place, 2:3] = gate
        hidden = yield from feed_forward(
            0, middle, inner, gate, weights, columns, gated_kept.at[place], twice_kept.at[place]
        )
        xhat, spread_one, normed, projected = yield from project(1, hidden, weights, columns)
        middle, inner, mixed, xhat_two, spread_two, normed_two, gate = yield from forward_layer(
            1, hidden, projected, segments, masks, weights, columns, power_last.at[item], mixed_scratch.at[item],
            scale_last.at[item],
        )
        kept = (
            normed, projected[:WIDTH], projected[WIDTH : 2 * WIDTH], projected[2 * WIDTH :], mixed, xhat, xhat_two,
            normed_two, jnp.concatenate([spread_one, spread_two, gate], axis=0),
        )

        def last_units(rows):
            return gated_unit(inner[rows], gate)

        def write_result(active):
            result_ref[tokens] = feed_output(1, middle, active, weights, columns).T.astype(BF16)

        gradient = cot_ref[tokens].astype(F32).T
        grad_kept[place] = yield from backward_layer(
            1, gradient, masks, kept, power_last.at[item], scale_last.at[item], last_units, write_result, raw, columns,
            totals_one, dq_ref.at[item], turned_ref.at[item],
        )

    def downward(item):
        tokens = slice(item * LEN, (item + 1) * LEN)
        place = (step - steps) * per_step + item
        kept = (
            normed_kept[place], qkv_kept[place, :WIDTH], qkv_kept[place, WIDTH : 2 * WIDTH],
            qkv_kept[place, 2 * WIDTH :], mixed_kept[place], xhat_kept[place], xhat_two_kept[place],
            normed_two_kept[place], rows_kept[place],
        )
        gradient = yield from backward_layer(
            0, grad_kept[place], masks, kept, power_kept.at[place], scale_kept.at[place],
            lambda rows: (gated_kept[place, rows], twice_kept[place, rows]), lambda active: None, raw, columns,
            totals_zero, dq_ref.at[item], turned_ref.at[item],
        )
        grad_inputs_ref[tokens] = gradient.T

    @pl.when(step == 0)
    def begin():
        together([ahead(item, x_ref, 0) for item in range(per_step)])

    @pl.when(step < steps)
    def first_half():
        following = lax.rem(step + 1, steps)
        together(
            [upward(item) for item in range(per_step)],
            [ahead(item, x_next_ref, following) for item in range(per_step)],
            AHEAD,
        )

    @pl.when(step >= steps)
    def second_half():
        together([downward(item) for item in range(per_step)])

    @pl.when(step == 2 * steps - 1)
    def finish():
        for layer, part in enumerate((totals_zero, totals_one)):
            write_totals(
                part, grads_ref.at[layer], w_qkv[layer], w_gate[layer : layer + 1], w_up[layer], gains[layer],
                shifts[layer],
            )


def totals_scratch():
    return [
        pltpu.VMEM((WIDTH + 16, 3 * WIDTH), F32),
        pltpu.VMEM((WIDTH + 16, WIDTH), F32),
        pltpu.VMEM((WIDTH + 16, FF), F32),
        pltpu.VMEM((WIDTH, FF), F32),
        pltpu.VMEM((SUMS + 1, WIDTH, WIDTH), F32),
    ]


def local_part(inputs, segment_ids, cotangent, *parameters, per_step=4):
    seqs = segment_ids.shape[0]
    per_step = min(per_step, seqs)
    steps = seqs // per_step
    rows = (per_step * LEN, WIDTH)

    def whole(array):
        zero = (0,) * array.ndim
        return pl.BlockSpec(array.shape, lambda i: zero)

    def kept(rows, dtype, count=seqs):
        return pltpu.VMEM((count, rows, LEN), dtype)

    return pl.pallas_call(
        lambda *refs: kernel(per_step, steps, *refs),
        grid=(2 * steps,),
        in_specs=[
            pl.BlockSpec(rows, lambda i: (jnp.minimum(i, steps - 1), 0)),
            pl.BlockSpec(rows, lambda i: (jnp.minimum(i + 1, steps) % steps, 0)),
            whole(segment_ids),
            pl.BlockSpec(rows, lambda i: (jnp.minimum(i, steps - 1), 0)),
        ]
        + [whole(entry) for entry in parameters],
        out_specs=[
            pl.BlockSpec(rows, lambda i: (jnp.minimum(i, steps - 1), 0)),
            pl.BlockSpec(rows, lambda i: (jnp.maximum(i - steps, 0), 0)),
            pl.BlockSpec(memory_space=pltpu.VMEM),
        ],
        out_shape=[
            jax.ShapeDtypeStruct(inputs.shape, BF16),
            jax.ShapeDtypeStruct(inputs.shape, F32),
            pltpu.VMEM((LAYERS, ROWS, WIDTH), F32),
        ],
        scratch_shapes=[
            pltpu.VMEM((LAYERS, COLUMNS, WIDTH, WIDTH), F32),
            pltpu.VMEM((LAYERS, 3 * WIDTH, 2 * WIDTH), BF16),
            pltpu.VMEM((LAYERS, WIDTH, 2 * WIDTH), BF16),
            pltpu.VMEM((LAYERS, FF + 16, 2 * WIDTH), BF16),
            pltpu.VMEM((LAYERS, WIDTH, FF), BF16),
            pltpu.VMEM((LAYERS, FF, WIDTH), BF16),
            kept(WIDTH, F32, per_step),
            kept(WIDTH, F32, per_step),
            pltpu.VMEM((per_step, 8, LEN, LEN), BF16),
            kept(POWER_ROWS, BF16, per_step),
            kept(8 * HEADS, F32, per_step),
            kept(WIDTH, F32),
            kept(WIDTH, BF16),
            kept(3 * WIDTH, BF16),
            kept(WIDTH, F32),
            kept(8 * HEADS, F32),
            kept(WIDTH, F32),
            kept(WIDTH, F32),
            kept(WIDTH, BF16),
            kept(8, F32),
            kept(POWER_ROWS, BF16),
            kept(FF, F32),
            kept(FF, F32),
        ]
        + totals_scratch()
        + totals_scratch(),
        compiler_params=pltpu.CompilerParams(vmem_limit_bytes=60 * 1024 * 1024),
        name="layers",
    )(inputs, inputs, segment_ids, cotangent, *parameters)


def unpack_kernel(
    where_ref, near_ref, far_ref,
    gains_ref, shifts_ref, qkv_ref, qv_bias_ref, out_ref, out_bias_ref, gate_ref, up_ref, up_bias_ref, down_ref,
    down_bias_ref,
    grads,
):
    core, part = where_ref[0], where_ref[1]
    quarter = ROWS // 4
    for mask in range(4):
        place = pl.ds(pl.multiple_of((part ^ mask) * quarter, 8), quarter)
        rows = slice(mask * quarter, (mask + 1) * quarter)
        grads[core, place] = near_ref[rows]
        grads[1 - core, place] = far_ref[rows]
    for layer in range(LAYERS):
        for part in range(3):
            lanes = slice(part * WIDTH, (part + 1) * WIDTH)
            qkv_ref[layer, :, lanes] = grads[layer, R_QKV + part * WIDTH : R_QKV + (part + 1) * WIDTH]
        out_ref[layer] = grads[layer, R_OUT : R_OUT + WIDTH]
        for part in range(2):
            lanes = slice(part * WIDTH, (part + 1) * WIDTH)
            up_ref[layer, :, lanes] = grads[layer, R_UP + part * WIDTH : R_UP + (part + 1) * WIDTH]
        down_ref[layer] = grads[layer, R_DOWN : R_DOWN + FF]
        one = slice(layer, layer + 1)

        def row(which):
            return grads[layer, R_SMALL + which : R_SMALL + which + 1]

        gains_ref[layer, 0:1], gains_ref[layer, 1:2] = row(S_GAIN_ONE), row(S_GAIN_TWO)
        shifts_ref[layer, 0:1], shifts_ref[layer, 1:2] = row(S_SHIFT_ONE), row(S_SHIFT_TWO)
        qv_bias_ref[one, :WIDTH], qv_bias_ref[one, WIDTH:] = row(S_Q), row(S_V)
        out_bias_ref[one], gate_ref[one], down_bias_ref[one] = row(S_OUT), row(S_GATE), row(S_DOWN)
        up_bias_ref[one, :WIDTH], up_bias_ref[one, WIDTH:] = row(S_UP_LOW), row(S_UP_HIGH)


def unpack(where, near, far):
    shapes = [
        (LAYERS, 2, WIDTH), (LAYERS, 2, WIDTH), (LAYERS, WIDTH, 3 * WIDTH), (LAYERS, 2 * WIDTH), (LAYERS, WIDTH, WIDTH),
        (LAYERS, WIDTH), (LAYERS, WIDTH), (LAYERS, WIDTH, FF), (LAYERS, FF), (LAYERS, FF, WIDTH), (LAYERS, WIDTH),
    ]
    return pl.pallas_call(
        unpack_kernel,
        in_specs=[pl.BlockSpec(memory_space=pltpu.SMEM), pl.BlockSpec(), pl.BlockSpec()],
        out_shape=[jax.ShapeDtypeStruct(shape, F32) for shape in shapes],
        scratch_shapes=[pltpu.VMEM((LAYERS, ROWS, WIDTH), F32)],
        compiler_params=pltpu.CompilerParams(vmem_limit_bytes=16 * 1024 * 1024),
        name="unpack",
    )(where, near, far)


def all_sum(grads, size):
    me = lax.axis_index("seq")
    bits = size.bit_length() - 1
    core, part = me & 1, (me >> 1) & 3

    def swap(value, mask):
        return lax.ppermute(value, "seq", [(i, i ^ mask) for i in range(size)])

    def pick(value, index):
        return lax.dynamic_index_in_dim(value, index, 0, keepdims=False)

    layer = pick(grads, core) + swap(pick(grads, 1 - core), 1)
    quarters = layer.reshape(4, ROWS // 4, WIDTH)
    others = [swap(pick(quarters, part ^ mask), 2 * mask) for mask in (1, 2, 3)]
    mine = pick(quarters, part) + others[0] + others[1] + others[2]
    for bit in range(3, bits):
        mine = mine + swap(mine, 1 << bit)
    near = jnp.concatenate([mine] + [swap(mine, 2 * mask) for mask in (1, 2, 3)], axis=0)
    return jnp.stack([core, part]).astype(jnp.int32), near, swap(near, 1)


def body(size, *arguments):
    result, grad_inputs, grads = local_part(*arguments)
    if size & (size - 1) or size < 8:
        grads = lax.psum(grads, "seq")
        summed = (jnp.zeros((2,), jnp.int32), grads[0], grads[1])
    else:
        summed = all_sum(grads, size)
    return (result, grad_inputs) + tuple(unpack(*summed))


def solution(mesh):
    rows = P("seq", None)
    return jax.shard_map(
        lambda *arguments: body(mesh.shape["seq"], *arguments),
        mesh=mesh,
        in_specs=(rows, rows, rows) + (P(),) * 11,
        out_specs=(rows, rows) + (P(),) * 11,
        check_vma=False,
    )
```

```python
import jax
import jax.numpy as jnp
from jax import lax
from jax.experimental import pallas as pl
from jax.experimental.pallas import tpu as pltpu
from jax.sharding import PartitionSpec as P

HEADS = 8
LAYERS = 2
WIDTH = 128
FF = 256
LEN = 256
HALF = 128
CHUNK = 256
AHEAD = 44
QUARTER = 64
WINDOWS = ((0, 128), (0, 192), (64, 256), (128, 256))
PLACES = ((0, 128), (256, 448), (640, 832), (1024, 1152))
POWER_ROWS = 1280
FAR = -1.0e9
GELU_A = 0.7978845608028654
GELU_B = 0.044715
F32 = jnp.float32
BF16 = jnp.bfloat16

GAIN_ONE, SHIFT_ONE, GAIN_TWO, SHIFT_TWO, DOWN_BIAS, GATE = range(6)
COLUMNS = 6
EXTENDED = WIDTH + 16
S_DOWN, S_GATE = range(2)
SUMS = 2
S_LOGIT = 2
S_OUT, S_Q, S_K, S_V, S_UP_LOW, S_UP_HIGH, S_SHIFT_ONE, S_SHIFT_TWO, S_GAIN_ONE, S_GAIN_TWO = range(2, 12)
R_QKV, R_OUT, R_UP, R_DOWN, R_SMALL, ROWS = 0, 384, 512, 768, 1024, 1056


def dot(left, right):
    return lax.dot_general(left, right, (((1,), (0,)), ((), ())), preferred_element_type=F32)


def both(column):
    return jnp.concatenate([column, column], axis=1)


def fold(value):
    return value[:, :HALF] + value[:, HALF:]


def zeros(rows, lanes=LEN):
    return jnp.zeros((rows, lanes), BF16)


def ones(rows, lanes=LEN):
    return jnp.ones((rows, lanes), BF16)


def split_three(value):
    high = value.astype(BF16)
    rest = value - high.astype(F32)
    middle = rest.astype(BF16)
    low = (rest - middle.astype(F32)).astype(BF16)
    return high, middle, low


def norm_parts(value):
    average = jnp.sum(value, axis=0, keepdims=True) * (1.0 / WIDTH)
    centered = value - average
    variance = jnp.sum(centered * centered, axis=0, keepdims=True) * (1.0 / WIDTH)
    scale = lax.rsqrt(variance + 1e-05)
    return centered * scale, scale


def lane_mask(rows, which):
    row = lax.broadcasted_iota(jnp.int32, (rows, HALF), 0)
    lane = lax.broadcasted_iota(jnp.int32, (rows, HALF), 1)
    return jnp.where(which(row, lane < QUARTER), 1.0, 0.0).astype(BF16)


def turned(rows):
    return jnp.concatenate(
        [rows[:, 64:128], rows[:, :64], rows[:, 192:256], rows[:, 128:192]], axis=1
    )


def make_masks():
    low = lane_mask(16, lambda row, left: left)
    high = lane_mask(16, lambda row, left: ~left)
    heads = [
        lane_mask(16, lambda row, left, head=head: (row % 4 == head) & (left if head % 2 == 0 else ~left))
        for head in range(4)
    ]
    return low, high, heads


def halves_of(rows, masks):
    low, high, unused = masks
    count = rows.shape[0] // 16
    low_all = jnp.concatenate([both(low)] * count, axis=0)
    high_all = jnp.concatenate([both(high)] * count, axis=0)
    other = turned(rows)
    return ((rows * low_all, other * high_all), (other * low_all, rows * high_all))


def head_block(variants, block, group):
    lanes = slice((block // 2) * HALF, (block // 2 + 1) * HALF)
    gap = zeros(16, HALF)
    pieces = []
    for head in range(4):
        first = QUARTER * group + 16 * head
        piece = variants[block % 2][head % 2][first : first + 16, lanes]
        pieces.append(jnp.concatenate([piece, gap] if head < 2 else [gap, piece], axis=1))
    return jnp.concatenate(pieces, axis=0)


def with_extra(features, extra):
    return jnp.concatenate([features, extra], axis=0)


def spread_marks(rows, masks, block):
    low, high, unused = masks
    lanes = slice((block // 2) * HALF, (block // 2 + 1) * HALF)
    here, there = rows[:, lanes], turned(rows)[:, lanes]
    once = here * low + there * high if block % 2 == 0 else there * low + here * high
    return both(once)


def spread_rows(rows, masks, block):
    unused, unused, heads = masks
    lanes = slice((block // 2) * HALF, (block // 2 + 1) * HALF)
    here, there = rows[:, lanes], turned(rows)[:, lanes]
    if block % 2 == 1:
        here, there = there, here
    return jnp.concatenate([here * heads[0] + there * heads[1], here * heads[2] + there * heads[3]], axis=1)


def join_blocks(even, odd, head):
    left = lax.broadcasted_iota(jnp.int32, even.shape, 1) < QUARTER
    if head % 2 == 0:
        return jnp.where(left, even, pltpu.roll(odd, QUARTER, 1))
    return jnp.where(left, pltpu.roll(even, QUARTER, 1), odd)


def token_rows(rows, extra):
    return [
        jnp.concatenate([rows[QUARTER * group : QUARTER * group + QUARTER], extra], axis=0).T for group in range(2)
    ]


def skewed(units):
    running, waiting = [], list(units)
    while running or waiting:
        if waiting:
            running.append(waiting.pop(0))
        running = [unit for unit in running if next(unit, "end") != "end"]
        yield


def together(parts, late=(), wait=0):
    running, waiting, turn = [], list(parts), 0
    while running or waiting:
        if waiting:
            running.append(waiting.pop(0))
        if turn >= wait and late:
            running.append(late.pop(0))
        running = [part for part in running if next(part, "end") != "end"]
        turn += 1
    assert not late


def segment_masks(segments):
    ids = lax.broadcasted_iota(jnp.int32, (16, LEN), 0)
    same = ids == segments
    one_hot = jnp.where(same, 1.0, 0.0).astype(BF16)
    other = jnp.where(same | (ids >= 8), 0.0, FAR).astype(BF16)
    return one_hot, other


def forward_unit(block, group, keys_rows, variants, values, marks, power_ref, mixed_ref, scale_ref, results):
    first, last = WINDOWS[block]
    weights = with_extra(head_block(variants, block, group), marks[block])
    scores = dot(keys_rows[first:last], weights)
    yield
    peak = jnp.max(scores, axis=0, keepdims=True)
    powers = jnp.exp(scores - peak).astype(BF16)
    start = PLACES[block][group]
    power_ref[start : start + last - first] = powers
    yield
    rows = values[QUARTER * group : QUARTER * group + QUARTER, first:last]
    mixed = dot(jnp.concatenate([rows, ones(16, last - first)], axis=0), powers)
    yield
    scale = 1.0 / mixed[QUARTER : QUARTER + 8]
    results[block, group] = (mixed, scale)
    if block % 2 == 0:
        return
    even, even_scale = results[block - 1, group]
    lanes = slice((block // 2) * HALF, (block // 2 + 1) * HALF)
    for head in range(4):
        tile = slice((head // 2) * HALF, (head // 2 + 1) * HALF)
        rows = slice(16 * head, 16 * head + 16)
        factor = join_blocks(even_scale[:, tile], scale[:, tile], head)
        joined = join_blocks(even[rows, tile], mixed[rows, tile], head)
        place = QUARTER * group + 16 * head
        mixed_ref[place : place + 16, lanes] = joined * jnp.concatenate([factor, factor], axis=0)
        place = 8 * (4 * group + head)
        scale_ref[place : place + 8, lanes] = factor


def attention_forward(query, keys, values, segments, masks, power_ref, mixed_ref, scale_ref):
    one_hot, other = segments
    rows = token_rows(keys, other)
    variants = halves_of(query, masks)
    marks = [spread_marks(one_hot, masks, block) for block in range(4)]
    yield
    results = {}
    yield from skewed(
        forward_unit(block, group, rows[group], variants, values, marks, power_ref, mixed_ref, scale_ref, results)
        for block in (0, 1, 2, 3)
        for group in range(2)
    )


def project(layer, hidden, weights, columns):
    column = lambda which: both(columns[layer, which])
    xhat, spread_one = norm_parts(hidden)
    normed = (xhat * column(GAIN_ONE) + column(SHIFT_ONE)).astype(BF16)
    yield
    projected = dot(weights[0][layer][:, :EXTENDED], jnp.concatenate([normed, ones(16)], axis=0))
    yield
    return xhat, spread_one, normed, projected.astype(BF16)


def forward_layer(layer, hidden, projected, segments, masks, weights, columns, power_ref, mixed_ref, scale_ref):
    unused, out_t, up_t, unused = weights
    column = lambda which: both(columns[layer, which])
    query, keys, values = (projected[part * WIDTH : (part + 1) * WIDTH] for part in range(3))
    yield from attention_forward(query, keys, values, segments, masks, power_ref, mixed_ref, scale_ref)
    mixed = mixed_ref[...]
    middle = hidden + dot(out_t[layer][:, :EXTENDED], jnp.concatenate([mixed.astype(BF16), ones(16)], axis=0))
    yield
    xhat_two, spread_two = norm_parts(middle)
    normed_two = (xhat_two * column(GAIN_TWO) + column(SHIFT_TWO)).astype(BF16)
    yield
    inner = dot(up_t[layer][:, :EXTENDED], jnp.concatenate([normed_two, ones(16)], axis=0))
    yield
    gate = jax.nn.sigmoid(inner[FF : FF + 1])
    return middle, inner[:FF], mixed, xhat_two, spread_two, normed_two, gate


def gated_unit(inner, gate):
    gated = inner * gate
    return gated, 1.0 + jnp.tanh(gated * (GELU_A + (GELU_A * GELU_B) * (gated * gated)))


def feed_forward(layer, middle, inner, gate, weights, columns, gated_ref, twice_ref):
    parts = []
    for start in range(0, FF, CHUNK):
        rows = slice(start, start + CHUNK)
        gated, twice_up = gated_unit(inner[rows], gate)
        gated_ref[rows] = gated
        twice_ref[rows] = twice_up
        parts.append((gated * twice_up).astype(BF16))
        yield
    return feed_output(layer, middle, jnp.concatenate(parts, axis=0), weights, columns)


def feed_output(layer, middle, active, weights, columns):
    return middle + (dot(weights[3][layer], active) + both(columns[layer, DOWN_BIAS]))


def norm_backward(gradient, xhat, scale, gain):
    inner = gradient * gain
    first = jnp.sum(inner, axis=0, keepdims=True) * (1.0 / WIDTH)
    second = jnp.sum(inner * xhat, axis=0, keepdims=True) * (1.0 / WIDTH)
    return scale * (inner - first - xhat * second)


def backward_unit(block, values_rows, query_variants, grad_variants, keys, deltas, power_ref, results, dq_ref, turned_ref):
    first, last = WINDOWS[block]
    query_blocks = [head_block(query_variants, block, group) for group in range(2)]
    grad_blocks = [head_block(grad_variants, block, group) for group in range(2)]
    products = [
        dot(values_rows[group][first:last], with_extra(grad_blocks[group], deltas[block][group]))
        for group in range(2)
    ]
    yield
    powers, grad_scores = [], []
    for group in range(2):
        start = PLACES[block][group]
        powers.append(power_ref[start : start + last - first])
        grad_scores.append((powers[group].astype(F32) * products[group]).astype(BF16))
        yield
    mixed = [
        dot(keys[QUARTER * group : QUARTER * group + QUARTER, first:last], grad_scores[group]) for group in range(2)
    ]

    def together_rows(blocks):
        gap = zeros(QUARTER)
        low = jnp.concatenate([blocks[0], gap], axis=0)
        high = jnp.concatenate([gap, blocks[1]], axis=0)
        return jnp.concatenate([low, high], axis=1)

    grad_keys = dot(jnp.concatenate(grad_scores, axis=1), together_rows(query_blocks).T)
    flipped = []
    for group in range(2):
        turned_ref[0 + 2 * block + group, :, : last - first] = powers[group].T
        flipped.append(dot(grad_blocks[group], turned_ref[0 + 2 * block + group, :, : last - first]))
    grad_values = jnp.concatenate(flipped, axis=0)
    results[block] = (grad_keys, grad_values, mixed)
    yield
    if block % 2 == 0:
        return
    lanes = slice((block // 2) * HALF, (block // 2 + 1) * HALF)
    for group in range(2):
        even, odd = results[block - 1][2][group], mixed[group]
        for head in range(4):
            tile = slice((head // 2) * HALF, (head // 2 + 1) * HALF)
            rows = slice(16 * head, 16 * head + 16)
            place = QUARTER * group + 16 * head
            dq_ref[place : place + 16, lanes] = join_blocks(even[rows, tile], odd[rows, tile], head)


def attention_backward(query, keys, values, mixed, scale, grad_mixed, masks, power_ref, dq_ref, turned_ref):
    factors = [scale[8 * head : 8 * head + 8] for head in range(HEADS)]
    grad = (grad_mixed * jnp.concatenate([row for factor in factors for row in (factor, factor)], axis=0)).astype(BF16)
    product = grad.astype(F32) * mixed
    delta = jnp.concatenate(
        [jnp.sum(product[16 * head : 16 * head + 16], axis=0, keepdims=True) for head in range(HEADS)], axis=0
    )
    yield
    parts = [part.astype(F32) for part in split_three(-delta)]
    gap = jnp.zeros((4, LEN), F32)
    extras = [
        jnp.concatenate([part[4 * group : 4 * group + 4] for part in parts] + [gap], axis=0).astype(BF16)
        for group in range(2)
    ]
    deltas = [[spread_rows(extras[group], masks, block) for group in range(2)] for block in range(4)]
    query_variants = halves_of(query, masks)
    grad_variants = halves_of(grad, masks)
    rows = token_rows(values, ones(16))
    yield
    results = {}
    yield from skewed(
        backward_unit(block, rows, query_variants, grad_variants, keys, deltas, power_ref, results, dq_ref, turned_ref)
        for block in range(4)
    )

    def collect_lanes(which):
        parts = [results[block][which] for block in range(4)]
        gap = jnp.zeros((WIDTH, QUARTER), F32)
        first = jnp.concatenate([parts[0], parts[3]], axis=1)
        second = jnp.concatenate([parts[1], gap], axis=1)
        third = jnp.concatenate([gap, parts[2]], axis=1)
        return (first + second + third).astype(BF16)

    def collect(which):
        parts = [results[block][which] for block in range(4)]
        return jnp.concatenate(
            [
                parts[0][:64] + parts[1][:64],
                parts[0][64:] + parts[1][64:128] + parts[2][:64],
                parts[1][128:] + parts[2][64:128] + parts[3][:64],
                parts[2][128:] + parts[3][64:],
            ],
            axis=0,
        ).astype(BF16)

    return (dq_ref[...] * 0.25).astype(BF16), collect(0), collect_lanes(1).T


def backward_layer(
    layer, gradient, masks, kept, power_ref, scale_ref, units, use_active, raw, columns, totals, dq_ref, turned_ref
):
    w_qkv, w_out, w_up, w_down = raw
    normed, query, keys, values, mixed, xhat, xhat_two, normed_two, rows = kept
    spread_one, spread_two, gate = rows[0:1], rows[1:2], rows[2:3]
    qkv_total, out_total, up_total, down_total, sums = totals
    column = lambda which: both(columns[layer, which])
    branch = gradient.astype(BF16)
    sums[S_DOWN] += fold(gradient)
    grad_active = dot(w_down[layer], branch)
    yield
    actives, inners = [], []
    logit_sum = jnp.zeros((1, LEN), F32)
    for start in range(0, FF, CHUNK):
        rows = slice(start, start + CHUNK)
        gated, twice_up = units(rows)
        active = gated * twice_up
        curve = GELU_A + (3.0 * GELU_A * GELU_B) * (gated * gated)
        slope = twice_up + (active * (2.0 - twice_up)) * curve
        grad_gated = grad_active[rows] * slope
        logit_sum = logit_sum + jnp.sum(grad_gated * gated, axis=0, keepdims=True)
        actives.append(active.astype(BF16))
        inners.append((grad_gated * gate).astype(BF16))
        yield
    grad_logit = logit_sum * (1.0 - gate)
    active = jnp.concatenate(actives, axis=0)
    use_active(active)
    grad_inner = jnp.concatenate(inners, axis=0)
    grad_two = dot(w_up[layer], grad_inner) + column(GATE) * grad_logit
    down_total[...] += dot(branch, active.T)
    up_total[...] += dot(jnp.concatenate([normed_two, ones(16)], axis=0), grad_inner.T)
    sums[S_GATE] += fold(normed_two.astype(F32) * grad_logit)
    sums[S_LOGIT, 0:1] += fold(grad_logit)
    yield
    grad_middle = gradient + norm_backward(grad_two, xhat_two, spread_two, column(GAIN_TWO))
    attended = grad_middle.astype(BF16)
    yield
    grad_mixed = dot(w_out[layer], attended)
    out_total[...] += dot(jnp.concatenate([mixed.astype(BF16), ones(16)], axis=0), attended.T)
    yield
    grad_query, grad_keys, grad_values = yield from attention_backward(
        query, keys, values, mixed, scale_ref[...], grad_mixed, masks, power_ref, dq_ref, turned_ref
    )
    yield
    grad_rows = jnp.concatenate([grad_query.T, grad_keys, grad_values], axis=1)
    qkv_total[...] += dot(jnp.concatenate([normed, ones(16)], axis=0), grad_rows)
    grad_one = dot(w_qkv[layer], jnp.concatenate([grad_query, grad_keys.T, grad_values.T], axis=0))
    yield
    return grad_middle + norm_backward(grad_one, xhat, spread_one, column(GAIN_ONE))


def spread(row):
    return jnp.broadcast_to(row, (WIDTH, WIDTH)).T


def bias_lanes(row):
    parts = [part.astype(F32) for part in split_three(row)]
    return jnp.concatenate(parts + [jnp.zeros((13, WIDTH), F32)], axis=0).T.astype(BF16)


def fill_columns(layer, columns, gains, shifts, w_gate, down_bias):
    columns[layer, GAIN_ONE] = spread(gains[layer, 0:1])
    columns[layer, GAIN_TWO] = spread(gains[layer, 1:2])
    columns[layer, SHIFT_ONE] = spread(shifts[layer, 0:1])
    columns[layer, SHIFT_TWO] = spread(shifts[layer, 1:2])
    columns[layer, DOWN_BIAS] = spread(down_bias[layer : layer + 1])
    columns[layer, GATE] = spread(w_gate[layer : layer + 1].astype(F32))


def clear_totals(totals):
    for ref in totals:
        ref[...] = jnp.zeros_like(ref)


def through(weights, row):
    parts = jnp.concatenate(split_three(row), axis=0)
    return jnp.sum(lax.dot_general(parts, weights, (((1,), (1,)), ((), ())), preferred_element_type=F32), axis=0, keepdims=True)


def across(value):
    parts = [value[:, start : start + WIDTH] for start in range(0, value.shape[1], WIDTH)]
    total = parts[0]
    for part in parts[1:]:
        total = total + part
    return jnp.sum(total.T, axis=0, keepdims=True)


def write_totals(totals, grads_ref, w_qkv, w_gate, w_up, gains, shifts):
    qkv_total, out_total, up_total, down_total, sums = totals
    for part in range(3):
        rows = slice(R_QKV + part * WIDTH, R_QKV + (part + 1) * WIDTH)
        grads_ref[rows] = qkv_total[:WIDTH, part * WIDTH : (part + 1) * WIDTH]
    grads_ref[R_OUT : R_OUT + WIDTH] = out_total[:WIDTH]
    for part in range(2):
        lanes = slice(part * WIDTH, (part + 1) * WIDTH)
        grads_ref[R_UP + part * WIDTH : R_UP + (part + 1) * WIDTH] = up_total[:WIDTH, lanes]
        grads_ref[R_DOWN + part * WIDTH : R_DOWN + (part + 1) * WIDTH] = down_total[:, lanes].T * 0.5
    rows = [jnp.sum(sums[which].T, axis=0, keepdims=True) for which in range(SUMS)]
    rows.append(out_total[WIDTH : WIDTH + 1])
    rows.extend(qkv_total[WIDTH : WIDTH + 1, part * WIDTH : (part + 1) * WIDTH] for part in range(3))
    rows.extend(up_total[WIDTH : WIDTH + 1, part * WIDTH : (part + 1) * WIDTH] for part in range(2))
    rows.append(through(w_qkv, qkv_total[WIDTH : WIDTH + 1]))
    logit = jnp.sum(sums[S_LOGIT, 0:1], axis=1, keepdims=True)
    rows.append(through(w_up, up_total[WIDTH : WIDTH + 1]) + logit * w_gate.astype(F32))
    moments = (
        across(qkv_total[:WIDTH] * w_qkv.astype(F32)),
        across(up_total[:WIDTH] * w_up.astype(F32)) + rows[S_GATE] * w_gate.astype(F32),
    )
    for which, moment in enumerate(moments):
        norm = slice(which, which + 1)
        rows.append((moment - shifts[norm] * rows[S_SHIFT_ONE + which]) / gains[norm])
    rows.append(jnp.zeros((ROWS - R_SMALL - len(rows), WIDTH), F32))
    grads_ref[R_SMALL:ROWS] = jnp.concatenate(rows, axis=0)


def kernel(
    per_step, steps,
    x_ref, x_next_ref, seg_ref, cot_ref, gains, shifts, w_qkv, qv_bias, w_out, out_bias, w_gate, w_up, up_bias, w_down, down_bias,
    result_ref, grad_inputs_ref, grads_ref,
    columns, qkv_t, out_t, up_t, down_t, half_down, mixed_scratch, dq_ref, turned_ref, power_last, scale_last,
    grad_kept, normed_kept, qkv_kept, mixed_kept, scale_kept, xhat_kept, xhat_two_kept, normed_two_kept, rows_kept,
    power_kept, gated_kept, twice_kept, *totals,
):
    step = pl.program_id(0)
    totals_zero, totals_one = totals[: len(totals) // 2], totals[len(totals) // 2 :]

    @pl.when(step == 0)
    def start():
        clear_totals(totals)
        for layer in range(LAYERS):
            fill_columns(layer, columns, gains, shifts, w_gate, down_bias)
            for ref in (qkv_t, out_t, up_t):
                ref[layer, :, WIDTH:] = zeros(ref.shape[1], WIDTH)
            qkv_t[layer, :WIDTH, :WIDTH] = (w_qkv[layer][:, :WIDTH] * jnp.asarray(0.25, BF16)).T
            qkv_t[layer, WIDTH:, :WIDTH] = w_qkv[layer][:, WIDTH:].T
            biases = qv_bias[layer : layer + 1]
            qkv_t[layer, :WIDTH, WIDTH:EXTENDED] = bias_lanes(biases[:, :WIDTH] * 0.25)
            qkv_t[layer, 2 * WIDTH :, WIDTH:EXTENDED] = bias_lanes(biases[:, WIDTH:])
            out_t[layer, :, :WIDTH] = w_out[layer].T
            out_t[layer, :, WIDTH:EXTENDED] = bias_lanes(out_bias[layer : layer + 1])
            up_t[layer, :FF, :WIDTH] = w_up[layer].T
            up_t[layer, FF:, :WIDTH] = jnp.concatenate(
                [w_gate[layer : layer + 1].astype(F32), jnp.zeros((15, WIDTH), F32)], axis=0
            ).astype(BF16)
            biases = up_bias[layer : layer + 1]
            up_t[layer, :WIDTH, WIDTH:EXTENDED] = bias_lanes(biases[:, :WIDTH])
            up_t[layer, WIDTH:FF, WIDTH:EXTENDED] = bias_lanes(biases[:, WIDTH:])
            half_down[layer] = w_down[layer] * jnp.asarray(0.5, BF16)
            down_t[layer] = half_down[layer].T

    masks = make_masks()
    weights = (qkv_t, out_t, up_t, down_t)
    raw = (w_qkv, w_out, w_up, half_down)

    def ahead(item, ref, group):
        place = group * per_step + item
        hidden = ref[item * LEN : (item + 1) * LEN].astype(F32).T
        xhat, spread_one, normed, projected = yield from project(0, hidden, weights, columns)
        xhat_kept[place] = xhat
        rows_kept[place, 0:1] = spread_one
        normed_kept[place] = normed
        qkv_kept[place] = projected

    def upward(item):
        tokens = slice(item * LEN, (item + 1) * LEN)
        place = step * per_step + item
        segments = segment_masks(seg_ref[pl.ds(place, 1)])
        hidden = x_ref[tokens].astype(F32).T
        middle, inner, mixed, xhat_two, spread_two, normed_two, gate = yield from forward_layer(
            0, hidden, qkv_kept[place], segments, masks, weights, columns, power_kept.at[place], mixed_scratch.at[item],
            scale_kept.at[place],
        )
        mixed_kept[place] = mixed
        xhat_two_kept[place] = xhat_two
        normed_two_kept[place] = normed_two
        rows_kept[place, 1:2] = spread_two
        rows_kept[place, 2:3] = gate
        hidden = yield from feed_forward(
            0, middle, inner, gate, weights, columns, gated_kept.at[place], twice_kept.at[place]
        )
        xhat, spread_one, normed, projected = yield from project(1, hidden, weights, columns)
        middle, inner, mixed, xhat_two, spread_two, normed_two, gate = yield from forward_layer(
            1, hidden, projected, segments, masks, weights, columns, power_last.at[item], mixed_scratch.at[item],
            scale_last.at[item],
        )
        kept = (
            normed, projected[:WIDTH], projected[WIDTH : 2 * WIDTH], projected[2 * WIDTH :], mixed, xhat, xhat_two,
            normed_two, jnp.concatenate([spread_one, spread_two, gate], axis=0),
        )

        def last_units(rows):
            return gated_unit(inner[rows], gate)

        def write_result(active):
            result_ref[tokens] = feed_output(1, middle, active, weights, columns).T.astype(BF16)

        gradient = cot_ref[tokens].astype(F32).T
        grad_kept[place] = yield from backward_layer(
            1, gradient, masks, kept, power_last.at[item], scale_last.at[item], last_units, write_result, raw, columns,
            totals_one, dq_ref.at[item], turned_ref.at[item],
        )

    def downward(item):
        tokens = slice(item * LEN, (item + 1) * LEN)
        place = (step - steps) * per_step + item
        kept = (
            normed_kept[place], qkv_kept[place, :WIDTH], qkv_kept[place, WIDTH : 2 * WIDTH],
            qkv_kept[place, 2 * WIDTH :], mixed_kept[place], xhat_kept[place], xhat_two_kept[place],
            normed_two_kept[place], rows_kept[place],
        )
        gradient = yield from backward_layer(
            0, grad_kept[place], masks, kept, power_kept.at[place], scale_kept.at[place],
            lambda rows: (gated_kept[place, rows], twice_kept[place, rows]), lambda active: None, raw, columns,
            totals_zero, dq_ref.at[item], turned_ref.at[item],
        )
        grad_inputs_ref[tokens] = gradient.T

    @pl.when(step == 0)
    def begin():
        together([ahead(item, x_ref, 0) for item in range(per_step)])

    @pl.when(step < steps)
    def first_half():
        following = lax.rem(step + 1, steps)
        together(
            [upward(item) for item in range(per_step)],
            [ahead(item, x_next_ref, following) for item in range(per_step)],
            AHEAD,
        )

    @pl.when(step >= steps)
    def second_half():
        together([downward(item) for item in range(per_step)])

    @pl.when(step == 2 * steps - 1)
    def finish():
        for layer, part in enumerate((totals_zero, totals_one)):
            write_totals(
                part, grads_ref.at[layer], w_qkv[layer], w_gate[layer : layer + 1], w_up[layer], gains[layer],
                shifts[layer],
            )


def totals_scratch():
    return [
        pltpu.VMEM((WIDTH + 16, 3 * WIDTH), F32),
        pltpu.VMEM((WIDTH + 16, WIDTH), F32),
        pltpu.VMEM((WIDTH + 16, FF), F32),
        pltpu.VMEM((WIDTH, FF), F32),
        pltpu.VMEM((SUMS + 1, WIDTH, WIDTH), F32),
    ]


def local_part(inputs, segment_ids, cotangent, *parameters, per_step=4):
    seqs = segment_ids.shape[0]
    per_step = min(per_step, seqs)
    steps = seqs // per_step
    rows = (per_step * LEN, WIDTH)

    def whole(array):
        zero = (0,) * array.ndim
        return pl.BlockSpec(array.shape, lambda i: zero)

    def kept(rows, dtype, count=seqs):
        return pltpu.VMEM((count, rows, LEN), dtype)

    return pl.pallas_call(
        lambda *refs: kernel(per_step, steps, *refs),
        grid=(2 * steps,),
        in_specs=[
            pl.BlockSpec(rows, lambda i: (jnp.minimum(i, steps - 1), 0)),
            pl.BlockSpec(rows, lambda i: (jnp.minimum(i + 1, steps) % steps, 0)),
            whole(segment_ids),
            pl.BlockSpec(rows, lambda i: (jnp.minimum(i, steps - 1), 0)),
        ]
        + [whole(entry) for entry in parameters],
        out_specs=[
            pl.BlockSpec(rows, lambda i: (jnp.minimum(i, steps - 1), 0)),
            pl.BlockSpec(rows, lambda i: (jnp.maximum(i - steps, 0), 0)),
            pl.BlockSpec(memory_space=pltpu.VMEM),
        ],
        out_shape=[
            jax.ShapeDtypeStruct(inputs.shape, BF16),
            jax.ShapeDtypeStruct(inputs.shape, F32),
            pltpu.VMEM((LAYERS, ROWS, WIDTH), F32),
        ],
        scratch_shapes=[
            pltpu.VMEM((LAYERS, COLUMNS, WIDTH, WIDTH), F32),
            pltpu.VMEM((LAYERS, 3 * WIDTH, 2 * WIDTH), BF16),
            pltpu.VMEM((LAYERS, WIDTH, 2 * WIDTH), BF16),
            pltpu.VMEM((LAYERS, FF + 16, 2 * WIDTH), BF16),
            pltpu.VMEM((LAYERS, WIDTH, FF), BF16),
            pltpu.VMEM((LAYERS, FF, WIDTH), BF16),
            kept(WIDTH, F32, per_step),
            kept(WIDTH, F32, per_step),
            pltpu.VMEM((per_step, 8, LEN, LEN), BF16),
            kept(POWER_ROWS, BF16, per_step),
            kept(8 * HEADS, F32, per_step),
            kept(WIDTH, F32),
            kept(WIDTH, BF16),
            kept(3 * WIDTH, BF16),
            kept(WIDTH, F32),
            kept(8 * HEADS, F32),
            kept(WIDTH, F32),
            kept(WIDTH, F32),
            kept(WIDTH, BF16),
            kept(8, F32),
            kept(POWER_ROWS, BF16),
            kept(FF, F32),
            kept(FF, F32),
        ]
        + totals_scratch()
        + totals_scratch(),
        compiler_params=pltpu.CompilerParams(vmem_limit_bytes=60 * 1024 * 1024),
        name="layers",
    )(inputs, inputs, segment_ids, cotangent, *parameters)


def unpack_kernel(
    where_ref, near_zero, near_one, near_two, near_three, far_zero, far_one, far_two, far_three,
    gains_ref, shifts_ref, qkv_ref, qv_bias_ref, out_ref, out_bias_ref, gate_ref, up_ref, up_bias_ref, down_ref,
    down_bias_ref,
    grads,
):
    core, part = where_ref[0], where_ref[1]
    quarter = ROWS // 4
    near, far = (near_zero, near_one, near_two, near_three), (far_zero, far_one, far_two, far_three)
    for mask in range(4):
        place = pl.ds(pl.multiple_of((part ^ mask) * quarter, 8), quarter)
        grads[core, place] = near[mask][...]
        grads[1 - core, place] = far[mask][...]
    for layer in range(LAYERS):
        for part in range(3):
            lanes = slice(part * WIDTH, (part + 1) * WIDTH)
            qkv_ref[layer, :, lanes] = grads[layer, R_QKV + part * WIDTH : R_QKV + (part + 1) * WIDTH]
        out_ref[layer] = grads[layer, R_OUT : R_OUT + WIDTH]
        for part in range(2):
            lanes = slice(part * WIDTH, (part + 1) * WIDTH)
            up_ref[layer, :, lanes] = grads[layer, R_UP + part * WIDTH : R_UP + (part + 1) * WIDTH]
        down_ref[layer] = grads[layer, R_DOWN : R_DOWN + FF]
        one = slice(layer, layer + 1)

        def row(which):
            return grads[layer, R_SMALL + which : R_SMALL + which + 1]

        gains_ref[layer, 0:1], gains_ref[layer, 1:2] = row(S_GAIN_ONE), row(S_GAIN_TWO)
        shifts_ref[layer, 0:1], shifts_ref[layer, 1:2] = row(S_SHIFT_ONE), row(S_SHIFT_TWO)
        qv_bias_ref[one, :WIDTH], qv_bias_ref[one, WIDTH:] = row(S_Q), row(S_V)
        out_bias_ref[one], gate_ref[one], down_bias_ref[one] = row(S_OUT), row(S_GATE), row(S_DOWN)
        up_bias_ref[one, :WIDTH], up_bias_ref[one, WIDTH:] = row(S_UP_LOW), row(S_UP_HIGH)


def unpack(where, *quarters):
    shapes = [
        (LAYERS, 2, WIDTH), (LAYERS, 2, WIDTH), (LAYERS, WIDTH, 3 * WIDTH), (LAYERS, 2 * WIDTH), (LAYERS, WIDTH, WIDTH),
        (LAYERS, WIDTH), (LAYERS, WIDTH), (LAYERS, WIDTH, FF), (LAYERS, FF), (LAYERS, FF, WIDTH), (LAYERS, WIDTH),
    ]
    return pl.pallas_call(
        unpack_kernel,
        in_specs=[pl.BlockSpec(memory_space=pltpu.SMEM)] + [pl.BlockSpec()] * 8,
        out_shape=[jax.ShapeDtypeStruct(shape, F32) for shape in shapes],
        scratch_shapes=[pltpu.VMEM((LAYERS, ROWS, WIDTH), F32)],
        compiler_params=pltpu.CompilerParams(vmem_limit_bytes=16 * 1024 * 1024),
        name="unpack",
    )(where, *quarters)


def all_sum(grads, size):
    me = lax.axis_index("seq")
    bits = size.bit_length() - 1
    core, part = me & 1, (me >> 1) & 3

    def swap(value, mask):
        return lax.ppermute(value, "seq", [(i, i ^ mask) for i in range(size)])

    def pick(value, index):
        return lax.dynamic_index_in_dim(value, index, 0, keepdims=False)

    layer = pick(grads, core) + swap(pick(grads, 1 - core), 1)
    quarters = layer.reshape(4, ROWS // 4, WIDTH)
    others = [swap(pick(quarters, part ^ mask), 2 * mask) for mask in (1, 2, 3)]
    mine = pick(quarters, part) + others[0] + others[1] + others[2]
    for bit in range(3, bits):
        mine = mine + swap(mine, 1 << bit)
    near = [mine] + [swap(mine, 2 * mask) for mask in (1, 2, 3)]
    return jnp.stack([core, part]).astype(jnp.int32), *near, *(swap(value, 1) for value in near)


def body(size, *arguments):
    result, grad_inputs, grads = local_part(*arguments)
    if size & (size - 1) or size < 8:
        grads = lax.psum(grads, "seq")
        summed = (jnp.zeros((2,), jnp.int32), *grads.reshape(8, ROWS // 4, WIDTH))
    else:
        summed = all_sum(grads, size)
    return (result, grad_inputs) + tuple(unpack(*summed))


def solution(mesh):
    rows = P("seq", None)
    return jax.shard_map(
        lambda *arguments: body(mesh.shape["seq"], *arguments),
        mesh=mesh,
        in_specs=(rows, rows, rows) + (P(),) * 11,
        out_specs=(rows, rows) + (P(),) * 11,
        check_vma=False,
    )
```

```python
import jax
import jax.numpy as jnp
from jax import lax
from jax.experimental import pallas as pl
from jax.experimental.pallas import tpu as pltpu
from jax.sharding import PartitionSpec as P

HEADS = 8
LAYERS = 2
WIDTH = 128
FF = 256
LEN = 256
HALF = 128
CHUNK = 256
AHEAD = 34
QUARTER = 64
WINDOWS = ((0, 128), (0, 192), (64, 256), (128, 256))
PLACES = ((0, 128), (256, 448), (640, 832), (1024, 1152))
POWER_ROWS = 1280
FAR = -1.0e9
GELU_A = 0.7978845608028654
GELU_B = 0.044715
F32 = jnp.float32
BF16 = jnp.bfloat16

GAIN_ONE, SHIFT_ONE, GAIN_TWO, SHIFT_TWO, DOWN_BIAS, GATE = range(6)
COLUMNS = 6
EXTENDED = WIDTH + 16
S_DOWN, S_GATE = range(2)
SUMS = 2
S_LOGIT = 2
S_OUT, S_Q, S_K, S_V, S_UP_LOW, S_UP_HIGH, S_SHIFT_ONE, S_SHIFT_TWO, S_GAIN_ONE, S_GAIN_TWO = range(2, 12)
R_QKV, R_OUT, R_UP, R_DOWN, R_SMALL, ROWS = 0, 384, 512, 768, 1024, 1056


def dot(left, right):
    return lax.dot_general(left, right, (((1,), (0,)), ((), ())), preferred_element_type=F32)


def both(column):
    return jnp.concatenate([column, column], axis=1)


def fold(value):
    return value[:, :HALF] + value[:, HALF:]


def zeros(rows, lanes=LEN):
    return jnp.zeros((rows, lanes), BF16)


def ones(rows, lanes=LEN):
    return jnp.ones((rows, lanes), BF16)


def split_three(value):
    high = value.astype(BF16)
    rest = value - high.astype(F32)
    middle = rest.astype(BF16)
    low = (rest - middle.astype(F32)).astype(BF16)
    return high, middle, low


def norm_parts(value):
    average = jnp.sum(value, axis=0, keepdims=True) * (1.0 / WIDTH)
    centered = value - average
    variance = jnp.sum(centered * centered, axis=0, keepdims=True) * (1.0 / WIDTH)
    scale = lax.rsqrt(variance + 1e-05)
    return centered * scale, scale


def lane_mask(rows, which):
    row = lax.broadcasted_iota(jnp.int32, (rows, HALF), 0)
    lane = lax.broadcasted_iota(jnp.int32, (rows, HALF), 1)
    return jnp.where(which(row, lane < QUARTER), 1.0, 0.0).astype(BF16)


def turned(rows):
    return jnp.concatenate(
        [rows[:, 64:128], rows[:, :64], rows[:, 192:256], rows[:, 128:192]], axis=1
    )


def make_masks():
    low = lane_mask(16, lambda row, left: left)
    high = lane_mask(16, lambda row, left: ~left)
    heads = [
        lane_mask(16, lambda row, left, head=head: (row % 4 == head) & (left if head % 2 == 0 else ~left))
        for head in range(4)
    ]
    return low, high, heads


def halves_of(rows, masks):
    low, high, unused = masks
    count = rows.shape[0] // 16
    low_all = jnp.concatenate([both(low)] * count, axis=0)
    high_all = jnp.concatenate([both(high)] * count, axis=0)
    other = turned(rows)
    return ((rows * low_all, other * high_all), (other * low_all, rows * high_all))


def head_block(variants, block, group):
    lanes = slice((block // 2) * HALF, (block // 2 + 1) * HALF)
    gap = zeros(16, HALF)
    pieces = []
    for head in range(4):
        first = QUARTER * group + 16 * head
        piece = variants[block % 2][head % 2][first : first + 16, lanes]
        pieces.append(jnp.concatenate([piece, gap] if head < 2 else [gap, piece], axis=1))
    return jnp.concatenate(pieces, axis=0)


def with_extra(features, extra):
    return jnp.concatenate([features, extra], axis=0)


def spread_marks(rows, masks, block):
    low, high, unused = masks
    lanes = slice((block // 2) * HALF, (block // 2 + 1) * HALF)
    here, there = rows[:, lanes], turned(rows)[:, lanes]
    once = here * low + there * high if block % 2 == 0 else there * low + here * high
    return both(once)


def spread_rows(rows, masks, block):
    unused, unused, heads = masks
    lanes = slice((block // 2) * HALF, (block // 2 + 1) * HALF)
    here, there = rows[:, lanes], turned(rows)[:, lanes]
    if block % 2 == 1:
        here, there = there, here
    return jnp.concatenate([here * heads[0] + there * heads[1], here * heads[2] + there * heads[3]], axis=1)


def join_blocks(even, odd, head):
    left = lax.broadcasted_iota(jnp.int32, even.shape, 1) < QUARTER
    if head % 2 == 0:
        return jnp.where(left, even, pltpu.roll(odd, QUARTER, 1))
    return jnp.where(left, pltpu.roll(even, QUARTER, 1), odd)


def token_rows(rows, extra):
    return [
        jnp.concatenate([rows[QUARTER * group : QUARTER * group + QUARTER], extra], axis=0).T for group in range(2)
    ]


def skewed(units):
    running, waiting = [], list(units)
    while running or waiting:
        for unused in range(2):
            if waiting:
                running.append(waiting.pop(0))
        running = [unit for unit in running if next(unit, "end") != "end"]
        yield


def together(parts, late=(), wait=0):
    running, waiting, turn = [], list(parts), 0
    while running or waiting:
        if waiting:
            running.append(waiting.pop(0))
        if turn >= wait and late:
            running.append(late.pop(0))
        running = [part for part in running if next(part, "end") != "end"]
        turn += 1
    assert not late


def segment_masks(segments):
    ids = lax.broadcasted_iota(jnp.int32, (16, LEN), 0)
    same = ids == segments
    one_hot = jnp.where(same, 1.0, 0.0).astype(BF16)
    other = jnp.where(same | (ids >= 8), 0.0, FAR).astype(BF16)
    return one_hot, other


def forward_unit(block, group, keys_rows, variants, values, marks, power_ref, mixed_ref, scale_ref, results):
    first, last = WINDOWS[block]
    weights = with_extra(head_block(variants, block, group), marks[block])
    scores = dot(keys_rows[first:last], weights)
    yield
    peak = jnp.max(scores, axis=0, keepdims=True)
    powers = jnp.exp(scores - peak).astype(BF16)
    start = PLACES[block][group]
    power_ref[start : start + last - first] = powers
    yield
    rows = values[QUARTER * group : QUARTER * group + QUARTER, first:last]
    mixed = dot(jnp.concatenate([rows, ones(16, last - first)], axis=0), powers)
    yield
    scale = 1.0 / mixed[QUARTER : QUARTER + 8]
    results[block, group] = (mixed, scale)
    if block % 2 == 0:
        return
    even, even_scale = results[block - 1, group]
    lanes = slice((block // 2) * HALF, (block // 2 + 1) * HALF)
    for head in range(4):
        tile = slice((head // 2) * HALF, (head // 2 + 1) * HALF)
        rows = slice(16 * head, 16 * head + 16)
        factor = join_blocks(even_scale[:, tile], scale[:, tile], head)
        joined = join_blocks(even[rows, tile], mixed[rows, tile], head)
        place = QUARTER * group + 16 * head
        mixed_ref[place : place + 16, lanes] = joined * jnp.concatenate([factor, factor], axis=0)
        place = 8 * (4 * group + head)
        scale_ref[place : place + 8, lanes] = factor


def attention_forward(query, keys, values, segments, masks, power_ref, mixed_ref, scale_ref):
    one_hot, other = segments
    rows = token_rows(keys, other)
    variants = halves_of(query, masks)
    marks = [spread_marks(one_hot, masks, block) for block in range(4)]
    yield
    results = {}
    yield from skewed(
        forward_unit(block, group, rows[group], variants, values, marks, power_ref, mixed_ref, scale_ref, results)
        for group in range(2)
        for block in range(4)
    )


def project(layer, hidden, weights, columns):
    column = lambda which: both(columns[layer, which])
    xhat, spread_one = norm_parts(hidden)
    normed = (xhat * column(GAIN_ONE) + column(SHIFT_ONE)).astype(BF16)
    yield
    projected = dot(weights[0][layer][:, :EXTENDED], jnp.concatenate([normed, ones(16)], axis=0))
    yield
    return xhat, spread_one, normed, projected.astype(BF16)


def forward_layer(layer, hidden, projected, segments, masks, weights, columns, power_ref, mixed_ref, scale_ref):
    unused, out_t, up_t, unused = weights
    column = lambda which: both(columns[layer, which])
    query, keys, values = (projected[part * WIDTH : (part + 1) * WIDTH] for part in range(3))
    yield from attention_forward(query, keys, values, segments, masks, power_ref, mixed_ref, scale_ref)
    mixed = mixed_ref[...]
    middle = hidden + dot(out_t[layer][:, :EXTENDED], jnp.concatenate([mixed.astype(BF16), ones(16)], axis=0))
    yield
    xhat_two, spread_two = norm_parts(middle)
    normed_two = (xhat_two * column(GAIN_TWO) + column(SHIFT_TWO)).astype(BF16)
    yield
    inner = dot(up_t[layer][:, :EXTENDED], jnp.concatenate([normed_two, ones(16)], axis=0))
    yield
    gate = jax.nn.sigmoid(inner[FF : FF + 1])
    return middle, inner[:FF], mixed, xhat_two, spread_two, normed_two, gate


def gated_unit(inner, gate):
    gated = inner * gate
    return gated, 1.0 + jnp.tanh(gated * (GELU_A + (GELU_A * GELU_B) * (gated * gated)))


def feed_forward(layer, middle, inner, gate, weights, columns, gated_ref, twice_ref):
    parts = []
    for start in range(0, FF, CHUNK):
        rows = slice(start, start + CHUNK)
        gated, twice_up = gated_unit(inner[rows], gate)
        gated_ref[rows] = gated
        twice_ref[rows] = twice_up
        parts.append((gated * twice_up).astype(BF16))
        yield
    return feed_output(layer, middle, jnp.concatenate(parts, axis=0), weights, columns)


def feed_output(layer, middle, active, weights, columns):
    return middle + (dot(weights[3][layer], active) + both(columns[layer, DOWN_BIAS]))


def norm_backward(gradient, xhat, scale, gain):
    inner = gradient * gain
    first = jnp.sum(inner, axis=0, keepdims=True) * (1.0 / WIDTH)
    second = jnp.sum(inner * xhat, axis=0, keepdims=True) * (1.0 / WIDTH)
    return scale * (inner - first - xhat * second)


def backward_unit(block, values_rows, query_variants, grad_variants, keys, deltas, power_ref, results, dq_ref, turned_ref):
    first, last = WINDOWS[block]
    query_blocks = [head_block(query_variants, block, group) for group in range(2)]
    grad_blocks = [head_block(grad_variants, block, group) for group in range(2)]
    products = [
        dot(values_rows[group][first:last], with_extra(grad_blocks[group], deltas[block][group]))
        for group in range(2)
    ]
    yield
    powers, grad_scores = [], []
    for group in range(2):
        start = PLACES[block][group]
        powers.append(power_ref[start : start + last - first])
        grad_scores.append((powers[group].astype(F32) * products[group]).astype(BF16))
        yield
    mixed = [
        dot(keys[QUARTER * group : QUARTER * group + QUARTER, first:last], grad_scores[group]) for group in range(2)
    ]

    def together_rows(blocks):
        gap = zeros(QUARTER)
        low = jnp.concatenate([blocks[0], gap], axis=0)
        high = jnp.concatenate([gap, blocks[1]], axis=0)
        return jnp.concatenate([low, high], axis=1)

    grad_keys = dot(jnp.concatenate(grad_scores, axis=1), together_rows(query_blocks).T)
    flipped = []
    for group in range(2):
        turned_ref[0 + 2 * block + group, :, : last - first] = powers[group].T
        flipped.append(dot(grad_blocks[group], turned_ref[0 + 2 * block + group, :, : last - first]))
    grad_values = jnp.concatenate(flipped, axis=0)
    results[block] = (grad_keys, grad_values, mixed)
    yield
    if block % 2 == 0:
        return
    lanes = slice((block // 2) * HALF, (block // 2 + 1) * HALF)
    for group in range(2):
        even, odd = results[block - 1][2][group], mixed[group]
        for head in range(4):
            tile = slice((head // 2) * HALF, (head // 2 + 1) * HALF)
            rows = slice(16 * head, 16 * head + 16)
            place = QUARTER * group + 16 * head
            dq_ref[place : place + 16, lanes] = join_blocks(even[rows, tile], odd[rows, tile], head)


def attention_backward(query, keys, values, mixed, scale, grad_mixed, masks, power_ref, dq_ref, turned_ref):
    factors = [scale[8 * head : 8 * head + 8] for head in range(HEADS)]
    grad = (grad_mixed * jnp.concatenate([row for factor in factors for row in (factor, factor)], axis=0)).astype(BF16)
    product = grad.astype(F32) * mixed
    delta = jnp.concatenate(
        [jnp.sum(product[16 * head : 16 * head + 16], axis=0, keepdims=True) for head in range(HEADS)], axis=0
    )
    yield
    parts = [part.astype(F32) for part in split_three(-delta)]
    gap = jnp.zeros((4, LEN), F32)
    extras = [
        jnp.concatenate([part[4 * group : 4 * group + 4] for part in parts] + [gap], axis=0).astype(BF16)
        for group in range(2)
    ]
    deltas = [[spread_rows(extras[group], masks, block) for group in range(2)] for block in range(4)]
    query_variants = halves_of(query, masks)
    grad_variants = halves_of(grad, masks)
    rows = token_rows(values, ones(16))
    yield
    results = {}
    yield from skewed(
        backward_unit(block, rows, query_variants, grad_variants, keys, deltas, power_ref, results, dq_ref, turned_ref)
        for block in range(4)
    )

    def collect_lanes(which):
        parts = [results[block][which] for block in range(4)]
        gap = jnp.zeros((WIDTH, QUARTER), F32)
        first = jnp.concatenate([parts[0], parts[3]], axis=1)
        second = jnp.concatenate([parts[1], gap], axis=1)
        third = jnp.concatenate([gap, parts[2]], axis=1)
        return (first + second + third).astype(BF16)

    def collect(which):
        parts = [results[block][which] for block in range(4)]
        return jnp.concatenate(
            [
                parts[0][:64] + parts[1][:64],
                parts[0][64:] + parts[1][64:128] + parts[2][:64],
                parts[1][128:] + parts[2][64:128] + parts[3][:64],
                parts[2][128:] + parts[3][64:],
            ],
            axis=0,
        ).astype(BF16)

    return (dq_ref[...] * 0.25).astype(BF16), collect(0), collect_lanes(1).T


def backward_layer(
    layer, gradient, masks, kept, power_ref, scale_ref, units, use_active, raw, columns, totals, dq_ref, turned_ref
):
    w_qkv, w_out, w_up, w_down = raw
    normed, query, keys, values, mixed, xhat, xhat_two, normed_two, rows = kept
    spread_one, spread_two, gate = rows[0:1], rows[1:2], rows[2:3]
    qkv_total, out_total, up_total, down_total, sums = totals
    column = lambda which: both(columns[layer, which])
    branch = gradient.astype(BF16)
    sums[S_DOWN] += fold(gradient)
    grad_active = dot(w_down[layer], branch)
    yield
    actives, inners = [], []
    logit_sum = jnp.zeros((1, LEN), F32)
    for start in range(0, FF, CHUNK):
        rows = slice(start, start + CHUNK)
        gated, twice_up = units(rows)
        active = gated * twice_up
        curve = GELU_A + (3.0 * GELU_A * GELU_B) * (gated * gated)
        slope = twice_up + (active * (2.0 - twice_up)) * curve
        grad_gated = grad_active[rows] * slope
        logit_sum = logit_sum + jnp.sum(grad_gated * gated, axis=0, keepdims=True)
        actives.append(active.astype(BF16))
        inners.append((grad_gated * gate).astype(BF16))
        yield
    grad_logit = logit_sum * (1.0 - gate)
    active = jnp.concatenate(actives, axis=0)
    use_active(active)
    grad_inner = jnp.concatenate(inners, axis=0)
    grad_two = dot(w_up[layer], grad_inner) + column(GATE) * grad_logit
    down_total[...] += dot(branch, active.T)
    up_total[...] += dot(jnp.concatenate([normed_two, ones(16)], axis=0), grad_inner.T)
    sums[S_GATE] += fold(normed_two.astype(F32) * grad_logit)
    sums[S_LOGIT, 0:1] += fold(grad_logit)
    yield
    grad_middle = gradient + norm_backward(grad_two, xhat_two, spread_two, column(GAIN_TWO))
    attended = grad_middle.astype(BF16)
    yield
    grad_mixed = dot(w_out[layer], attended)
    out_total[...] += dot(jnp.concatenate([mixed.astype(BF16), ones(16)], axis=0), attended.T)
    yield
    grad_query, grad_keys, grad_values = yield from attention_backward(
        query, keys, values, mixed, scale_ref[...], grad_mixed, masks, power_ref, dq_ref, turned_ref
    )
    yield
    grad_rows = jnp.concatenate([grad_query.T, grad_keys, grad_values], axis=1)
    qkv_total[...] += dot(jnp.concatenate([normed, ones(16)], axis=0), grad_rows)
    grad_one = dot(w_qkv[layer], jnp.concatenate([grad_query, grad_keys.T, grad_values.T], axis=0))
    yield
    return grad_middle + norm_backward(grad_one, xhat, spread_one, column(GAIN_ONE))


def spread(row):
    return jnp.broadcast_to(row, (WIDTH, WIDTH)).T


def bias_lanes(row):
    parts = [part.astype(F32) for part in split_three(row)]
    return jnp.concatenate(parts + [jnp.zeros((13, WIDTH), F32)], axis=0).T.astype(BF16)


def fill_columns(layer, columns, gains, shifts, w_gate, down_bias):
    columns[layer, GAIN_ONE] = spread(gains[layer, 0:1])
    columns[layer, GAIN_TWO] = spread(gains[layer, 1:2])
    columns[layer, SHIFT_ONE] = spread(shifts[layer, 0:1])
    columns[layer, SHIFT_TWO] = spread(shifts[layer, 1:2])
    columns[layer, DOWN_BIAS] = spread(down_bias[layer : layer + 1])
    columns[layer, GATE] = spread(w_gate[layer : layer + 1].astype(F32))


def clear_totals(totals):
    for ref in totals:
        ref[...] = jnp.zeros_like(ref)


def through(weights, row):
    parts = jnp.concatenate(split_three(row), axis=0)
    return jnp.sum(lax.dot_general(parts, weights, (((1,), (1,)), ((), ())), preferred_element_type=F32), axis=0, keepdims=True)


def across(value):
    parts = [value[:, start : start + WIDTH] for start in range(0, value.shape[1], WIDTH)]
    total = parts[0]
    for part in parts[1:]:
        total = total + part
    return jnp.sum(total.T, axis=0, keepdims=True)


def write_totals(totals, grads_ref, w_qkv, w_gate, w_up, gains, shifts):
    qkv_total, out_total, up_total, down_total, sums = totals
    for part in range(3):
        rows = slice(R_QKV + part * WIDTH, R_QKV + (part + 1) * WIDTH)
        grads_ref[rows] = qkv_total[:WIDTH, part * WIDTH : (part + 1) * WIDTH]
    grads_ref[R_OUT : R_OUT + WIDTH] = out_total[:WIDTH]
    for part in range(2):
        lanes = slice(part * WIDTH, (part + 1) * WIDTH)
        grads_ref[R_UP + part * WIDTH : R_UP + (part + 1) * WIDTH] = up_total[:WIDTH, lanes]
        grads_ref[R_DOWN + part * WIDTH : R_DOWN + (part + 1) * WIDTH] = down_total[:, lanes].T * 0.5
    rows = [jnp.sum(sums[which].T, axis=0, keepdims=True) for which in range(SUMS)]
    rows.append(out_total[WIDTH : WIDTH + 1])
    rows.extend(qkv_total[WIDTH : WIDTH + 1, part * WIDTH : (part + 1) * WIDTH] for part in range(3))
    rows.extend(up_total[WIDTH : WIDTH + 1, part * WIDTH : (part + 1) * WIDTH] for part in range(2))
    rows.append(through(w_qkv, qkv_total[WIDTH : WIDTH + 1]))
    logit = jnp.sum(sums[S_LOGIT, 0:1], axis=1, keepdims=True)
    rows.append(through(w_up, up_total[WIDTH : WIDTH + 1]) + logit * w_gate.astype(F32))
    moments = (
        across(qkv_total[:WIDTH] * w_qkv.astype(F32)),
        across(up_total[:WIDTH] * w_up.astype(F32)) + rows[S_GATE] * w_gate.astype(F32),
    )
    for which, moment in enumerate(moments):
        norm = slice(which, which + 1)
        rows.append((moment - shifts[norm] * rows[S_SHIFT_ONE + which]) / gains[norm])
    rows.append(jnp.zeros((ROWS - R_SMALL - len(rows), WIDTH), F32))
    grads_ref[R_SMALL:ROWS] = jnp.concatenate(rows, axis=0)


def kernel(
    per_step, steps,
    x_ref, x_next_ref, seg_ref, cot_ref, gains, shifts, w_qkv, qv_bias, w_out, out_bias, w_gate, w_up, up_bias, w_down, down_bias,
    result_ref, grad_inputs_ref, grads_ref,
    columns, qkv_t, out_t, up_t, down_t, half_down, mixed_scratch, dq_ref, turned_ref, power_last, scale_last,
    grad_kept, normed_kept, qkv_kept, mixed_kept, scale_kept, xhat_kept, xhat_two_kept, normed_two_kept, rows_kept,
    power_kept, gated_kept, twice_kept, *totals,
):
    step = pl.program_id(0)
    totals_zero, totals_one = totals[: len(totals) // 2], totals[len(totals) // 2 :]

    @pl.when(step == 0)
    def start():
        clear_totals(totals)
        for layer in range(LAYERS):
            fill_columns(layer, columns, gains, shifts, w_gate, down_bias)
            for ref in (qkv_t, out_t, up_t):
                ref[layer, :, WIDTH:] = zeros(ref.shape[1], WIDTH)
            qkv_t[layer, :WIDTH, :WIDTH] = (w_qkv[layer][:, :WIDTH] * jnp.asarray(0.25, BF16)).T
            qkv_t[layer, WIDTH:, :WIDTH] = w_qkv[layer][:, WIDTH:].T
            biases = qv_bias[layer : layer + 1]
            qkv_t[layer, :WIDTH, WIDTH:EXTENDED] = bias_lanes(biases[:, :WIDTH] * 0.25)
            qkv_t[layer, 2 * WIDTH :, WIDTH:EXTENDED] = bias_lanes(biases[:, WIDTH:])
            out_t[layer, :, :WIDTH] = w_out[layer].T
            out_t[layer, :, WIDTH:EXTENDED] = bias_lanes(out_bias[layer : layer + 1])
            up_t[layer, :FF, :WIDTH] = w_up[layer].T
            up_t[layer, FF:, :WIDTH] = jnp.concatenate(
                [w_gate[layer : layer + 1].astype(F32), jnp.zeros((15, WIDTH), F32)], axis=0
            ).astype(BF16)
            biases = up_bias[layer : layer + 1]
            up_t[layer, :WIDTH, WIDTH:EXTENDED] = bias_lanes(biases[:, :WIDTH])
            up_t[layer, WIDTH:FF, WIDTH:EXTENDED] = bias_lanes(biases[:, WIDTH:])
            half_down[layer] = w_down[layer] * jnp.asarray(0.5, BF16)
            down_t[layer] = half_down[layer].T

    masks = make_masks()
    weights = (qkv_t, out_t, up_t, down_t)
    raw = (w_qkv, w_out, w_up, half_down)

    def ahead(item, ref, group):
        place = group * per_step + item
        hidden = ref[item * LEN : (item + 1) * LEN].astype(F32).T
        xhat, spread_one, normed, projected = yield from project(0, hidden, weights, columns)
        xhat_kept[place] = xhat
        rows_kept[place, 0:1] = spread_one
        normed_kept[place] = normed
        qkv_kept[place] = projected

    def upward(item):
        tokens = slice(item * LEN, (item + 1) * LEN)
        place = step * per_step + item
        segments = segment_masks(seg_ref[pl.ds(place, 1)])
        hidden = x_ref[tokens].astype(F32).T
        middle, inner, mixed, xhat_two, spread_two, normed_two, gate = yield from forward_layer(
            0, hidden, qkv_kept[place], segments, masks, weights, columns, power_kept.at[place], mixed_scratch.at[item],
            scale_kept.at[place],
        )
        mixed_kept[place] = mixed
        xhat_two_kept[place] = xhat_two
        normed_two_kept[place] = normed_two
        rows_kept[place, 1:2] = spread_two
        rows_kept[place, 2:3] = gate
        hidden = yield from feed_forward(
            0, middle, inner, gate, weights, columns, gated_kept.at[place], twice_kept.at[place]
        )
        xhat, spread_one, normed, projected = yield from project(1, hidden, weights, columns)
        middle, inner, mixed, xhat_two, spread_two, normed_two, gate = yield from forward_layer(
            1, hidden, projected, segments, masks, weights, columns, power_last.at[item], mixed_scratch.at[item],
            scale_last.at[item],
        )
        kept = (
            normed, projected[:WIDTH], projected[WIDTH : 2 * WIDTH], projected[2 * WIDTH :], mixed, xhat, xhat_two,
            normed_two, jnp.concatenate([spread_one, spread_two, gate], axis=0),
        )

        def last_units(rows):
            return gated_unit(inner[rows], gate)

        def write_result(active):
            result_ref[tokens] = feed_output(1, middle, active, weights, columns).T.astype(BF16)

        gradient = cot_ref[tokens].astype(F32).T
        grad_kept[place] = yield from backward_layer(
            1, gradient, masks, kept, power_last.at[item], scale_last.at[item], last_units, write_result, raw, columns,
            totals_one, dq_ref.at[item], turned_ref.at[item],
        )

    def downward(item):
        tokens = slice(item * LEN, (item + 1) * LEN)
        place = (step - steps) * per_step + item
        kept = (
            normed_kept[place], qkv_kept[place, :WIDTH], qkv_kept[place, WIDTH : 2 * WIDTH],
            qkv_kept[place, 2 * WIDTH :], mixed_kept[place], xhat_kept[place], xhat_two_kept[place],
            normed_two_kept[place], rows_kept[place],
        )
        gradient = yield from backward_layer(
            0, grad_kept[place], masks, kept, power_kept.at[place], scale_kept.at[place],
            lambda rows: (gated_kept[place, rows], twice_kept[place, rows]), lambda active: None, raw, columns,
            totals_zero, dq_ref.at[item], turned_ref.at[item],
        )
        grad_inputs_ref[tokens] = gradient.T

    @pl.when(step == 0)
    def begin():
        together([ahead(item, x_ref, 0) for item in range(per_step)])

    @pl.when(step < steps)
    def first_half():
        following = lax.rem(step + 1, steps)
        together(
            [upward(item) for item in range(per_step)],
            [ahead(item, x_next_ref, following) for item in range(per_step)],
            AHEAD,
        )

    @pl.when(step >= steps)
    def second_half():
        together([downward(item) for item in range(per_step)])

    @pl.when(step == 2 * steps - 1)
    def finish():
        for layer, part in enumerate((totals_zero, totals_one)):
            write_totals(
                part, grads_ref.at[layer], w_qkv[layer], w_gate[layer : layer + 1], w_up[layer], gains[layer],
                shifts[layer],
            )


def totals_scratch():
    return [
        pltpu.VMEM((WIDTH + 16, 3 * WIDTH), F32),
        pltpu.VMEM((WIDTH + 16, WIDTH), F32),
        pltpu.VMEM((WIDTH + 16, FF), F32),
        pltpu.VMEM((WIDTH, FF), F32),
        pltpu.VMEM((SUMS + 1, WIDTH, WIDTH), F32),
    ]


def local_part(inputs, segment_ids, cotangent, *parameters, per_step=4):
    seqs = segment_ids.shape[0]
    per_step = min(per_step, seqs)
    steps = seqs // per_step
    rows = (per_step * LEN, WIDTH)

    def whole(array):
        zero = (0,) * array.ndim
        return pl.BlockSpec(array.shape, lambda i: zero)

    def kept(rows, dtype, count=seqs):
        return pltpu.VMEM((count, rows, LEN), dtype)

    return pl.pallas_call(
        lambda *refs: kernel(per_step, steps, *refs),
        grid=(2 * steps,),
        in_specs=[
            pl.BlockSpec(rows, lambda i: (jnp.minimum(i, steps - 1), 0)),
            pl.BlockSpec(rows, lambda i: (jnp.minimum(i + 1, steps) % steps, 0)),
            whole(segment_ids),
            pl.BlockSpec(rows, lambda i: (jnp.minimum(i, steps - 1), 0)),
        ]
        + [whole(entry) for entry in parameters],
        out_specs=[
            pl.BlockSpec(rows, lambda i: (jnp.minimum(i, steps - 1), 0)),
            pl.BlockSpec(rows, lambda i: (jnp.maximum(i - steps, 0), 0)),
            pl.BlockSpec(memory_space=pltpu.VMEM),
        ],
        out_shape=[
            jax.ShapeDtypeStruct(inputs.shape, BF16),
            jax.ShapeDtypeStruct(inputs.shape, F32),
            pltpu.VMEM((LAYERS, ROWS, WIDTH), F32),
        ],
        scratch_shapes=[
            pltpu.VMEM((LAYERS, COLUMNS, WIDTH, WIDTH), F32),
            pltpu.VMEM((LAYERS, 3 * WIDTH, 2 * WIDTH), BF16),
            pltpu.VMEM((LAYERS, WIDTH, 2 * WIDTH), BF16),
            pltpu.VMEM((LAYERS, FF + 16, 2 * WIDTH), BF16),
            pltpu.VMEM((LAYERS, WIDTH, FF), BF16),
            pltpu.VMEM((LAYERS, FF, WIDTH), BF16),
            kept(WIDTH, F32, per_step),
            kept(WIDTH, F32, per_step),
            pltpu.VMEM((per_step, 8, LEN, LEN), BF16),
            kept(POWER_ROWS, BF16, per_step),
            kept(8 * HEADS, F32, per_step),
            kept(WIDTH, F32),
            kept(WIDTH, BF16),
            kept(3 * WIDTH, BF16),
            kept(WIDTH, F32),
            kept(8 * HEADS, F32),
            kept(WIDTH, F32),
            kept(WIDTH, F32),
            kept(WIDTH, BF16),
            kept(8, F32),
            kept(POWER_ROWS, BF16),
            kept(FF, F32),
            kept(FF, F32),
        ]
        + totals_scratch()
        + totals_scratch(),
        compiler_params=pltpu.CompilerParams(vmem_limit_bytes=60 * 1024 * 1024),
        name="layers",
    )(inputs, inputs, segment_ids, cotangent, *parameters)


def unpack_kernel(
    where_ref, near_zero, near_one, near_two, near_three, far_zero, far_one, far_two, far_three,
    gains_ref, shifts_ref, qkv_ref, qv_bias_ref, out_ref, out_bias_ref, gate_ref, up_ref, up_bias_ref, down_ref,
    down_bias_ref,
    grads,
):
    core, part = where_ref[0], where_ref[1]
    quarter = ROWS // 4
    near, far = (near_zero, near_one, near_two, near_three), (far_zero, far_one, far_two, far_three)
    for mask in range(4):
        place = pl.ds(pl.multiple_of((part ^ mask) * quarter, 8), quarter)
        grads[core, place] = near[mask][...]
        grads[1 - core, place] = far[mask][...]
    for layer in range(LAYERS):
        for part in range(3):
            lanes = slice(part * WIDTH, (part + 1) * WIDTH)
            qkv_ref[layer, :, lanes] = grads[layer, R_QKV + part * WIDTH : R_QKV + (part + 1) * WIDTH]
        out_ref[layer] = grads[layer, R_OUT : R_OUT + WIDTH]
        for part in range(2):
            lanes = slice(part * WIDTH, (part + 1) * WIDTH)
            up_ref[layer, :, lanes] = grads[layer, R_UP + part * WIDTH : R_UP + (part + 1) * WIDTH]
        down_ref[layer] = grads[layer, R_DOWN : R_DOWN + FF]
        one = slice(layer, layer + 1)

        def row(which):
            return grads[layer, R_SMALL + which : R_SMALL + which + 1]

        gains_ref[layer, 0:1], gains_ref[layer, 1:2] = row(S_GAIN_ONE), row(S_GAIN_TWO)
        shifts_ref[layer, 0:1], shifts_ref[layer, 1:2] = row(S_SHIFT_ONE), row(S_SHIFT_TWO)
        qv_bias_ref[one, :WIDTH], qv_bias_ref[one, WIDTH:] = row(S_Q), row(S_V)
        out_bias_ref[one], gate_ref[one], down_bias_ref[one] = row(S_OUT), row(S_GATE), row(S_DOWN)
        up_bias_ref[one, :WIDTH], up_bias_ref[one, WIDTH:] = row(S_UP_LOW), row(S_UP_HIGH)


def unpack(where, *quarters):
    shapes = [
        (LAYERS, 2, WIDTH), (LAYERS, 2, WIDTH), (LAYERS, WIDTH, 3 * WIDTH), (LAYERS, 2 * WIDTH), (LAYERS, WIDTH, WIDTH),
        (LAYERS, WIDTH), (LAYERS, WIDTH), (LAYERS, WIDTH, FF), (LAYERS, FF), (LAYERS, FF, WIDTH), (LAYERS, WIDTH),
    ]
    return pl.pallas_call(
        unpack_kernel,
        in_specs=[pl.BlockSpec(memory_space=pltpu.SMEM)] + [pl.BlockSpec()] * 8,
        out_shape=[jax.ShapeDtypeStruct(shape, F32) for shape in shapes],
        scratch_shapes=[pltpu.VMEM((LAYERS, ROWS, WIDTH), F32)],
        compiler_params=pltpu.CompilerParams(vmem_limit_bytes=16 * 1024 * 1024),
        name="unpack",
    )(where, *quarters)


def all_sum(grads, size):
    me = lax.axis_index("seq")
    bits = size.bit_length() - 1
    core, part = me & 1, (me >> 1) & 3

    def swap(value, mask):
        return lax.ppermute(value, "seq", [(i, i ^ mask) for i in range(size)])

    def pick(value, index):
        return lax.dynamic_index_in_dim(value, index, 0, keepdims=False)

    layer = pick(grads, core) + swap(pick(grads, 1 - core), 1)
    quarters = layer.reshape(4, ROWS // 4, WIDTH)
    others = [swap(pick(quarters, part ^ mask), 2 * mask) for mask in (1, 2, 3)]
    mine = pick(quarters, part) + others[0] + others[1] + others[2]
    for bit in range(3, bits):
        mine = mine + swap(mine, 1 << bit)
    near = [mine] + [swap(mine, 2 * mask) for mask in (1, 2, 3)]
    return jnp.stack([core, part]).astype(jnp.int32), *near, *(swap(value, 1) for value in near)


def body(size, *arguments):
    result, grad_inputs, grads = local_part(*arguments)
    if size & (size - 1) or size < 8:
        grads = lax.psum(grads, "seq")
        summed = (jnp.zeros((2,), jnp.int32), *grads.reshape(8, ROWS // 4, WIDTH))
    else:
        summed = all_sum(grads, size)
    return (result, grad_inputs) + tuple(unpack(*summed))


def solution(mesh):
    rows = P("seq", None)
    return jax.shard_map(
        lambda *arguments: body(mesh.shape["seq"], *arguments),
        mesh=mesh,
        in_specs=(rows, rows, rows) + (P(),) * 11,
        out_specs=(rows, rows) + (P(),) * 11,
        check_vma=False,
    )
```
